32 devices in a mesh: grp: 4 (over x, core), blk: 8 (over z, y).
Axes of the slice: x: 2, y: 2, z: 4, core: 2. Of those that a mesh axis runs over, the one named last changes fastest.
Arguments:
- fine_pops: float32 [4, 19, 128, 256], P('grp', None, 'blk'), may hold values from 0.38 to 8.7, as said below
- fine_solid: float32 [4, 128, 256], P('grp', 'blk'), may hold values from 0.05 to 0.6
- coarse_pops: float32 [4, 19, 64, 256], P('grp', None, 'blk'), may hold values from 0.38 to 8.7, as said below
- coarse_solid: float32 [4, 64, 256], P('grp', 'blk'), may hold values from 0.05 to 0.6
- coarse_slot: int32 [4], replicated, may hold values from 0 to 15, as said below
Outputs:
- fine_out: float32 [4, 19, 128, 256], P('grp', None, 'blk')
- coarse_out: float32 [4, 19, 64, 256], P('grp', None, 'blk')
The draws below stay inside these ranges and needn't reach their ends.
Inputs may be any that keep to these rules, and one draw needn't show every extreme that they name: `fine_pops`: each population is between 0.7 and 1.3 times 20 w_i. `coarse_pops`: each population is between 0.7 and 1.3 times 20 w_i. `coarse_slot`: the 4 entries are distinct, and 15 is one of them.
All inputs are finite; a program needn't handle non-finite values.
Results may differ from the reference program's by a relative error of at most 0.0001.
Values sent between devices are 32-bit elements; how exact they have to be, the bound alone decides.
No kernel may reach another device: no remote copies, remote signals or barrier semaphores. Data moves between devices by JAX's collectives and lax.ppermute only.
A program may use at most 128 MiB of HBM per device.

```python
import jax
import jax.numpy as jnp
import numpy as np
from jax import lax

BX = 16
ZB = 1
GROUPS = 4
FX = 128
CX = 64
CELLS = 256


def weight_column():
    return jnp.array([1.0 / 3.0] + [1.0 / 18.0] * 6 + [1.0 / 36.0] * 12, jnp.float32)[None, :, None, None]


def draw_fine_pops(key, part):
    shape = (GROUPS, 19, FX, CELLS)
    jitter = jax.random.uniform(key, shape, jnp.float32, -0.3, 0.3)
    return 20.0 * weight_column() * (1.0 + jitter)


def draw_coarse_pops(key, part):
    shape = (GROUPS, 19, CX, CELLS)
    jitter = jax.random.uniform(key, shape, jnp.float32, -0.3, 0.3)
    return 20.0 * weight_column() * (1.0 + jitter)


def draw_coarse_slot(key, part):
    leading = jax.random.permutation(jax.random.fold_in(key, 11), 4 * GROUPS - 1)[:GROUPS - 1].astype(jnp.int32)
    codes = jnp.concatenate([leading, jnp.array([4 * GROUPS - 1], jnp.int32)])
    order = jax.random.permutation(jax.random.fold_in(key, 12), GROUPS)
    return codes[order].astype(jnp.int32)


def levels(rng, shape, split, smallest, top_value):
    def one(dim, blocks):
        draws = jax.random.uniform(jax.random.fold_in(jax.random.fold_in(rng, 6), dim), (blocks,), jnp.float32, smallest / len(split), top_value / len(split))
        return jnp.repeat(jnp.exp(draws), shape[dim] // blocks).reshape((-1,) + (1,) * (len(shape) - dim - 1))

    level = one(*split[0])
    for cut in split[1:]:
        level = level * one(*cut)
    return level


def setup_inputs(seed: int = 0) -> dict:
    seeds = jax.random.split(jax.random.key(seed), 6)
    fine_pops = draw_fine_pops(jax.random.fold_in(seeds[5], 71), 0)
    fine_solid = jnp.clip(0.05 + 0.55 * jax.random.uniform(seeds[1], (GROUPS, FX, CELLS), jnp.float32) ** levels(seeds[1], (GROUPS, FX, CELLS), ((0, 4), (1, 8)), -0.2, 0.2), 0.05, 0.6)
    coarse_pops = draw_coarse_pops(jax.random.fold_in(seeds[5], 71), 0)
    coarse_solid = jnp.clip(0.05 + 0.55 * jax.random.uniform(seeds[3], (GROUPS, CX, CELLS), jnp.float32) ** levels(seeds[3], (GROUPS, CX, CELLS), ((0, 4), (1, 8)), -0.2, 0.2), 0.05, 0.6)
    coarse_slot = draw_coarse_slot(jax.random.fold_in(seeds[5], 71), 0)
    return dict(fine_pops=fine_pops, fine_solid=fine_solid, coarse_pops=coarse_pops, coarse_solid=coarse_solid, coarse_slot=coarse_slot)


lattice_vel = np.array([[0, 0, 0], [1, 0, 0], [-1, 0, 0], [0, 1, 0], [0, -1, 0], [0, 0, 1], [0, 0, -1], [1, 1, 0], [-1, -1, 0], [1, -1, 0], [-1, 1, 0], [1, 0, 1], [-1, 0, -1], [1, 0, -1], [-1, 0, 1], [0, 1, 1], [0, -1, -1], [0, 1, -1], [0, -1, 1]])
lattice_weight = np.array([1.0 / 3.0] + [1.0 / 18.0] * 6 + [1.0 / 36.0] * 12)
opposite_index = [0, 2, 1, 4, 3, 6, 5, 8, 7, 10, 9, 12, 11, 14, 13, 16, 15, 18, 17]
tau_fine = 0.6
tau_coarse = 0.55


def spread_table(table, populations):
    return jnp.asarray(table, populations.dtype).reshape((19,) + (1,) * (populations.ndim - 1))


def equilibrium(populations):
    density = jnp.sum(populations, axis=0)
    velocity = [jnp.sum(spread_table(lattice_vel[:, k], populations) * populations, axis=0) / density for k in range(3)]
    projected = spread_table(lattice_vel[:, 0], populations) * velocity[0]
    projected = projected + spread_table(lattice_vel[:, 1], populations) * velocity[1]
    projected = projected + spread_table(lattice_vel[:, 2], populations) * velocity[2]
    speed_sq = velocity[0] * velocity[0] + velocity[1] * velocity[1] + velocity[2] * velocity[2]
    return spread_table(lattice_weight, populations) * density * (1.0 + 3.0 * projected + 4.5 * projected * projected - 1.5 * speed_sq)


def collide_cells(populations, solid, relax):
    equil = equilibrium(populations)
    mirrored = jnp.stack([populations[j] for j in opposite_index])
    return populations - (1.0 - solid) * (populations - equil) / relax + solid * (mirrored - populations)


def stream_periodic(collided):
    return jnp.stack([jnp.roll(collided[j], (int(lattice_vel[j, 0]), int(lattice_vel[j, 1]), int(lattice_vel[j, 2])), axis=(0, 1, 2)) for j in range(19)])


def restrict_block(populations):
    shape = populations.shape
    averaged = populations.reshape(19, shape[1] // 2, 2, shape[2] // 2, 2, shape[3] // 2, 2).mean(axis=(2, 4, 6))
    equil = equilibrium(averaged)
    return equil + (2.0 * tau_coarse / tau_fine) * (averaged - equil)


def reference(fine_pops, fine_solid, coarse_pops, coarse_solid, coarse_slot):
    zlength = BX * ZB

    def fine_group(arrays):
        populations, solid = arrays
        populations = populations.reshape(19, FX, BX, zlength)
        solid = solid.reshape(FX, BX, zlength)
        for substep in range(2):
            populations = stream_periodic(collide_cells(populations, solid, tau_fine))
        return populations

    fine_new = lax.map(fine_group, (fine_pops, fine_solid))
    restricted = lax.map(restrict_block, fine_new)
    half_y = BX // 2
    half_z = zlength // 2
    outputs = []
    for group in range(GROUPS):
        populations = coarse_pops[group].reshape(19, CX, BX, zlength)
        for quadrant in range(4):
            matched = coarse_slot == group * 4 + quadrant
            source = jnp.argmax(matched.astype(jnp.int32)).astype(jnp.int32)
            matched_tile = restricted[source]
            low_y = (quadrant // 2) * half_y
            low_z = (quadrant % 2) * half_z
            region = populations[:, :, low_y:low_y + half_y, low_z:low_z + half_z]
            populations = populations.at[:, :, low_y:low_y + half_y, low_z:low_z + half_z].set(jnp.where(jnp.any(matched), matched_tile, region))
        solid = coarse_solid[group].reshape(CX, BX, zlength)
        populations = stream_periodic(collide_cells(populations, solid, tau_coarse))
        outputs.append(populations.reshape(19, CX, BX * zlength))
    return fine_new.reshape(GROUPS, 19, FX, BX * zlength), jnp.stack(outputs)
```

```python
import jax
import jax.numpy as jnp
import numpy as np
from jax import lax
from jax.experimental import pallas as pl
from jax.experimental.pallas import tpu as pltpu
from jax.sharding import PartitionSpec as P

VEL = np.array(
    [
        [0, 0, 0],
        [1, 0, 0],
        [-1, 0, 0],
        [0, 1, 0],
        [0, -1, 0],
        [0, 0, 1],
        [0, 0, -1],
        [1, 1, 0],
        [-1, -1, 0],
        [1, -1, 0],
        [-1, 1, 0],
        [1, 0, 1],
        [-1, 0, -1],
        [1, 0, -1],
        [-1, 0, 1],
        [0, 1, 1],
        [0, -1, -1],
        [0, 1, -1],
        [0, -1, 1],
    ]
)
NPOP = 19
BX = 16
TAU_FINE = 0.6
TAU_COARSE = 0.55
RESCALE = 2.0 * TAU_COARSE / TAU_FINE

ROWS, LANES = 8, 128
TILE = (ROWS, LANES)
VMEM = pltpu.VMEM


def row_ids():
    return lax.broadcasted_iota(jnp.int32, TILE, 0)


def lane_ids():
    return lax.broadcasted_iota(jnp.int32, TILE, 1)


def roll_rows(tile, shift):
    return pltpu.roll(tile, shift % ROWS, 0)


def roll_lanes(tile, shift):
    return pltpu.roll(tile, shift % LANES, 1)


def moments(f, scale):
    minus = [f[i] - f[i + 1] for i in range(1, NPOP, 2)]
    plus = [f[i] + f[i + 1] for i in range(1, NPOP, 2)]
    rho = ((f[0] + plus[0]) + (plus[1] + plus[2])) + (
        (plus[3] + plus[4]) + (plus[5] + plus[6])
    ) + (plus[7] + plus[8])
    jx = (minus[0] + minus[3]) + (minus[4] + minus[5]) + minus[6]
    jy = (minus[1] + minus[3]) - (minus[4] - minus[7]) + minus[8]
    jz = (minus[2] + minus[5]) - (minus[6] - minus[7]) - minus[8]
    inverse = 1.5 / rho
    ux, uy, uz = jx * inverse, jy * inverse, jz * inverse
    amount = scale(rho)
    base = amount * (1.0 - (2.0 / 3.0) * (ux * ux + uy * uy + uz * uz))
    directions = [ux, uy, uz, ux + uy, ux - uy, ux + uz, ux - uz, uy + uz, uy - uz]
    base_axis, base_diag = base * (1.0 / 18.0), base * (1.0 / 36.0)
    amount_axis, amount_diag = amount * (1.0 / 9.0), amount * (1.0 / 18.0)
    pairs = []
    for k, along in enumerate(directions):
        odd = (amount_axis if k < 3 else amount_diag) * along
        pairs.append(((base_axis if k < 3 else base_diag) + odd * along, odd))
    return base * (1.0 / 3.0), pairs, plus, minus


def collide(f, solid, tau):
    rate = (1.0 - solid) * (1.0 / tau)
    rest, pairs, plus, minus = moments(f, lambda rho: rate * rho)
    keep = 1.0 - rate
    half = 0.5 * keep
    half_odd = half - solid
    out = [keep * f[0] + rest]
    for (even, odd), p, m in zip(pairs, plus, minus):
        symmetric = half * p + even
        antisymmetric = half_odd * m + odd
        out += [symmetric + antisymmetric, symmetric - antisymmetric]
    return out


def restrict(f):
    rest, pairs, _, _ = moments(f, lambda rho: (1.0 - RESCALE) * rho)
    out = [RESCALE * f[0] + rest]
    for k, (even, odd) in enumerate(pairs):
        out += [RESCALE * f[2 * k + 1] + (even + odd), RESCALE * f[2 * k + 2] + (even - odd)]
    return out


def shift_plane(halves, cy, cz):
    lane = lane_ids()
    if cz:
        edge = lane % BX == (0 if cz > 0 else BX - 1)
        halves = [
            jnp.where(
                edge,
                roll_lanes(v, BX * cy + cz - BX * cz),
                roll_lanes(v, BX * cy + cz),
            )
            for v in halves
        ]
    elif cy:
        halves = [roll_lanes(v, BX * cy) for v in halves]
    if cy:
        carried = lane < BX if cy > 0 else lane >= LANES - BX
        halves = [
            jnp.where(carried, halves[1], halves[0]),
            jnp.where(carried, halves[0], halves[1]),
        ]
    return halves


def shift_ring(tiles, cx):
    if not cx:
        return tiles
    row = row_ids()
    turned = [roll_rows(t, cx) for t in tiles]
    if len(tiles) == 1:
        return turned
    edge = row == (0 if cx > 0 else ROWS - 1)
    n = len(tiles)
    return [jnp.where(edge, turned[(i - cx) % n], turned[i]) for i in range(n)]


def stream_ring(ring):
    out = [[[], []] for _ in ring]
    for i in range(NPOP):
        cx, cy, cz = (int(c) for c in VEL[i])
        moved = [shift_plane([tile[0][i], tile[1][i]], cy, cz) for tile in ring]
        for h in range(2):
            for t, v in enumerate(shift_ring([m[h] for m in moved], cx)):
                out[t][h].append(v)
    return out


def squeeze(halves):
    lane = lane_ids()
    low, high = (v + roll_lanes(v, -1) for v in halves)
    both = jnp.where(lane % 2 == 1, roll_lanes(high, 1), low)
    return both + roll_lanes(both, -BX)


def pair_up(first, second):
    if second is None:
        return first
    return jnp.where(lane_ids() // BX % 2 == 1, roll_lanes(second, BX), first)


def spread(tile, which):
    lane = lane_ids()
    y, z = lane // BX, lane % BX
    source = 2 * BX * (y % 4) + BX * which + 2 * (z % 8) + y // 4
    return jnp.take_along_axis(tile, source, axis=1, mode="promise_in_bounds")


def half_lanes(h):
    return pl.ds(h * LANES, LANES)


def pack_kernel(fine, solid, coarse, coarse_solid, own, high, low, strip, rim, sem):
    planes = fine.shape[2]
    coarse_planes = coarse.shape[2]
    copies = []

    def bring(source, target):
        copies.append(pltpu.make_async_copy(source, target, sem.at[len(copies)]))
        copies[-1].start()

    for first, row in ((0, 0), (planes - 4, 4)):
        bring(fine.at[0, :, pl.ds(first, 4), :], strip.at[pl.ds(0, NPOP), pl.ds(row, 4), :])
        bring(solid.at[0, pl.ds(first, 4), :], strip.at[NPOP, pl.ds(row, 4), :])
    for side, plane in ((0, 0), (1, coarse_planes - 1)):
        bring(coarse.at[0, :, pl.ds(plane, 1), :], rim.at[side, pl.ds(0, NPOP)])
        bring(coarse_solid.at[0, pl.ds(plane, 1), :], rim.at[side, NPOP])
    for copy in copies[:4]:
        copy.wait()
    upper = row_ids() < 4
    for h in range(2):
        at = half_lanes(h)
        s = strip[NPOP, :, at]
        out = collide([strip[i, :, at] for i in range(NPOP)], s, TAU_FINE)
        for i, v in enumerate(out + [s]):
            own[i, h] = v
    for i in range(NPOP + 1):
        first, second = own[i, 0], roll_rows(own[i, 1], 4)
        high[i] = jnp.where(upper, second, first)
        low[i] = jnp.where(upper, first, second)
    for copy in copies[4:]:
        copy.wait()
    for side, message in ((0, low), (1, high)):
        for i in range(NPOP + 1):
            for h in range(2):
                index, row = rim_place(i, h)
                message[index, pl.ds(row, 1), :] = rim[side, i, :, half_lanes(h)]


def rim_place(i, h):
    return NPOP + 1 + (2 * i + h) // ROWS, (2 * i + h) % ROWS


def rim_row(message, i, h):
    index, row = rim_place(i, h)
    return jnp.broadcast_to(message[index, pl.ds(row, 1), :], TILE)


def inner_kernel(fine, solid, slot, inner, packed, chosen, work):
    groups = chosen.shape[1]
    ring = []
    for t in range(2):
        ring.append([])
        for h in range(2):
            rows, at = pl.ds(ROWS * t, ROWS), half_lanes(h)
            f = [fine[0, i, rows, at] for i in range(NPOP)]
            ring[t].append(collide(f, solid[0, rows, at], TAU_FINE))
    ring = stream_ring(ring)
    for t in range(2):
        for h in range(2):
            s = solid[0, pl.ds(ROWS * t, ROWS), half_lanes(h)]
            ring[t][h] = collide(ring[t][h], s, TAU_FINE)
    ring = stream_ring(ring)
    for i in range(NPOP):
        for h in range(2):
            for t in range(2):
                inner[i, h, pl.ds(ROWS * t, ROWS), :] = ring[t][h][i]
                work[i, h, pl.ds(ROWS * t, ROWS), :] = ring[t][h][i]
    mean = []
    for i in range(NPOP):
        halves = [
            work[i, h, pl.ds(0, ROWS, stride=2), :] + work[i, h, pl.ds(1, ROWS, stride=2), :]
            for h in range(2)
        ]
        mean.append(0.125 * squeeze(halves))
    out = restrict(mean) + [None]
    for j in range((NPOP + 1) // 2):
        packed[j] = pair_up(out[2 * j], out[2 * j + 1])
    me = lax.axis_index("grp")
    quadrant = lane_ids() % BX // 8
    for s in range(groups):
        code = slot[me ^ s]
        for h in range(2):
            chosen[h, s] = jnp.where(4 * me + 2 * h + quadrant == code, 1.0, 0.0)


def edge_kernel(own, below, above, edges, packed):
    row = row_ids()
    upper = row < 4
    rings, solids = [], []
    for message, is_low in ((below, True), (above, False)):
        halves = []
        for h in range(2):
            got = []
            for i in range(NPOP + 1):
                other = message[i] if h == 0 else roll_rows(message[i], 4)
                mine = own[i, h]
                got.append(jnp.where(upper, mine, other) if is_low else jnp.where(upper, other, mine))
            halves.append(got)
        rings.append([[half[:NPOP] for half in halves]])
        solids.append([half[NPOP] for half in halves])
    for r in range(2):
        ring = stream_ring(rings[r])
        ring[0] = [collide(ring[0][h], solids[r][h], TAU_FINE) for h in range(2)]
        rings[r] = stream_ring(ring)
    from_above = (row == 1) | (row == ROWS - 1)
    mean = []
    for i in range(NPOP):
        halves = []
        for h in range(2):
            low, high = rings[0][0][h][i], rings[1][0][h][i]
            edges[i, h] = jnp.where(upper, low, high)
            low = low + roll_rows(low, -1)
            high = high + roll_rows(high, -1)
            halves.append(jnp.where(from_above, roll_rows(high, 1), low))
        mean.append(0.125 * squeeze(halves))
    out = restrict(mean) + [None]
    pairs = [pair_up(out[2 * j], out[2 * j + 1]) for j in range((NPOP + 1) // 2)]
    outer = (row < 2) | (row >= 6)
    for j in range(len(pairs) // 2):
        packed[j] = jnp.where(outer, pairs[2 * j], roll_rows(pairs[2 * j + 1], 4))


def write_kernel(inner, edges, out):
    row = row_ids()
    for i in range(NPOP):
        for h in range(2):
            edge = edges[i, h]
            out[0, i, pl.ds(0, ROWS), half_lanes(h)] = jnp.where(
                row < 2, edge, inner[i, h, pl.ds(0, ROWS), :]
            )
            out[0, i, pl.ds(ROWS, ROWS), half_lanes(h)] = jnp.where(
                row >= 6, edge, inner[i, h, pl.ds(ROWS, ROWS), :]
            )


def coarse_kernel(coarse, solid, chosen, *refs):
    packed, out = refs[:-1], refs[-1]
    f = [[], []]
    for i in range(NPOP):
        tiles = [spread(m[i // 2], i % 2) for m in packed]
        for h in range(2):
            v = coarse[0, i, :, half_lanes(h)]
            for s, tile in enumerate(tiles):
                v = jnp.where(chosen[h, s] > 0.5, tile, v)
            f[h].append(v)
    for h in range(2):
        for i, v in enumerate(collide(f[h], solid[0, :, half_lanes(h)], TAU_COARSE)):
            out[i, h] = v


def last_kernel(coarse, solid, chosen, below, above, middle, *refs):
    packed, out = refs[:-1], refs[-1]
    row = row_ids()

    def framed(tile, i, h):
        tile = jnp.where(row == 6, rim_row(below, i, h), tile)
        return jnp.where(row == 1, rim_row(above, i, h), tile)

    f = [[], []]
    for i in range(NPOP):
        tiles = []
        for m in packed:
            tile = m[i // 4]
            tiles.append(spread(roll_rows(tile, 4) if i % 4 >= 2 else tile, i % 2))
        for h in range(2):
            v = framed(coarse[0, i, :, half_lanes(h)], i, h)
            for s, tile in enumerate(tiles):
                v = jnp.where(chosen[h, s] > 0.5, tile, v)
            f[h].append(v)
    ends = [
        collide(f[h], framed(solid[0, :, half_lanes(h)], NPOP, h), TAU_COARSE)
        for h in range(2)
    ]
    outer = (row == 0) | (row == ROWS - 1)
    for i in range(NPOP):
        cx, cy, cz = (int(c) for c in VEL[i])
        halves = []
        for h in range(2):
            v = jnp.where(outer, ends[h][i], middle[i, h])
            if cx > 0:
                v = jnp.where(row == 0, roll_rows(ends[h][i], 2), roll_rows(v, 1))
            elif cx < 0:
                v = jnp.where(row == ROWS - 1, roll_rows(ends[h][i], -2), roll_rows(v, -1))
            halves.append(v)
        for h, v in enumerate(shift_plane(halves, cy, cz)):
            out[0, i, :, half_lanes(h)] = v


def held(array):
    return pltpu.with_memory_space_constraint(array, VMEM)


def in_vmem(*shape):
    return VMEM(shape, jnp.float32)


def call(kernel, args, specs, outs, scratch=(), flops=0, name=None):
    single = not isinstance(outs, (list, tuple))
    outs = [outs] if single else list(outs)
    result = pl.pallas_call(
        kernel,
        in_specs=[pl.BlockSpec(memory_space=s) for s in specs],
        out_specs=[pl.BlockSpec(memory_space=VMEM)] * len(outs),
        out_shape=outs,
        scratch_shapes=list(scratch),
        compiler_params=pltpu.CompilerParams(vmem_limit_bytes=24 << 20),
        cost_estimate=pl.CostEstimate(flops=flops, bytes_accessed=1 << 20, transcendentals=0),
        name=name,
    )(*args)
    return result[0] if single else result


def per_device(fine_pops, fine_solid, coarse_pops, coarse_solid, coarse_slot):
    groups = lax.axis_size("grp")
    blocks = lax.axis_size("blk")
    words = NPOP + 6
    any_, smem = pl.ANY, pltpu.SMEM
    own, high, low = call(
        pack_kernel,
        (fine_pops, fine_solid, coarse_pops, coarse_solid),
        [any_] * 4,
        [in_vmem(NPOP + 1, 2, *TILE), in_vmem(words, *TILE), in_vmem(words, *TILE)],
        [
            in_vmem(NPOP + 1, ROWS, 2 * LANES),
            in_vmem(2, NPOP + 1, 1, 2 * LANES),
            pltpu.SemaphoreType.DMA((8,)),
        ],
        name="pack",
    )
    forward = [(i, (i + 1) % blocks) for i in range(blocks)]
    backward = [(i, (i - 1) % blocks) for i in range(blocks)]
    below = lax.ppermute(high, "blk", forward)
    above = lax.ppermute(low, "blk", backward)

    fine_v, solid_v = held(fine_pops), held(fine_solid)
    coarse_v, coarse_solid_v = held(coarse_pops), held(coarse_solid)
    inner, packed_inner, chosen = call(
        inner_kernel,
        (fine_v, solid_v, coarse_slot),
        [VMEM, VMEM, smem],
        [
            in_vmem(NPOP, 2, 2 * ROWS, LANES),
            in_vmem((NPOP + 1) // 2, *TILE),
            in_vmem(2, groups, *TILE),
        ],
        [in_vmem(NPOP, 2, 2 * ROWS, LANES)],
        name="inner",
    )

    def around(array):
        swaps = [[(i, i ^ s) for i in range(groups)] for s in range(1, groups)]
        return [array] + [lax.ppermute(array, "grp", swap) for swap in swaps]

    inner_parts = around(packed_inner)
    edges, packed_edges = call(
        edge_kernel,
        (held(own), held(below), held(above)),
        [VMEM] * 3,
        [in_vmem(NPOP, 2, *TILE), in_vmem((NPOP + 1) // 4, *TILE)],
        name="edge",
    )
    edge_parts = around(packed_edges)
    fine_out = call(
        write_kernel,
        (held(inner), held(edges)),
        [VMEM] * 2,
        jax.ShapeDtypeStruct(fine_pops.shape, jnp.float32),
        name="write",
    )
    middle = call(
        coarse_kernel,
        (coarse_v, coarse_solid_v, held(chosen), *map(held, inner_parts)),
        [VMEM] * (3 + groups),
        in_vmem(NPOP, 2, *TILE),
        name="coarse",
    )
    coarse_out = call(
        last_kernel,
        (
            coarse_v,
            coarse_solid_v,
            held(chosen),
            held(below),
            held(above),
            held(middle),
            *map(held, edge_parts),
        ),
        [VMEM] * (6 + groups),
        jax.ShapeDtypeStruct(coarse_pops.shape, jnp.float32),
        name="last",
    )
    return fine_out, coarse_out


def solution(mesh):
    placed = (
        P("grp", None, "blk", None),
        P("grp", "blk", None),
        P("grp", None, "blk", None),
        P("grp", "blk", None),
        P(),
    )
    return jax.shard_map(
        per_device,
        mesh=mesh,
        in_specs=placed,
        out_specs=(P("grp", None, "blk", None), P("grp", None, "blk", None)),
        check_vma=False,
    )
```

```python
import jax
import jax.numpy as jnp
import numpy as np
from jax import lax
from jax.experimental import pallas as pl
from jax.experimental.pallas import tpu as pltpu
from jax.sharding import PartitionSpec as P

VEL = np.array(
    [
        [0, 0, 0],
        [1, 0, 0],
        [-1, 0, 0],
        [0, 1, 0],
        [0, -1, 0],
        [0, 0, 1],
        [0, 0, -1],
        [1, 1, 0],
        [-1, -1, 0],
        [1, -1, 0],
        [-1, 1, 0],
        [1, 0, 1],
        [-1, 0, -1],
        [1, 0, -1],
        [-1, 0, 1],
        [0, 1, 1],
        [0, -1, -1],
        [0, 1, -1],
        [0, -1, 1],
    ]
)
NPOP = 19
BX = 16
TAU_FINE = 0.6
TAU_COARSE = 0.55
RESCALE = 2.0 * TAU_COARSE / TAU_FINE

ROWS, LANES = 8, 128
TILE = (ROWS, LANES)
VMEM = pltpu.VMEM


def row_ids():
    return lax.broadcasted_iota(jnp.int32, TILE, 0)


def lane_ids():
    return lax.broadcasted_iota(jnp.int32, TILE, 1)


def roll_rows(tile, shift):
    return pltpu.roll(tile, shift % ROWS, 0)


def roll_lanes(tile, shift):
    return pltpu.roll(tile, shift % LANES, 1)


def moments(f, scale):
    minus = [f[i] - f[i + 1] for i in range(1, NPOP, 2)]
    plus = [f[i] + f[i + 1] for i in range(1, NPOP, 2)]
    rho = ((f[0] + plus[0]) + (plus[1] + plus[2])) + (
        (plus[3] + plus[4]) + (plus[5] + plus[6])
    ) + (plus[7] + plus[8])
    jx = (minus[0] + minus[3]) + (minus[4] + minus[5]) + minus[6]
    jy = (minus[1] + minus[3]) - (minus[4] - minus[7]) + minus[8]
    jz = (minus[2] + minus[5]) - (minus[6] - minus[7]) - minus[8]
    inverse = 1.5 / rho
    ux, uy, uz = jx * inverse, jy * inverse, jz * inverse
    amount = scale(rho)
    base = amount * (1.0 - (2.0 / 3.0) * (ux * ux + uy * uy + uz * uz))
    directions = [ux, uy, uz, ux + uy, ux - uy, ux + uz, ux - uz, uy + uz, uy - uz]
    base_axis, base_diag = base * (1.0 / 18.0), base * (1.0 / 36.0)
    amount_axis, amount_diag = amount * (1.0 / 9.0), amount * (1.0 / 18.0)
    pairs = []
    for k, along in enumerate(directions):
        odd = (amount_axis if k < 3 else amount_diag) * along
        pairs.append(((base_axis if k < 3 else base_diag) + odd * along, odd))
    return base * (1.0 / 3.0), pairs, plus, minus


def collide(f, solid, tau):
    rate = (1.0 - solid) * (1.0 / tau)
    rest, pairs, plus, minus = moments(f, lambda rho: rate * rho)
    keep = 1.0 - rate
    half = 0.5 * keep
    half_odd = half - solid
    out = [keep * f[0] + rest]
    for (even, odd), p, m in zip(pairs, plus, minus):
        symmetric = half * p + even
        antisymmetric = half_odd * m + odd
        out += [symmetric + antisymmetric, symmetric - antisymmetric]
    return out


def restrict(f):
    rest, pairs, _, _ = moments(f, lambda rho: (1.0 - RESCALE) * rho)
    out = [RESCALE * f[0] + rest]
    for k, (even, odd) in enumerate(pairs):
        out += [RESCALE * f[2 * k + 1] + (even + odd), RESCALE * f[2 * k + 2] + (even - odd)]
    return out


def shift_plane(halves, cy, cz):
    lane = lane_ids()
    if cz:
        edge = lane % BX == (0 if cz > 0 else BX - 1)
        halves = [
            jnp.where(
                edge,
                roll_lanes(v, BX * cy + cz - BX * cz),
                roll_lanes(v, BX * cy + cz),
            )
            for v in halves
        ]
    elif cy:
        halves = [roll_lanes(v, BX * cy) for v in halves]
    if cy:
        carried = lane < BX if cy > 0 else lane >= LANES - BX
        halves = [
            jnp.where(carried, halves[1], halves[0]),
            jnp.where(carried, halves[0], halves[1]),
        ]
    return halves


def shift_ring(tiles, cx):
    if not cx:
        return tiles
    row = row_ids()
    turned = [roll_rows(t, cx) for t in tiles]
    if len(tiles) == 1:
        return turned
    edge = row == (0 if cx > 0 else ROWS - 1)
    n = len(tiles)
    return [jnp.where(edge, turned[(i - cx) % n], turned[i]) for i in range(n)]


def move_in_planes(halves):
    moved = [
        shift_plane([halves[0][i], halves[1][i]], int(VEL[i, 1]), int(VEL[i, 2]))
        for i in range(NPOP)
    ]
    return [[moved[i][h] for i in range(NPOP)] for h in range(2)]


def move_along(ring):
    out = [[[], []] for _ in ring]
    for h in range(2):
        for i in range(NPOP):
            for t, v in enumerate(shift_ring([tile[h][i] for tile in ring], int(VEL[i, 0]))):
                out[t][h].append(v)
    return out


def merge(mask, first, second):
    return [
        [jnp.where(mask, v, w) for v, w in zip(a, b)] for a, b in zip(first, second)
    ]


def squeeze(halves):
    even = lane_ids() % 2 == 0
    first = jnp.where(even, halves[0], roll_lanes(halves[1], 1))
    second = jnp.where(even, roll_lanes(halves[0], -1), halves[1])
    both = first + second
    return both + roll_lanes(both, -BX)


def pair_up(first, second):
    if second is None:
        return first
    return jnp.where(lane_ids() // BX % 2 == 1, roll_lanes(second, BX), first)


def spread(tile, which):
    lane = lane_ids()
    y, z = lane // BX, lane % BX
    source = 2 * BX * (y % 4) + BX * which + 2 * (z % 8) + y // 4
    return jnp.take_along_axis(tile, source, axis=1, mode="promise_in_bounds")


def half_lanes(h):
    return pl.ds(h * LANES, LANES)


FORWARD = [i for i in range(NPOP) if VEL[i, 0] > 0]
LEVEL = [i for i in range(NPOP) if VEL[i, 0] == 0]
BACKWARD = [i for i in range(NPOP) if VEL[i, 0] < 0]
MOVING = len(FORWARD)
FIRST_LEVEL = MOVING
FIRST_PAIR = FIRST_LEVEL + len(LEVEL)
WORDS = FIRST_PAIR + (MOVING + 1) // 2
FIRST_RIM = FIRST_LEVEL + 1


def pack_message(message, tile, rim, towards, away, up):
    place = row_ids() % 4
    spare = place == (0 if up > 0 else 3)
    near = place >= 2 if up > 0 else place < 2
    for k, i in enumerate(towards):
        message[k] = tile(i)
    for k, i in enumerate(LEVEL):
        other = roll_rows(tile(NPOP), -up) if k == 0 else rim(k - 1)
        message[FIRST_LEVEL + k] = tile(i) if other is None else jnp.where(spare, other, tile(i))
    for k in range((MOVING + 1) // 2):
        second = away[2 * k + 1] if 2 * k + 1 < MOVING else NPOP
        message[FIRST_PAIR + k] = jnp.where(near, tile(away[2 * k]), roll_rows(tile(second), -2 * up))


def unpack_message(message, towards, away, up):
    near = row_ids() % 4 >= 2 if up > 0 else row_ids() % 4 < 2
    found = [None] * (NPOP + 1)
    for k, i in enumerate(towards):
        found[i] = message[k]
    for k, i in enumerate(LEVEL):
        found[i] = message[FIRST_LEVEL + k]
    for k in range((MOVING + 1) // 2):
        tile = message[FIRST_PAIR + k]
        found[away[2 * k]] = tile
        found[away[2 * k + 1] if 2 * k + 1 < MOVING else NPOP] = roll_rows(tile, 2 * up)
    found[NPOP] = jnp.where(near, found[NPOP], roll_rows(message[FIRST_LEVEL], up))
    return found


def rim_row(message, k, h, up):
    row = (4, 0)[h] if up > 0 else (3, 7)[h]
    return jnp.broadcast_to(message[FIRST_RIM + k, pl.ds(row, 1), :], TILE)


def pack_kernel(fine, solid, coarse, coarse_solid, own, high, low, strip, rim, sem):
    planes = fine.shape[2]
    last = coarse.shape[2] - 1

    def bring(source, target, which):
        pltpu.make_async_copy(source, target, sem.at[which]).start()

    def arrive(target, which):
        pltpu.make_async_copy(target, target, sem.at[which]).wait()

    ends = ((0, 0), (planes - 4, 4))
    for h in range(2):
        at = half_lanes(h)
        for first, row in ends:
            bring(fine.at[0, :, pl.ds(first, 4), at], strip.at[pl.ds(0, NPOP), pl.ds(row, 4), at], 0)
    for first, row in ends:
        bring(solid.at[0, pl.ds(first, 4), :], strip.at[NPOP, pl.ds(row, 4), :], 0)
    for plane, h, row in ((last, 1, 0), (last, 0, 4), (0, 0, 3), (0, 1, 7)):
        target = rim.at[pl.ds(0, NPOP), pl.ds(row, 1), :]
        bring(coarse.at[0, :, pl.ds(plane, 1), half_lanes(h)], target, 1)
        bring(coarse_solid.at[0, pl.ds(plane, 1), half_lanes(h)], rim.at[NPOP, pl.ds(row, 1), :], 1)
    arrive(strip, 0)
    for h in range(2):
        at = half_lanes(h)
        s = strip[NPOP, :, at]
        out = collide([strip[i, :, at] for i in range(NPOP)], s, TAU_FINE)
        for i, v in enumerate(out + [s]):
            own[i, h] = v
    arrive(rim.at[:, pl.ds(0, 4), :], 1)
    s = rim[NPOP]
    ends = collide([rim[i] for i in range(NPOP)], s, TAU_COARSE) + [s]
    upper = row_ids() < 4

    def ending(i):
        return jnp.where(upper, roll_rows(own[i, 1], 4), own[i, 0])

    def beginning(i):
        return jnp.where(upper, own[i, 0], roll_rows(own[i, 1], 4))

    def rim_of(towards):
        return lambda k: ends[(towards + [NPOP])[k]] if k <= MOVING else None

    pack_message(high, ending, rim_of(FORWARD), FORWARD, BACKWARD, 1)
    pack_message(low, beginning, rim_of(BACKWARD), BACKWARD, FORWARD, -1)


def inner_kernel(fine, solid, own, slot, inner, packed, chosen, moved, work):
    groups = chosen.shape[1]
    upper = row_ids() < 4

    def middle(ref, h, *i):
        at = half_lanes(h)
        return jnp.where(upper, ref[(0, *i, pl.ds(ROWS, ROWS), at)], ref[(0, *i, pl.ds(0, ROWS), at)])

    outer = move_in_planes([[own[i, h] for i in range(NPOP)] for h in range(2)])
    center = move_in_planes(
        [
            collide([middle(fine, h, i) for i in range(NPOP)], middle(solid, h), TAU_FINE)
            for h in range(2)
        ]
    )
    for i in range(NPOP):
        for h in range(2):
            moved[i, h] = outer[h][i]
    ring = move_along([merge(upper, outer, center), merge(upper, center, outer)])
    for t in range(2):
        for h in range(2):
            s = solid[0, pl.ds(ROWS * t, ROWS), half_lanes(h)]
            ring[t][h] = collide(ring[t][h], s, TAU_FINE)
        ring[t] = move_in_planes(ring[t])
    ring = move_along(ring)
    for i in range(NPOP):
        for h in range(2):
            for t in range(2):
                inner[i, h, pl.ds(ROWS * t, ROWS), :] = ring[t][h][i]
                work[i, h, pl.ds(ROWS * t, ROWS), :] = ring[t][h][i]
    mean = []
    for i in range(NPOP):
        halves = [
            work[i, h, pl.ds(0, ROWS, stride=2), :] + work[i, h, pl.ds(1, ROWS, stride=2), :]
            for h in range(2)
        ]
        mean.append(0.125 * squeeze(halves))
    out = restrict(mean) + [None]
    for j in range((NPOP + 1) // 2):
        packed[j] = pair_up(out[2 * j], out[2 * j + 1])
    me = lax.axis_index("grp")
    codes = slot[...].reshape(1, groups)
    group_ids = lax.broadcasted_iota(jnp.int32, codes.shape, 1)
    quadrant = 4 * me + lane_ids() % BX // 8
    for s, other in enumerate(peers(groups)):
        code = jnp.sum(jnp.where(group_ids == me ^ other, codes, 0), axis=1, keepdims=True)
        for h in range(2):
            chosen[h, s] = jnp.where(quadrant + 2 * h == code, 1.0, 0.0)


def edge_kernel(own, moved, below, above, edges, packed):
    row = row_ids()
    upper = row < 4
    below = unpack_message(below, FORWARD, BACKWARD, 1)
    above = unpack_message(above, BACKWARD, FORWARD, -1)
    halos = [
        [jnp.where(upper, a, b) for a, b in zip(above, below)],
        [roll_rows(jnp.where(upper, b, a), 4) for a, b in zip(above, below)],
    ]
    solids = [(own[NPOP, h], halos[h][NPOP]) for h in range(2)]
    halos = move_in_planes([half[:NPOP] for half in halos])
    mine = [[moved[i, h] for i in range(NPOP)] for h in range(2)]
    low, high = (
        move_along([ring])[0] for ring in (merge(upper, mine, halos), merge(upper, halos, mine))
    )
    low = [collide(low[h], jnp.where(upper, *solids[h]), TAU_FINE) for h in range(2)]
    high = [collide(high[h], jnp.where(upper, *solids[h][::-1]), TAU_FINE) for h in range(2)]
    low, high = (move_along([ring])[0] for ring in (low, high))
    high = [[roll_rows(v, 4) for v in half] for half in high]
    both = move_in_planes(merge((row < 2) | (row >= 6), low, high))
    sums = [[v + roll_rows(v, -1) for v in half] + [None] for half in both]
    odd = row % 2 == 1
    mean = []
    for i in range(0, NPOP, 2):
        pair = [half[i] if half[i + 1] is None else jnp.where(odd, roll_rows(half[i + 1], 1), half[i]) for half in sums]
        pair = 0.125 * squeeze(pair)
        mean += [pair, roll_rows(pair, -1)]
    out = restrict(mean[:NPOP]) + [None]
    pairs = [
        out[i] if out[i + 1] is None else jnp.where(odd, roll_rows(out[i + 1], 1), out[i])
        for i in range(0, NPOP, 2)
    ]
    for j in range(len(pairs) // 2):
        packed[j] = pair_up(pairs[2 * j], pairs[2 * j + 1])
    for i in range(NPOP):
        for h in range(2):
            edges[i, h] = both[h][i]


def write_kernel(inner, edges, out):
    row = row_ids()
    for i in range(NPOP):
        for h in range(2):
            edge = edges[i, h]
            out[0, i, pl.ds(0, ROWS), half_lanes(h)] = jnp.where(
                row < 2, edge, inner[i, h, pl.ds(0, ROWS), :]
            )
            out[0, i, pl.ds(ROWS, ROWS), half_lanes(h)] = jnp.where(
                row >= 6, roll_rows(edge, 4), inner[i, h, pl.ds(ROWS, ROWS), :]
            )


def coarse_kernel(coarse, solid, chosen, *refs):
    packed, out = refs[:-1], refs[-1]
    f = [[], []]
    for i in range(NPOP):
        tiles = [spread(m[i // 2], i % 2) for m in packed]
        for h in range(2):
            v = coarse[0, i, :, half_lanes(h)]
            for s, tile in enumerate(tiles):
                v = jnp.where(chosen[h, s] > 0.5, tile, v)
            f[h].append(v)
    for h in range(2):
        for i, v in enumerate(collide(f[h], solid[0, :, half_lanes(h)], TAU_COARSE)):
            out[i, h] = v


def last_kernel(coarse, solid, chosen, below, above, middle, *refs):
    packed, out = refs[:-1], refs[-1]
    row = row_ids()
    masks = [[chosen[h, s] > 0.5 for s in range(len(packed))] for h in range(2)]
    pasted = []
    for h in range(2):
        total = chosen[h, 0]
        for s in range(1, len(packed)):
            total = total + chosen[h, s]
        pasted.append(total > 0.5)
    f = [[None] * NPOP, [None] * NPOP]
    for j in range((NPOP + 1) // 4):
        for which in range(2):
            tiles = [spread(m[j], which) for m in packed]
            for h in range(2):
                chosen_tile = tiles[0]
                for s in range(1, len(packed)):
                    chosen_tile = jnp.where(masks[h][s], tiles[s], chosen_tile)
                for i in (4 * j + 2 * which, 4 * j + 2 * which + 1):
                    if i < NPOP:
                        tile = roll_rows(chosen_tile, -(i % 2))
                        here = coarse[0, i, :, half_lanes(h)]
                        here = jnp.where(row == 2, roll_rows(here, 3), here)
                        f[h][i] = jnp.where(pasted[h], tile, here)
    ends = []
    for h in range(2):
        s = solid[0, :, half_lanes(h)]
        s = jnp.where(row == 2, roll_rows(s, 3), s)
        s = jnp.where(row == 6, rim_row(below, MOVING, h, 1), s)
        s = jnp.where(row == 4, rim_row(above, MOVING, h, -1), s)
        ends.append(collide(f[h], s, TAU_COARSE))
    for i in range(NPOP):
        cx, cy, cz = (int(c) for c in VEL[i])
        halves = []
        for h in range(2):
            v = jnp.where(row == 0, ends[h][i], middle[i, h])
            v = jnp.where(row == ROWS - 1, roll_rows(ends[h][i], 5), v)
            if cx > 0:
                rim = rim_row(below, FORWARD.index(i), h, 1)
                rim = jnp.where(pasted[h], roll_rows(ends[h][i], 2), rim)
                v = jnp.where(row == 0, rim, roll_rows(v, 1))
            elif cx < 0:
                rim = rim_row(above, BACKWARD.index(i), h, -1)
                rim = jnp.where(pasted[h], roll_rows(ends[h][i], 3), rim)
                v = jnp.where(row == ROWS - 1, rim, roll_rows(v, -1))
            halves.append(v)
        for h, v in enumerate(shift_plane(halves, cy, cz)):
            out[0, i, :, half_lanes(h)] = v


def peers(groups):
    return [0, *range(1, groups)]


def held(array):
    return pltpu.with_memory_space_constraint(array, VMEM)


def left(array):
    return pltpu.with_memory_space_constraint(array, pltpu.HBM)


def in_vmem(*shape):
    return VMEM(shape, jnp.float32)


def call(kernel, args, specs, outs, scratch=(), flops=0, name=None):
    single = not isinstance(outs, (list, tuple))
    outs = [outs] if single else list(outs)
    result = pl.pallas_call(
        kernel,
        in_specs=[pl.BlockSpec(memory_space=s) for s in specs],
        out_specs=[pl.BlockSpec(memory_space=VMEM)] * len(outs),
        out_shape=outs,
        scratch_shapes=list(scratch),
        compiler_params=pltpu.CompilerParams(vmem_limit_bytes=24 << 20),
        cost_estimate=pl.CostEstimate(flops=flops, bytes_accessed=1 << 20, transcendentals=0),
        name=name,
    )(*args)
    return result[0] if single else result


def per_device(fine_pops, fine_solid, coarse_pops, coarse_solid, coarse_slot):
    groups = lax.axis_size("grp")
    blocks = lax.axis_size("blk")
    own, high, low = call(
        pack_kernel,
        tuple(map(left, (fine_pops, fine_solid, coarse_pops, coarse_solid))),
        [pl.ANY] * 4,
        [in_vmem(NPOP + 1, 2, *TILE), in_vmem(WORDS, *TILE), in_vmem(WORDS, *TILE)],
        [
            in_vmem(NPOP + 1, ROWS, 2 * LANES),
            in_vmem(NPOP + 1, *TILE),
            pltpu.SemaphoreType.DMA((2,)),
        ],
        name="pack",
    )
    forward = [(i, (i + 1) % blocks) for i in range(blocks)]
    backward = [(i, (i - 1) % blocks) for i in range(blocks)]
    below = lax.ppermute(high, "blk", forward)
    above = lax.ppermute(low, "blk", backward)

    fine_v, solid_v = held(fine_pops), held(fine_solid)
    coarse_v, coarse_solid_v = held(coarse_pops), held(coarse_solid)
    inner, packed_inner, chosen, moved = call(
        inner_kernel,
        (fine_v, solid_v, held(own), held(coarse_slot)),
        [VMEM] * 4,
        [
            in_vmem(NPOP, 2, 2 * ROWS, LANES),
            in_vmem((NPOP + 1) // 2, *TILE),
            in_vmem(2, groups, *TILE),
            in_vmem(NPOP, 2, *TILE),
        ],
        [in_vmem(NPOP, 2, 2 * ROWS, LANES)],
        name="inner",
    )

    def around(array):
        swaps = [[(i, i ^ s) for i in range(groups)] for s in peers(groups)[1:]]
        return [array] + [lax.ppermute(array, "grp", swap) for swap in swaps]

    inner_parts = around(packed_inner)
    edges, packed_edges = call(
        edge_kernel,
        (held(own), held(moved), held(below), held(above)),
        [VMEM] * 4,
        [in_vmem(NPOP, 2, *TILE), in_vmem((NPOP + 1) // 4, *TILE)],
        name="edge",
    )
    edge_parts = around(packed_edges)
    fine_out = call(
        write_kernel,
        (held(inner), held(edges)),
        [VMEM] * 2,
        jax.ShapeDtypeStruct(fine_pops.shape, jnp.float32),
        name="write",
    )
    middle = call(
        coarse_kernel,
        (coarse_v, coarse_solid_v, held(chosen), *map(held, inner_parts)),
        [VMEM] * (3 + groups),
        in_vmem(NPOP, 2, *TILE),
        name="coarse",
    )
    coarse_out = call(
        last_kernel,
        (
            coarse_v,
            coarse_solid_v,
            held(chosen),
            held(below),
            held(above),
            held(middle),
            *map(held, edge_parts),
        ),
        [VMEM] * (6 + groups),
        jax.ShapeDtypeStruct(coarse_pops.shape, jnp.float32),
        name="last",
    )
    return fine_out, coarse_out


def solution(mesh):
    placed = (
        P("grp", None, "blk", None),
        P("grp", "blk", None),
        P("grp", None, "blk", None),
        P("grp", "blk", None),
        P(),
    )
    return jax.shard_map(
        per_device,
        mesh=mesh,
        in_specs=placed,
        out_specs=(P("grp", None, "blk", None), P("grp", None, "blk", None)),
        check_vma=False,
    )
```

```python
import jax
import jax.numpy as jnp
import numpy as np
from jax import lax
from jax.experimental import pallas as pl
from jax.experimental.pallas import tpu as pltpu
from jax.sharding import PartitionSpec as P

VEL = np.array(
    [
        [0, 0, 0],
        [1, 0, 0],
        [-1, 0, 0],
        [0, 1, 0],
        [0, -1, 0],
        [0, 0, 1],
        [0, 0, -1],
        [1, 1, 0],
        [-1, -1, 0],
        [1, -1, 0],
        [-1, 1, 0],
        [1, 0, 1],
        [-1, 0, -1],
        [1, 0, -1],
        [-1, 0, 1],
        [0, 1, 1],
        [0, -1, -1],
        [0, 1, -1],
        [0, -1, 1],
    ]
)
NPOP = 19
BX = 16
TAU_FINE = 0.6
TAU_COARSE = 0.55
RESCALE = 2.0 * TAU_COARSE / TAU_FINE

ROWS, LANES = 8, 128
TILE = (ROWS, LANES)
VMEM = pltpu.VMEM


def row_ids():
    return lax.broadcasted_iota(jnp.int32, TILE, 0)


def lane_ids():
    return lax.broadcasted_iota(jnp.int32, TILE, 1)


def roll_rows(tile, shift):
    return pltpu.roll(tile, shift % ROWS, 0)


def roll_lanes(tile, shift):
    return pltpu.roll(tile, shift % LANES, 1)


def moments(f, scale):
    minus = [f[i] - f[i + 1] for i in range(1, NPOP, 2)]
    plus = [f[i] + f[i + 1] for i in range(1, NPOP, 2)]
    rho = ((f[0] + plus[0]) + (plus[1] + plus[2])) + (
        (plus[3] + plus[4]) + (plus[5] + plus[6])
    ) + (plus[7] + plus[8])
    jx = (minus[0] + minus[3]) + (minus[4] + minus[5]) + minus[6]
    jy = (minus[1] + minus[3]) - (minus[4] - minus[7]) + minus[8]
    jz = (minus[2] + minus[5]) - (minus[6] - minus[7]) - minus[8]
    inverse = 1.5 / rho
    ux, uy, uz = jx * inverse, jy * inverse, jz * inverse
    amount = scale(rho)
    base = amount * (1.0 - (2.0 / 3.0) * (ux * ux + uy * uy + uz * uz))
    directions = [ux, uy, uz, ux + uy, ux - uy, ux + uz, ux - uz, uy + uz, uy - uz]
    base_axis, base_diag = base * (1.0 / 18.0), base * (1.0 / 36.0)
    amount_axis, amount_diag = amount * (1.0 / 9.0), amount * (1.0 / 18.0)
    pairs = []
    for k, along in enumerate(directions):
        odd = (amount_axis if k < 3 else amount_diag) * along
        pairs.append(((base_axis if k < 3 else base_diag) + odd * along, odd))
    return base * (1.0 / 3.0), pairs, plus, minus


def collide(f, solid, tau):
    rate = (1.0 - solid) * (1.0 / tau)
    rest, pairs, plus, minus = moments(f, lambda rho: rate * rho)
    keep = 1.0 - rate
    half = 0.5 * keep
    half_odd = half - solid
    out = [keep * f[0] + rest]
    for (even, odd), p, m in zip(pairs, plus, minus):
        symmetric = half * p + even
        antisymmetric = half_odd * m + odd
        out += [symmetric + antisymmetric, symmetric - antisymmetric]
    return out


def restrict(f):
    rest, pairs, _, _ = moments(f, lambda rho: (1.0 - RESCALE) * rho)
    out = [RESCALE * f[0] + rest]
    for k, (even, odd) in enumerate(pairs):
        out += [RESCALE * f[2 * k + 1] + (even + odd), RESCALE * f[2 * k + 2] + (even - odd)]
    return out


def shift_plane(halves, cy, cz):
    lane = lane_ids()
    if cz:
        edge = lane % BX == (0 if cz > 0 else BX - 1)
        halves = [
            jnp.where(
                edge,
                roll_lanes(v, BX * cy + cz - BX * cz),
                roll_lanes(v, BX * cy + cz),
            )
            for v in halves
        ]
    elif cy:
        halves = [roll_lanes(v, BX * cy) for v in halves]
    if cy:
        carried = lane < BX if cy > 0 else lane >= LANES - BX
        halves = [
            jnp.where(carried, halves[1], halves[0]),
            jnp.where(carried, halves[0], halves[1]),
        ]
    return halves


def shift_ring(tiles, cx):
    if not cx:
        return tiles
    row = row_ids()
    turned = [roll_rows(t, cx) for t in tiles]
    if len(tiles) == 1:
        return turned
    edge = row == (0 if cx > 0 else ROWS - 1)
    n = len(tiles)
    return [jnp.where(edge, turned[(i - cx) % n], turned[i]) for i in range(n)]


def move_in_planes(halves):
    moved = [
        shift_plane([halves[0][i], halves[1][i]], int(VEL[i, 1]), int(VEL[i, 2]))
        for i in range(NPOP)
    ]
    return [[moved[i][h] for i in range(NPOP)] for h in range(2)]


def move_along(ring):
    out = [[[], []] for _ in ring]
    for h in range(2):
        for i in range(NPOP):
            for t, v in enumerate(shift_ring([tile[h][i] for tile in ring], int(VEL[i, 0]))):
                out[t][h].append(v)
    return out


def merge(mask, first, second):
    return [
        [jnp.where(mask, v, w) for v, w in zip(a, b)] for a, b in zip(first, second)
    ]


def squeeze(halves):
    even = lane_ids() % 2 == 0
    first = jnp.where(even, halves[0], roll_lanes(halves[1], 1))
    second = jnp.where(even, roll_lanes(halves[0], -1), halves[1])
    both = first + second
    return both + roll_lanes(both, -BX)


def pair_up(first, second):
    if second is None:
        return first
    return jnp.where(lane_ids() // BX % 2 == 1, roll_lanes(second, BX), first)


def spread(tile, which):
    lane = lane_ids()
    y, z = lane // BX, lane % BX
    source = 2 * BX * (y % 4) + BX * which + 2 * (z % 8) + y // 4
    return jnp.take_along_axis(tile, source, axis=1, mode="promise_in_bounds")


def half_lanes(h):
    return pl.ds(h * LANES, LANES)


FORWARD = [i for i in range(NPOP) if VEL[i, 0] > 0]
LEVEL = [i for i in range(NPOP) if VEL[i, 0] == 0]
BACKWARD = [i for i in range(NPOP) if VEL[i, 0] < 0]
MOVING = len(FORWARD)
FIRST_LEVEL = MOVING
FIRST_PAIR = FIRST_LEVEL + len(LEVEL)
WORDS = FIRST_PAIR + (MOVING + 1) // 2
FIRST_RIM = FIRST_LEVEL + 1


def pack_message(message, tile, rim, towards, away, up):
    place = row_ids() % 4
    spare = place == (0 if up > 0 else 3)
    near = place >= 2 if up > 0 else place < 2
    for k, i in enumerate(towards):
        message[k] = tile(i)
    for k, i in enumerate(LEVEL):
        other = roll_rows(tile(NPOP), -up) if k == 0 else rim(k - 1)
        message[FIRST_LEVEL + k] = tile(i) if other is None else jnp.where(spare, other, tile(i))
    for k in range((MOVING + 1) // 2):
        second = away[2 * k + 1] if 2 * k + 1 < MOVING else NPOP
        message[FIRST_PAIR + k] = jnp.where(near, tile(away[2 * k]), roll_rows(tile(second), -2 * up))


def unpack_message(message, towards, away, up):
    near = row_ids() % 4 >= 2 if up > 0 else row_ids() % 4 < 2
    found = [None] * (NPOP + 1)
    for k, i in enumerate(towards):
        found[i] = message[k]
    for k, i in enumerate(LEVEL):
        found[i] = message[FIRST_LEVEL + k]
    for k in range((MOVING + 1) // 2):
        tile = message[FIRST_PAIR + k]
        found[away[2 * k]] = tile
        found[away[2 * k + 1] if 2 * k + 1 < MOVING else NPOP] = roll_rows(tile, 2 * up)
    found[NPOP] = jnp.where(near, found[NPOP], roll_rows(message[FIRST_LEVEL], up))
    return found


def rim_row(message, k, h, up):
    row = (4, 0)[h] if up > 0 else (3, 7)[h]
    return jnp.broadcast_to(message[FIRST_RIM + k, pl.ds(row, 1), :], TILE)


def pack_kernel(fine, solid, coarse, coarse_solid, own, high, low, strip, rim, sem):
    planes = fine.shape[2]
    last = coarse.shape[2] - 1

    def bring(source, target, which):
        pltpu.make_async_copy(source, target, sem.at[which]).start()

    def arrive(target, which):
        pltpu.make_async_copy(target, target, sem.at[which]).wait()

    ends = ((0, 0), (planes - 4, 4))
    for h in range(2):
        at = half_lanes(h)
        for first, row in ends:
            bring(fine.at[0, :, pl.ds(first, 4), at], strip.at[pl.ds(0, NPOP), pl.ds(row, 4), at], 0)
    for first, row in ends:
        bring(solid.at[0, pl.ds(first, 4), :], strip.at[NPOP, pl.ds(row, 4), :], 0)
    for plane, h, row in ((last, 1, 0), (last, 0, 4), (0, 0, 3), (0, 1, 7)):
        target = rim.at[pl.ds(0, NPOP), pl.ds(row, 1), :]
        bring(coarse.at[0, :, pl.ds(plane, 1), half_lanes(h)], target, 1)
        bring(coarse_solid.at[0, pl.ds(plane, 1), half_lanes(h)], rim.at[NPOP, pl.ds(row, 1), :], 1)
    arrive(strip, 0)
    for h in range(2):
        at = half_lanes(h)
        s = strip[NPOP, :, at]
        out = collide([strip[i, :, at] for i in range(NPOP)], s, TAU_FINE)
        for i, v in enumerate(out + [s]):
            own[i, h] = v
    arrive(rim.at[:, pl.ds(0, 4), :], 1)
    s = rim[NPOP]
    ends = collide([rim[i] for i in range(NPOP)], s, TAU_COARSE) + [s]
    upper = row_ids() < 4

    def ending(i):
        return jnp.where(upper, roll_rows(own[i, 1], 4), own[i, 0])

    def beginning(i):
        return jnp.where(upper, own[i, 0], roll_rows(own[i, 1], 4))

    def rim_of(towards):
        return lambda k: ends[(towards + [NPOP])[k]] if k <= MOVING else None

    pack_message(high, ending, rim_of(FORWARD), FORWARD, BACKWARD, 1)
    pack_message(low, beginning, rim_of(BACKWARD), BACKWARD, FORWARD, -1)


def inner_kernel(fine, solid, own, slot, inner, packed, chosen, moved, work):
    groups = chosen.shape[1]
    upper = row_ids() < 4

    def middle(ref, h, *i):
        at = half_lanes(h)
        return jnp.where(upper, ref[(0, *i, pl.ds(ROWS, ROWS), at)], ref[(0, *i, pl.ds(0, ROWS), at)])

    outer = move_in_planes([[own[i, h] for i in range(NPOP)] for h in range(2)])
    center = move_in_planes(
        [
            collide([middle(fine, h, i) for i in range(NPOP)], middle(solid, h), TAU_FINE)
            for h in range(2)
        ]
    )
    for i in range(NPOP):
        for h in range(2):
            moved[i, h] = outer[h][i]
    ring = move_along([merge(upper, outer, center), merge(upper, center, outer)])
    for t in range(2):
        for h in range(2):
            s = solid[0, pl.ds(ROWS * t, ROWS), half_lanes(h)]
            ring[t][h] = collide(ring[t][h], s, TAU_FINE)
        ring[t] = move_in_planes(ring[t])
    ring = move_along(ring)
    for i in range(NPOP):
        for h in range(2):
            for t in range(2):
                inner[i, h, pl.ds(ROWS * t, ROWS), :] = ring[t][h][i]
                work[i, h, pl.ds(ROWS * t, ROWS), :] = ring[t][h][i]
    mean = []
    for i in range(NPOP):
        halves = [
            work[i, h, pl.ds(0, ROWS, stride=2), :] + work[i, h, pl.ds(1, ROWS, stride=2), :]
            for h in range(2)
        ]
        mean.append(0.125 * squeeze(halves))
    out = restrict(mean) + [None]
    for j in range((NPOP + 1) // 2):
        packed[j] = pair_up(out[2 * j], out[2 * j + 1])
    me = lax.axis_index("grp")
    codes = slot[...].reshape(1, groups)
    group_ids = lax.broadcasted_iota(jnp.int32, codes.shape, 1)
    quadrant = 4 * me + lane_ids() % BX // 8
    for s in range(groups):
        code = jnp.sum(jnp.where(group_ids == me ^ s, codes, 0), axis=1, keepdims=True)
        for h in range(2):
            chosen[h, s] = jnp.where(quadrant + 2 * h == code, 1.0, 0.0)


def edge_kernel(own, moved, below, above, coarse, coarse_solid, edges, packed):
    row = row_ids()
    upper = row < 4
    below = unpack_message(below, FORWARD, BACKWARD, 1)
    above = unpack_message(above, BACKWARD, FORWARD, -1)
    halos = [
        [jnp.where(upper, a, b) for a, b in zip(above, below)],
        [roll_rows(jnp.where(upper, b, a), 4) for a, b in zip(above, below)],
    ]
    solids = [(own[NPOP, h], halos[h][NPOP]) for h in range(2)]
    halos = move_in_planes([half[:NPOP] for half in halos])
    mine = [[moved[i, h] for i in range(NPOP)] for h in range(2)]
    low, high = (
        move_along([ring])[0] for ring in (merge(upper, mine, halos), merge(upper, halos, mine))
    )
    low = [collide(low[h], jnp.where(upper, *solids[h]), TAU_FINE) for h in range(2)]
    high = [collide(high[h], jnp.where(upper, *solids[h][::-1]), TAU_FINE) for h in range(2)]
    low, high = (move_along([ring])[0] for ring in (low, high))
    high = [[roll_rows(v, 4) for v in half] for half in high]
    both = move_in_planes(merge((row < 2) | (row >= 6), low, high))
    sums = [[v + roll_rows(v, -1) for v in half] + [None] for half in both]
    odd = row % 2 == 1
    mean = []
    for i in range(0, NPOP, 2):
        pair = [half[i] if half[i + 1] is None else jnp.where(odd, roll_rows(half[i + 1], 1), half[i]) for half in sums]
        pair = 0.125 * squeeze(pair)
        mean += [pair, roll_rows(pair, -1)]
    out = restrict(mean[:NPOP]) + [None]
    pairs = [
        out[i] if out[i + 1] is None else jnp.where(odd, roll_rows(out[i + 1], 1), out[i])
        for i in range(0, NPOP, 2)
    ]
    for j in range(len(pairs) // 2):
        packed[j] = pair_up(pairs[2 * j], pairs[2 * j + 1])
    for i in range(NPOP):
        for h in range(2):
            edges[i, h] = both[h][i]


def write_kernel(inner, edges, out):
    row = row_ids()
    for i in range(NPOP):
        for h in range(2):
            edge = edges[i, h]
            out[0, i, pl.ds(0, ROWS), half_lanes(h)] = jnp.where(
                row < 2, edge, inner[i, h, pl.ds(0, ROWS), :]
            )
            out[0, i, pl.ds(ROWS, ROWS), half_lanes(h)] = jnp.where(
                row >= 6, roll_rows(edge, 4), inner[i, h, pl.ds(ROWS, ROWS), :]
            )


def split_kernel(after, tiles, first, second):
    half = first.shape[0]
    first[...] = tiles[pl.ds(0, half)]
    second[...] = tiles[pl.ds(half, half)]


def paste_kernel(coarse, chosen, *refs):
    packed, out = refs[:-1], refs[-1]
    groups = [1, *range(0, chosen.shape[1], 2)]
    for i in range(NPOP):
        tiles = [spread(m[i // 2], i % 2) for m in packed]
        for h in range(2):
            v = coarse[0, i, :, half_lanes(h)]
            for s, tile in zip(groups, tiles):
                v = jnp.where(chosen[h, s] > 0.5, tile, v)
            out[i, h] = v


def last_kernel(coarse, solid, chosen, below, above, base, *refs):
    groups = chosen.shape[1]
    packed, relayed, out = refs[:groups], refs[groups:-1], refs[-1]
    row = row_ids()
    masks = [[chosen[h, s] > 0.5 for s in range(len(packed))] for h in range(2)]
    pasted = []
    for h in range(2):
        total = chosen[h, 0]
        for s in range(1, len(packed)):
            total = total + chosen[h, s]
        pasted.append(total > 0.5)
    f = [[None] * NPOP, [None] * NPOP]
    for j in range((NPOP + 1) // 4):
        for which in range(2):
            tiles = [spread(m[j], which) for m in packed]
            for h in range(2):
                chosen_tile = tiles[0]
                for s in range(1, len(packed)):
                    chosen_tile = jnp.where(masks[h][s], tiles[s], chosen_tile)
                for i in (4 * j + 2 * which, 4 * j + 2 * which + 1):
                    if i < NPOP:
                        tile = roll_rows(chosen_tile, -(i % 2))
                        here = coarse[0, i, :, half_lanes(h)]
                        here = jnp.where(row == 2, roll_rows(here, 3), here)
                        f[h][i] = jnp.where(pasted[h], tile, here)
    middle = [[], []]
    for i in range(NPOP):
        half, at = divmod(i // 2, relayed[0].shape[0])
        tiles = [spread(part[at], i % 2) for part in relayed[half::2]]
        for h in range(2):
            v = base[i, h]
            for s, tile in enumerate(tiles):
                v = jnp.where(masks[h][2 * s + 3], tile, v)
            middle[h].append(v)
    middle = [collide(middle[h], solid[0, :, half_lanes(h)], TAU_COARSE) for h in range(2)]
    ends = []
    for h in range(2):
        s = solid[0, :, half_lanes(h)]
        s = jnp.where(row == 2, roll_rows(s, 3), s)
        s = jnp.where(row == 6, rim_row(below, MOVING, h, 1), s)
        s = jnp.where(row == 4, rim_row(above, MOVING, h, -1), s)
        ends.append(collide(f[h], s, TAU_COARSE))
    for i in range(NPOP):
        cx, cy, cz = (int(c) for c in VEL[i])
        halves = []
        for h in range(2):
            v = jnp.where(row == 0, ends[h][i], middle[h][i])
            v = jnp.where(row == ROWS - 1, roll_rows(ends[h][i], 5), v)
            if cx > 0:
                rim = rim_row(below, FORWARD.index(i), h, 1)
                rim = jnp.where(pasted[h], roll_rows(ends[h][i], 2), rim)
                v = jnp.where(row == 0, rim, roll_rows(v, 1))
            elif cx < 0:
                rim = rim_row(above, BACKWARD.index(i), h, -1)
                rim = jnp.where(pasted[h], roll_rows(ends[h][i], 3), rim)
                v = jnp.where(row == ROWS - 1, rim, roll_rows(v, -1))
            halves.append(v)
        for h, v in enumerate(shift_plane(halves, cy, cz)):
            out[0, i, :, half_lanes(h)] = v


def exchange(array, distance):
    groups = lax.axis_size("grp")
    return lax.ppermute(array, "grp", [(i, i ^ distance) for i in range(groups)])


def held(array):
    return pltpu.with_memory_space_constraint(array, VMEM)


def left(array):
    return pltpu.with_memory_space_constraint(array, pltpu.HBM)


def in_vmem(*shape):
    return VMEM(shape, jnp.float32)


def call(kernel, args, specs, outs, scratch=(), flops=0, name=None):
    single = not isinstance(outs, (list, tuple))
    outs = [outs] if single else list(outs)
    result = pl.pallas_call(
        kernel,
        in_specs=[pl.BlockSpec(memory_space=s) for s in specs],
        out_specs=[pl.BlockSpec(memory_space=VMEM)] * len(outs),
        out_shape=outs,
        scratch_shapes=list(scratch),
        compiler_params=pltpu.CompilerParams(vmem_limit_bytes=24 << 20),
        cost_estimate=pl.CostEstimate(flops=flops, bytes_accessed=1 << 20, transcendentals=0),
        name=name,
    )(*args)
    return result[0] if single else result


def per_device(fine_pops, fine_solid, coarse_pops, coarse_solid, coarse_slot):
    groups = lax.axis_size("grp")
    blocks = lax.axis_size("blk")
    own, high, low = call(
        pack_kernel,
        tuple(map(left, (fine_pops, fine_solid, coarse_pops, coarse_solid))),
        [pl.ANY] * 4,
        [in_vmem(NPOP + 1, 2, *TILE), in_vmem(WORDS, *TILE), in_vmem(WORDS, *TILE)],
        [
            in_vmem(NPOP + 1, ROWS, 2 * LANES),
            in_vmem(NPOP + 1, *TILE),
            pltpu.SemaphoreType.DMA((2,)),
        ],
        name="pack",
    )
    forward = [(i, (i + 1) % blocks) for i in range(blocks)]
    backward = [(i, (i - 1) % blocks) for i in range(blocks)]
    below = lax.ppermute(high, "blk", forward)
    above = lax.ppermute(low, "blk", backward)

    fine_v, solid_v = held(fine_pops), held(fine_solid)
    coarse_v, coarse_solid_v = held(coarse_pops), held(coarse_solid)
    inner, packed_inner, chosen, moved = call(
        inner_kernel,
        (fine_v, solid_v, held(own), held(coarse_slot)),
        [VMEM] * 4,
        [
            in_vmem(NPOP, 2, 2 * ROWS, LANES),
            in_vmem((NPOP + 1) // 2, *TILE),
            in_vmem(2, groups, *TILE),
            in_vmem(NPOP, 2, *TILE),
        ],
        [in_vmem(NPOP, 2, 2 * ROWS, LANES)],
        name="inner",
    )

    across = [exchange(packed_inner, s) for s in range(2, groups, 2)]
    beside = exchange(packed_inner, 1)
    edges, packed_edges = call(
        edge_kernel,
        (held(own), held(moved), held(below), held(above), coarse_v, coarse_solid_v),
        [VMEM] * 6,
        [in_vmem(NPOP, 2, *TILE), in_vmem((NPOP + 1) // 4, *TILE)],
        name="edge",
    )
    edge_parts = [packed_edges] + [exchange(packed_edges, s) for s in range(1, groups)]
    fine_out = call(
        write_kernel,
        (held(inner), held(edges)),
        [VMEM] * 2,
        jax.ShapeDtypeStruct(fine_pops.shape, jnp.float32),
        name="write",
    )
    relayed = []
    for part in across:
        halves = call(
            split_kernel,
            (held(edges), held(part)),
            [VMEM] * 2,
            [in_vmem(part.shape[0] // 2, *TILE)] * 2,
            name="split",
        )
        relayed += [exchange(half, 1) for half in halves]
    inner_parts = [beside, packed_inner, *across]
    base = call(
        paste_kernel,
        (coarse_v, held(chosen), *map(held, inner_parts)),
        [VMEM] * (2 + len(inner_parts)),
        in_vmem(NPOP, 2, *TILE),
        name="paste",
    )
    coarse_out = call(
        last_kernel,
        (
            coarse_v,
            coarse_solid_v,
            held(chosen),
            held(below),
            held(above),
            held(base),
            *map(held, edge_parts),
            *map(held, relayed),
        ),
        [VMEM] * (6 + len(edge_parts) + len(relayed)),
        jax.ShapeDtypeStruct(coarse_pops.shape, jnp.float32),
        name="last",
    )
    return fine_out, coarse_out


def solution(mesh):
    placed = (
        P("grp", None, "blk", None),
        P("grp", "blk", None),
        P("grp", None, "blk", None),
        P("grp", "blk", None),
        P(),
    )
    return jax.shard_map(
        per_device,
        mesh=mesh,
        in_specs=placed,
        out_specs=(P("grp", None, "blk", None), P("grp", None, "blk", None)),
        check_vma=False,
    )
```

```python
import jax
import jax.numpy as jnp
import numpy as np
from jax import lax
from jax.experimental import pallas as pl
from jax.experimental.pallas import tpu as pltpu
from jax.sharding import PartitionSpec as P

VEL = np.array(
    [
        [0, 0, 0],
        [1, 0, 0],
        [-1, 0, 0],
        [0, 1, 0],
        [0, -1, 0],
        [0, 0, 1],
        [0, 0, -1],
        [1, 1, 0],
        [-1, -1, 0],
        [1, -1, 0],
        [-1, 1, 0],
        [1, 0, 1],
        [-1, 0, -1],
        [1, 0, -1],
        [-1, 0, 1],
        [0, 1, 1],
        [0, -1, -1],
        [0, 1, -1],
        [0, -1, 1],
    ]
)
NPOP = 19
BX = 16
TAU_FINE = 0.6
TAU_COARSE = 0.55
RESCALE = 2.0 * TAU_COARSE / TAU_FINE

ROWS, LANES = 8, 128
TILE = (ROWS, LANES)
VMEM = pltpu.VMEM


def row_ids():
    return lax.broadcasted_iota(jnp.int32, TILE, 0)


def lane_ids():
    return lax.broadcasted_iota(jnp.int32, TILE, 1)


def roll_rows(tile, shift):
    return pltpu.roll(tile, shift % ROWS, 0)


def roll_lanes(tile, shift):
    return pltpu.roll(tile, shift % LANES, 1)


def moments(f, scale):
    minus = [f[i] - f[i + 1] for i in range(1, NPOP, 2)]
    plus = [f[i] + f[i + 1] for i in range(1, NPOP, 2)]
    rho = ((f[0] + plus[0]) + (plus[1] + plus[2])) + (
        (plus[3] + plus[4]) + (plus[5] + plus[6])
    ) + (plus[7] + plus[8])
    jx = (minus[0] + minus[3]) + (minus[4] + minus[5]) + minus[6]
    jy = (minus[1] + minus[3]) - (minus[4] - minus[7]) + minus[8]
    jz = (minus[2] + minus[5]) - (minus[6] - minus[7]) - minus[8]
    inverse = 1.5 / rho
    ux, uy, uz = jx * inverse, jy * inverse, jz * inverse
    amount = scale(rho)
    base = amount * (1.0 - (2.0 / 3.0) * (ux * ux + uy * uy + uz * uz))
    directions = [ux, uy, uz, ux + uy, ux - uy, ux + uz, ux - uz, uy + uz, uy - uz]
    base_axis, base_diag = base * (1.0 / 18.0), base * (1.0 / 36.0)
    amount_axis, amount_diag = amount * (1.0 / 9.0), amount * (1.0 / 18.0)
    pairs = []
    for k, along in enumerate(directions):
        odd = (amount_axis if k < 3 else amount_diag) * along
        pairs.append(((base_axis if k < 3 else base_diag) + odd * along, odd))
    return base * (1.0 / 3.0), pairs, plus, minus


def collide(f, solid, tau):
    rate = (1.0 - solid) * (1.0 / tau)
    rest, pairs, plus, minus = moments(f, lambda rho: rate * rho)
    keep = 1.0 - rate
    half = 0.5 * keep
    half_odd = half - solid
    out = [keep * f[0] + rest]
    for (even, odd), p, m in zip(pairs, plus, minus):
        symmetric = half * p + even
        antisymmetric = half_odd * m + odd
        out += [symmetric + antisymmetric, symmetric - antisymmetric]
    return out


def restrict(f):
    rest, pairs, _, _ = moments(f, lambda rho: (1.0 - RESCALE) * rho)
    out = [RESCALE * f[0] + rest]
    for k, (even, odd) in enumerate(pairs):
        out += [RESCALE * f[2 * k + 1] + (even + odd), RESCALE * f[2 * k + 2] + (even - odd)]
    return out


def shift_plane(halves, cy, cz):
    lane = lane_ids()
    if cz:
        edge = lane % BX == (0 if cz > 0 else BX - 1)
        halves = [
            jnp.where(
                edge,
                roll_lanes(v, BX * cy + cz - BX * cz),
                roll_lanes(v, BX * cy + cz),
            )
            for v in halves
        ]
    elif cy:
        halves = [roll_lanes(v, BX * cy) for v in halves]
    if cy:
        carried = lane < BX if cy > 0 else lane >= LANES - BX
        halves = [
            jnp.where(carried, halves[1], halves[0]),
            jnp.where(carried, halves[0], halves[1]),
        ]
    return halves


def shift_ring(tiles, cx):
    if not cx:
        return tiles
    row = row_ids()
    turned = [roll_rows(t, cx) for t in tiles]
    if len(tiles) == 1:
        return turned
    edge = row == (0 if cx > 0 else ROWS - 1)
    n = len(tiles)
    return [jnp.where(edge, turned[(i - cx) % n], turned[i]) for i in range(n)]


def move_in_planes(halves):
    moved = [
        shift_plane([halves[0][i], halves[1][i]], int(VEL[i, 1]), int(VEL[i, 2]))
        for i in range(NPOP)
    ]
    return [[moved[i][h] for i in range(NPOP)] for h in range(2)]


def move_along(ring):
    out = [[[], []] for _ in ring]
    for h in range(2):
        for i in range(NPOP):
            for t, v in enumerate(shift_ring([tile[h][i] for tile in ring], int(VEL[i, 0]))):
                out[t][h].append(v)
    return out


def merge(mask, first, second):
    return [
        [jnp.where(mask, v, w) for v, w in zip(a, b)] for a, b in zip(first, second)
    ]


def squeeze(halves):
    even = lane_ids() % 2 == 0
    first = jnp.where(even, halves[0], roll_lanes(halves[1], 1))
    second = jnp.where(even, roll_lanes(halves[0], -1), halves[1])
    both = first + second
    return both + roll_lanes(both, -BX)


def pair_up(first, second):
    if second is None:
        return first
    return jnp.where(lane_ids() // BX % 2 == 1, roll_lanes(second, BX), first)


def spread(tile, which):
    lane = lane_ids()
    y, z = lane // BX, lane % BX
    source = 2 * BX * (y % 4) + BX * which + 2 * (z % 8) + y // 4
    return jnp.take_along_axis(tile, source, axis=1, mode="promise_in_bounds")


def half_lanes(h):
    return pl.ds(h * LANES, LANES)


FORWARD = [i for i in range(NPOP) if VEL[i, 0] > 0]
LEVEL = [i for i in range(NPOP) if VEL[i, 0] == 0]
BACKWARD = [i for i in range(NPOP) if VEL[i, 0] < 0]
MOVING = len(FORWARD)

PAIRS = (len(LEVEL) + 1) // 2
FIRST_RIM = MOVING + PAIRS
WORDS = FIRST_RIM + (MOVING + 1 + 3) // 4


def pick(*choices):
    row = row_ids()
    out = choices[-1][-1]
    for rows, tile in choices[-2::-1]:
        mask = row == rows[0]
        for r in rows[1:]:
            mask = mask | (row == r)
        out = jnp.where(mask, tile, out)
    return out


def pack_message(message, first, second, rim, up):
    for k, i in enumerate(FORWARD if up else BACKWARD):
        f, s = [first(i, h) for h in range(2)], [second(i, h) for h in range(2)]
        if up:
            message[k] = pick(
                ((7, 0), roll_rows(f[0], 1)),
                ((1, 2), roll_rows(f[1], 3)),
                ((3, 4), roll_rows(s[0], -2)),
                (s[1],),
            )
        else:
            message[k] = pick(
                ((3, 4), roll_rows(f[0], 3)),
                ((5, 6), roll_rows(f[1], 5)),
                ((7, 0), roll_rows(s[0], -2)),
                (s[1],),
            )
    for k in range(PAIRS):
        shared = []
        for i in (LEVEL + [NPOP])[2 * k : 2 * k + 2]:
            f = [first(i, h) for h in range(2)]
            s = [second(i, h) for h in range(2)] if i < NPOP else f
            if up:
                shared.append(
                    pick(
                        ((7,), f[0]),
                        ((1,), roll_rows(f[1], 2)),
                        ((3,), roll_rows(s[0], -3)),
                        (roll_rows(s[1], -1),),
                    )
                )
            else:
                shared.append(
                    pick(
                        ((4,), roll_rows(f[0], 4)),
                        ((6,), roll_rows(f[1], -2)),
                        ((0,), roll_rows(s[0], -1)),
                        (roll_rows(s[1], 1),),
                    )
                )
        own_rows = (1, 3, 5, 7) if up else (0, 2, 4, 6)
        message[MOVING + k] = pick((own_rows, shared[0]), (roll_rows(shared[1], 1),))
    for j in range(WORDS - FIRST_RIM):
        tile = None
        for k, v in enumerate(rim[4 * j : 4 * j + 4]):
            v = roll_rows(v, k if up else -k)
            at = k if up else 3 - k
            tile = v if tile is None else jnp.where(row_ids() % 4 == at, v, tile)
        message[FIRST_RIM + j] = tile


def shared_tile(message, i):
    k = (LEVEL + [NPOP]).index(i)
    return roll_rows(message[MOVING + k // 2], -(k % 2))


def rim_row(message, k, h, up):
    row = 4 * (1 - h) + k % 4 if up else 4 * h + 3 - k % 4
    return jnp.broadcast_to(message[FIRST_RIM + k // 4, pl.ds(row, 1), :], TILE)


def pack_kernel(fine, solid, coarse, coarse_solid, slot, moved, second, high, low, slot_out, strip, rim, sem):
    planes = fine.shape[2]
    last = coarse.shape[2] - 1

    def bring(source, target, which):
        pltpu.make_async_copy(source, target, sem.at[which]).start()

    def arrive(target, which):
        pltpu.make_async_copy(target, target, sem.at[which]).wait()

    ends = ((0, 0), (planes - 4, 4))
    for h in range(2):
        at = half_lanes(h)
        for first, row in ends:
            bring(fine.at[0, :, pl.ds(first, 4), at], strip.at[pl.ds(0, NPOP), pl.ds(row, 4), at], 0)
    for first, row in ends:
        bring(solid.at[0, pl.ds(first, 4), :], strip.at[NPOP, pl.ds(row, 4), :], 0)
    for plane, h, row in ((last, 1, 0), (last, 0, 4), (0, 0, 3), (0, 1, 7)):
        target = rim.at[pl.ds(0, NPOP), pl.ds(row, 1), :]
        bring(coarse.at[0, :, pl.ds(plane, 1), half_lanes(h)], target, 1)
        bring(coarse_solid.at[0, pl.ds(plane, 1), half_lanes(h)], rim.at[NPOP, pl.ds(row, 1), :], 1)
    bring(slot, slot_out, 2)
    arrive(strip, 0)
    solids = [strip[NPOP, :, half_lanes(h)] for h in range(2)]
    once = move_in_planes(
        [collide([strip[i, :, half_lanes(h)] for i in range(NPOP)], solids[h], TAU_FINE) for h in range(2)]
    )
    arrive(slot_out, 2)
    arrive(rim.at[:, pl.ds(0, 4), :], 1)
    s = rim[NPOP]
    outer = collide([rim[i] for i in range(NPOP)], s, TAU_COARSE) + [s]
    ring = move_along([once])[0]
    twice = [collide(ring[h], solids[h], TAU_FINE) for h in range(2)]
    for h in range(2):
        for i in range(NPOP):
            moved[i, h] = once[h][i]
            second[i, h] = twice[h][i]
        moved[NPOP, h] = solids[h]

    def first_of(i, h):
        return moved[i, h]

    def second_of(i, h):
        return second[i, h]

    pack_message(high, first_of, second_of, [outer[i] for i in FORWARD + [NPOP]], True)
    pack_message(low, first_of, second_of, [outer[i] for i in BACKWARD + [NPOP]], False)


def inner_steps(fine, solid, moved, inner, packed, work):
    upper = row_ids() < 4

    def middle(ref, h, *i):
        at = half_lanes(h)
        return jnp.where(upper, ref[(0, *i, pl.ds(ROWS, ROWS), at)], ref[(0, *i, pl.ds(0, ROWS), at)])

    outer = [[moved[i, h] for i in range(NPOP)] for h in range(2)]
    center = move_in_planes(
        [
            collide([middle(fine, h, i) for i in range(NPOP)], middle(solid, h), TAU_FINE)
            for h in range(2)
        ]
    )
    ring = move_along([merge(upper, outer, center), merge(upper, center, outer)])
    for t in range(2):
        for h in range(2):
            s = solid[0, pl.ds(ROWS * t, ROWS), half_lanes(h)]
            ring[t][h] = collide(ring[t][h], s, TAU_FINE)
        ring[t] = move_in_planes(ring[t])
    ring = move_along(ring)
    for i in range(NPOP):
        for h in range(2):
            for t in range(2):
                inner[i, h, pl.ds(ROWS * t, ROWS), :] = ring[t][h][i]
                work[i, h, pl.ds(ROWS * t, ROWS), :] = ring[t][h][i]
    mean = []
    for i in range(NPOP):
        halves = [
            work[i, h, pl.ds(0, ROWS, stride=2), :] + work[i, h, pl.ds(1, ROWS, stride=2), :]
            for h in range(2)
        ]
        mean.append(0.125 * squeeze(halves))
    out = restrict(mean) + [None]
    for j in range((NPOP + 1) // 2):
        packed[j] = pair_up(out[2 * j], out[2 * j + 1])


def starts_early():
    return lax.axis_index("blk") == 0


def early_kernel(fine, solid, moved, low, inner, packed, low_out, work):
    low_out[...] = low[...]

    @pl.when(starts_early())
    def _():
        inner_steps(fine, solid, moved, inner, packed, work)


def inner_kernel(fine, solid, moved, early_inner, early_packed, slot, inner, packed, chosen, work):
    groups = chosen.shape[1]
    me = lax.axis_index("grp")
    codes = slot[...].reshape(1, groups)
    group_ids = lax.broadcasted_iota(jnp.int32, codes.shape, 1)
    quadrant = 4 * me + lane_ids() % BX // 8
    for s in range(groups):
        code = jnp.sum(jnp.where(group_ids == me ^ s, codes, 0), axis=1, keepdims=True)
        for h in range(2):
            chosen[h, s] = jnp.where(quadrant + 2 * h == code, 1.0, 0.0)

    @pl.when(starts_early())
    def _():
        inner[...] = early_inner[...]
        packed[...] = early_packed[...]

    @pl.when(jnp.logical_not(starts_early()))
    def _():
        inner_steps(fine, solid, moved, inner, packed, work)


def edge_kernel(moved, second, below, above, coarse, coarse_solid, edges, packed):
    row = row_ids()

    def middle(i):
        v = [moved[i, h] for h in range(2)]
        if i in FORWARD:
            return pick(
                ((3, 4), roll_rows(v[0], -3)),
                ((5, 6), roll_rows(v[1], -1)),
                (below[FORWARD.index(i)],),
            )
        if i in BACKWARD:
            return pick(
                ((7, 0), roll_rows(v[0], -1)),
                ((1, 2), roll_rows(v[1], 1)),
                (above[BACKWARD.index(i)],),
            )
        return pick(
            ((0,), v[0]),
            ((2,), roll_rows(v[1], 2)),
            ((3,), roll_rows(v[0], 4)),
            ((5,), roll_rows(v[1], -2)),
            ((1, 7), shared_tile(below, i)),
            (shared_tile(above, i),),
        )

    twice = collide([middle(i) for i in range(NPOP)], middle(NPOP), TAU_FINE)
    both = [[], []]
    for h in range(2):
        for i in range(NPOP):
            cx = int(VEL[i, 0])
            v, mine = roll_rows(twice[i], cx - 2 * h), second[i, h]
            if cx > 0:
                v = pick(
                    ((0, 1, 4, 5), v),
                    ((2, 3), roll_rows(mine, -3)),
                    (roll_rows(below[FORWARD.index(i)], 3 - 2 * h),),
                )
            elif cx < 0:
                v = pick(
                    ((2, 3, 6, 7), v),
                    ((0, 1), roll_rows(mine, -1)),
                    (roll_rows(above[BACKWARD.index(i)], -3 - 2 * h),),
                )
            else:
                v = pick(
                    ((0, 3, 4, 7), v),
                    ((1,), mine),
                    ((2,), roll_rows(mine, 4)),
                    ((6,), roll_rows(shared_tile(below, i), 3 - 2 * h)),
                    (roll_rows(shared_tile(above, i), -3 - 2 * h),),
                )
            both[h].append(v)
    both = move_in_planes(both)
    sums = [[v + roll_rows(v, -1) for v in half] + [None] for half in both]
    odd = row % 2 == 1
    mean = []
    for i in range(0, NPOP, 2):
        pair = [half[i] if half[i + 1] is None else jnp.where(odd, roll_rows(half[i + 1], 1), half[i]) for half in sums]
        pair = 0.125 * squeeze(pair)
        mean += [pair, roll_rows(pair, -1)]
    out = restrict(mean[:NPOP]) + [None]
    pairs = [
        out[i] if out[i + 1] is None else jnp.where(odd, roll_rows(out[i + 1], 1), out[i])
        for i in range(0, NPOP, 2)
    ]
    for j in range(len(pairs) // 2):
        packed[j] = pair_up(pairs[2 * j], pairs[2 * j + 1])
    packed[len(pairs) // 2] = jnp.zeros(TILE, jnp.float32)
    for i in range(NPOP):
        for h in range(2):
            edges[i, h] = both[h][i]


def write_kernel(inner, edges, out):
    row = row_ids()
    for i in range(NPOP):
        for h in range(2):
            edge = edges[i, h]
            out[0, i, pl.ds(0, ROWS), half_lanes(h)] = jnp.where(
                row < 2, edge, inner[i, h, pl.ds(0, ROWS), :]
            )
            out[0, i, pl.ds(ROWS, ROWS), half_lanes(h)] = jnp.where(
                row >= 6, roll_rows(edge, 4), inner[i, h, pl.ds(ROWS, ROWS), :]
            )


def split_kernel(after, tiles, first, second):
    half = first.shape[0]
    first[...] = tiles[pl.ds(0, half)]
    second[...] = tiles[pl.ds(half, half)]


def paste_kernel(after, coarse, chosen, *refs):
    packed, out = refs[:-1], refs[-1]
    groups = [1, *range(0, chosen.shape[1], 2)]
    for i in range(NPOP):
        tiles = [spread(m[i // 2], i % 2) for m in packed]
        for h in range(2):
            v = coarse[0, i, :, half_lanes(h)]
            for s, tile in zip(groups, tiles):
                v = jnp.where(chosen[h, s] > 0.5, tile, v)
            out[i, h] = v


def last_kernel(coarse, solid, chosen, below, above, base, *refs):
    groups = chosen.shape[1]
    packed, relayed, out = refs[:groups], refs[groups:-1], refs[-1]
    row = row_ids()
    masks = [[chosen[h, s] > 0.5 for s in others(groups)] for h in range(2)]
    pasted = []
    for h in range(2):
        total = chosen[h, 0]
        for s in range(1, groups):
            total = total + chosen[h, s]
        pasted.append(total > 0.5)
    f = [[None] * NPOP, [None] * NPOP]
    for j in range((NPOP + 1) // 4):
        for which in range(2):
            tiles = [spread(m[j], which) for m in packed]
            for h in range(2):
                chosen_tile = tiles[0]
                for mask, tile in zip(masks[h], tiles[1:]):
                    chosen_tile = jnp.where(mask, tile, chosen_tile)
                for i in (4 * j + 2 * which, 4 * j + 2 * which + 1):
                    if i < NPOP:
                        tile = roll_rows(chosen_tile, -(i % 2))
                        here = coarse[0, i, :, half_lanes(h)]
                        here = jnp.where(row == 2, roll_rows(here, 3), here)
                        f[h][i] = jnp.where(pasted[h], tile, here)
    middle = [[], []]
    for i in range(NPOP):
        half, at = divmod(i // 2, relayed[0].shape[0])
        tiles = [spread(part[at], i % 2) for part in relayed[half::2]]
        for h in range(2):
            v = base[i, h]
            for s, tile in enumerate(tiles):
                v = jnp.where(chosen[h, 2 * s + 3] > 0.5, tile, v)
            middle[h].append(v)
    middle = [collide(middle[h], solid[0, :, half_lanes(h)], TAU_COARSE) for h in range(2)]
    ends = []
    for h in range(2):
        s = solid[0, :, half_lanes(h)]
        s = jnp.where(row == 2, roll_rows(s, 3), s)
        s = jnp.where(row == 6, rim_row(below, MOVING, h, True), s)
        s = jnp.where(row == 4, rim_row(above, MOVING, h, False), s)
        ends.append(collide(f[h], s, TAU_COARSE))
    for i in range(NPOP):
        cx, cy, cz = (int(c) for c in VEL[i])
        halves = []
        for h in range(2):
            v = jnp.where(row == 0, ends[h][i], middle[h][i])
            v = jnp.where(row == ROWS - 1, roll_rows(ends[h][i], 5), v)
            if cx > 0:
                rim = rim_row(below, FORWARD.index(i), h, True)
                rim = jnp.where(pasted[h], roll_rows(ends[h][i], 2), rim)
                v = jnp.where(row == 0, rim, roll_rows(v, 1))
            elif cx < 0:
                rim = rim_row(above, BACKWARD.index(i), h, False)
                rim = jnp.where(pasted[h], roll_rows(ends[h][i], 3), rim)
                v = jnp.where(row == ROWS - 1, rim, roll_rows(v, -1))
            halves.append(v)
        for h, v in enumerate(shift_plane(halves, cy, cz)):
            out[0, i, :, half_lanes(h)] = v


def others(groups):
    return range(1, groups)


def exchange(array, distance):
    groups = lax.axis_size("grp")
    return lax.ppermute(array, "grp", [(i, i ^ distance) for i in range(groups)])


def held(array):
    return pltpu.with_memory_space_constraint(array, VMEM)


def left(array):
    return pltpu.with_memory_space_constraint(array, pltpu.HBM)


def in_vmem(*shape):
    return VMEM(shape, jnp.float32)


def call(kernel, args, specs, outs, scratch=(), flops=0, name=None):
    single = not isinstance(outs, (list, tuple))
    outs = [outs] if single else list(outs)
    result = pl.pallas_call(
        kernel,
        in_specs=[pl.BlockSpec(memory_space=s) for s in specs],
        out_specs=[pl.BlockSpec(memory_space=VMEM)] * len(outs),
        out_shape=outs,
        scratch_shapes=list(scratch),
        compiler_params=pltpu.CompilerParams(vmem_limit_bytes=24 << 20),
        cost_estimate=pl.CostEstimate(flops=flops, bytes_accessed=1 << 20, transcendentals=0),
        name=name,
    )(*args)
    return result[0] if single else result


def per_device(fine_pops, fine_solid, coarse_pops, coarse_solid, coarse_slot):
    groups = lax.axis_size("grp")
    blocks = lax.axis_size("blk")
    moved, second, high, low, slot = call(
        pack_kernel,
        tuple(map(left, (fine_pops, fine_solid, coarse_pops, coarse_solid, coarse_slot))),
        [pl.ANY] * 5,
        [
            in_vmem(NPOP + 1, 2, *TILE),
            in_vmem(NPOP, 2, *TILE),
            in_vmem(WORDS, *TILE),
            in_vmem(WORDS, *TILE),
            VMEM((groups,), jnp.int32),
        ],
        [
            in_vmem(NPOP + 1, ROWS, 2 * LANES),
            in_vmem(NPOP + 1, *TILE),
            pltpu.SemaphoreType.DMA((3,)),
        ],
        name="pack",
    )
    fine_v, solid_v = held(fine_pops), held(fine_solid)
    coarse_v, coarse_solid_v = held(coarse_pops), held(coarse_solid)
    inner_shapes = [in_vmem(NPOP, 2, 2 * ROWS, LANES), in_vmem((NPOP + 1) // 2, *TILE)]
    early_inner, early_packed, low = call(
        early_kernel,
        (fine_v, solid_v, held(moved), held(low)),
        [VMEM] * 4,
        [*inner_shapes, in_vmem(WORDS, *TILE)],
        inner_shapes[:1],
        name="early",
    )
    forward = [(i, (i + 1) % blocks) for i in range(blocks)]
    backward = [(i, (i - 1) % blocks) for i in range(blocks)]
    below = lax.ppermute(high, "blk", forward)
    above = lax.ppermute(low, "blk", backward)
    inner, packed_inner, chosen = call(
        inner_kernel,
        (fine_v, solid_v, held(moved), held(early_inner), held(early_packed), held(slot)),
        [VMEM] * 6,
        [*inner_shapes, in_vmem(2, groups, *TILE)],
        inner_shapes[:1],
        name="inner",
    )

    across = [exchange(packed_inner, s) for s in range(2, groups, 2)]
    beside = exchange(packed_inner, 1)
    edges, packed_edges = call(
        edge_kernel,
        (held(moved), held(second), held(below), held(above), coarse_v, coarse_solid_v),
        [VMEM] * 6,
        [in_vmem(NPOP, 2, *TILE), in_vmem((NPOP + 1) // 4 + 1, *TILE)],
        name="edge",
    )
    edge_parts = [packed_edges] + [exchange(packed_edges, s) for s in others(groups)]
    fine_out = call(
        write_kernel,
        (held(inner), held(edges)),
        [VMEM] * 2,
        jax.ShapeDtypeStruct(fine_pops.shape, jnp.float32),
        name="write",
    )
    inner_parts = [beside, packed_inner, *across]
    base = call(
        paste_kernel,
        (held(edges), coarse_v, held(chosen), *map(held, inner_parts)),
        [VMEM] * (3 + len(inner_parts)),
        in_vmem(NPOP, 2, *TILE),
        name="paste",
    )
    relayed = []
    for part in across:
        halves = call(
            split_kernel,
            (held(base), held(part)),
            [VMEM] * 2,
            [in_vmem(part.shape[0] // 2, *TILE)] * 2,
            name="split",
        )
        relayed += [exchange(half, 1) for half in halves]
    coarse_out = call(
        last_kernel,
        (
            coarse_v,
            coarse_solid_v,
            held(chosen),
            held(below),
            held(above),
            held(base),
            *map(held, edge_parts),
            *map(held, relayed),
        ),
        [VMEM] * (6 + len(edge_parts) + len(relayed)),
        jax.ShapeDtypeStruct(coarse_pops.shape, jnp.float32),
        name="last",
    )
    return fine_out, coarse_out


def solution(mesh):
    placed = (
        P("grp", None, "blk", None),
        P("grp", "blk", None),
        P("grp", None, "blk", None),
        P("grp", "blk", None),
        P(),
    )
    return jax.shard_map(
        per_device,
        mesh=mesh,
        in_specs=placed,
        out_specs=(P("grp", None, "blk", None), P("grp", None, "blk", None)),
        check_vma=False,
    )
```

```python
import jax
import jax.numpy as jnp
import numpy as np
from jax import lax
from jax.experimental import pallas as pl
from jax.experimental.pallas import tpu as pltpu
from jax.sharding import PartitionSpec as P

VEL = np.array(
    [
        [0, 0, 0],
        [1, 0, 0],
        [-1, 0, 0],
        [0, 1, 0],
        [0, -1, 0],
        [0, 0, 1],
        [0, 0, -1],
        [1, 1, 0],
        [-1, -1, 0],
        [1, -1, 0],
        [-1, 1, 0],
        [1, 0, 1],
        [-1, 0, -1],
        [1, 0, -1],
        [-1, 0, 1],
        [0, 1, 1],
        [0, -1, -1],
        [0, 1, -1],
        [0, -1, 1],
    ]
)
NPOP = 19
BX = 16
TAU_FINE = 0.6
TAU_COARSE = 0.55
RESCALE = 2.0 * TAU_COARSE / TAU_FINE

ROWS, LANES = 8, 128
TILE = (ROWS, LANES)
VMEM = pltpu.VMEM


def row_ids():
    return lax.broadcasted_iota(jnp.int32, TILE, 0)


def lane_ids():
    return lax.broadcasted_iota(jnp.int32, TILE, 1)


def roll_rows(tile, shift):
    return pltpu.roll(tile, shift % ROWS, 0)


def roll_lanes(tile, shift):
    return pltpu.roll(tile, shift % LANES, 1)


def moments(f, scale):
    minus = [f[i] - f[i + 1] for i in range(1, NPOP, 2)]
    plus = [f[i] + f[i + 1] for i in range(1, NPOP, 2)]
    rho = ((f[0] + plus[0]) + (plus[1] + plus[2])) + (
        (plus[3] + plus[4]) + (plus[5] + plus[6])
    ) + (plus[7] + plus[8])
    jx = (minus[0] + minus[3]) + (minus[4] + minus[5]) + minus[6]
    jy = (minus[1] + minus[3]) - (minus[4] - minus[7]) + minus[8]
    jz = (minus[2] + minus[5]) - (minus[6] - minus[7]) - minus[8]
    inverse = 1.5 / rho
    ux, uy, uz = jx * inverse, jy * inverse, jz * inverse
    amount = scale(rho)
    base = amount * (1.0 - (2.0 / 3.0) * (ux * ux + uy * uy + uz * uz))
    directions = [ux, uy, uz, ux + uy, ux - uy, ux + uz, ux - uz, uy + uz, uy - uz]
    base_axis, base_diag = base * (1.0 / 18.0), base * (1.0 / 36.0)
    amount_axis, amount_diag = amount * (1.0 / 9.0), amount * (1.0 / 18.0)
    pairs = []
    for k, along in enumerate(directions):
        odd = (amount_axis if k < 3 else amount_diag) * along
        pairs.append(((base_axis if k < 3 else base_diag) + odd * along, odd))
    return base * (1.0 / 3.0), pairs, plus, minus


def collide(f, solid, tau):
    rate = (1.0 - solid) * (1.0 / tau)
    rest, pairs, plus, minus = moments(f, lambda rho: rate * rho)
    keep = 1.0 - rate
    half = 0.5 * keep
    half_odd = half - solid
    out = [keep * f[0] + rest]
    for (even, odd), p, m in zip(pairs, plus, minus):
        symmetric = half * p + even
        antisymmetric = half_odd * m + odd
        out += [symmetric + antisymmetric, symmetric - antisymmetric]
    return out


def restrict(f):
    rest, pairs, _, _ = moments(f, lambda rho: (1.0 - RESCALE) * rho)
    out = [RESCALE * f[0] + rest]
    for k, (even, odd) in enumerate(pairs):
        out += [RESCALE * f[2 * k + 1] + (even + odd), RESCALE * f[2 * k + 2] + (even - odd)]
    return out


def shift_plane(halves, cy, cz):
    lane = lane_ids()
    if cz:
        edge = lane % BX == (0 if cz > 0 else BX - 1)
        halves = [
            jnp.where(
                edge,
                roll_lanes(v, BX * cy + cz - BX * cz),
                roll_lanes(v, BX * cy + cz),
            )
            for v in halves
        ]
    elif cy:
        halves = [roll_lanes(v, BX * cy) for v in halves]
    if cy:
        carried = lane < BX if cy > 0 else lane >= LANES - BX
        halves = [
            jnp.where(carried, halves[1], halves[0]),
            jnp.where(carried, halves[0], halves[1]),
        ]
    return halves


def shift_ring(tiles, cx):
    if not cx:
        return tiles
    row = row_ids()
    turned = [roll_rows(t, cx) for t in tiles]
    if len(tiles) == 1:
        return turned
    edge = row == (0 if cx > 0 else ROWS - 1)
    n = len(tiles)
    return [jnp.where(edge, turned[(i - cx) % n], turned[i]) for i in range(n)]


def move_in_planes(halves):
    moved = [
        shift_plane([halves[0][i], halves[1][i]], int(VEL[i, 1]), int(VEL[i, 2]))
        for i in range(NPOP)
    ]
    return [[moved[i][h] for i in range(NPOP)] for h in range(2)]


def move_along(ring):
    out = [[[], []] for _ in ring]
    for h in range(2):
        for i in range(NPOP):
            for t, v in enumerate(shift_ring([tile[h][i] for tile in ring], int(VEL[i, 0]))):
                out[t][h].append(v)
    return out


def merge(mask, first, second):
    return [
        [jnp.where(mask, v, w) for v, w in zip(a, b)] for a, b in zip(first, second)
    ]


def means():
    shape = (2 * LANES, LANES)
    fine = lax.broadcasted_iota(jnp.int32, shape, 0)
    place = lax.broadcasted_iota(jnp.int32, shape, 1)
    same = (fine // (2 * BX) == place // BX) & (fine % BX // 2 == place % 8)
    return jnp.where(same, 0.125, 0.0).astype(jnp.bfloat16)


def squeeze(planes, matrix):
    cells = jnp.concatenate([jnp.concatenate(halves, axis=1) for halves in planes], axis=0)
    found = None
    for _ in range(3):
        part = cells.astype(jnp.bfloat16)
        product = jnp.dot(part, matrix, preferred_element_type=jnp.float32)
        found = product if found is None else found + product
        cells = cells - part.astype(jnp.float32)
    return [found[ROWS * k : ROWS * (k + 1)] for k in range(len(planes))]


def lower():
    return lane_ids() % BX < 8


def pair_up(first, second):
    return first if second is None else jnp.where(lower(), first, second)


def spread(first, second, which):
    if which:
        return jnp.where(lower(), roll_lanes(first, -8), second)
    return jnp.where(lower(), first, roll_lanes(second, 8))


def filled(chosen, h, sources):
    low, high = (sum(chosen[2 * h + z, s] for s in sources) for z in range(2))
    return jnp.where(lower(), low, high) > 0.5


def choose(chosen, quadrant, tiles):
    (_, out), *rest = tiles
    for s, tile in rest:
        out = jnp.where(chosen[quadrant, s] > 0.5, tile, out)
    return out


def half_lanes(h):
    return pl.ds(h * LANES, LANES)


FORWARD = [i for i in range(NPOP) if VEL[i, 0] > 0]
LEVEL = [i for i in range(NPOP) if VEL[i, 0] == 0]
BACKWARD = [i for i in range(NPOP) if VEL[i, 0] < 0]
MOVING = len(FORWARD)

PAIRS = (len(LEVEL) + 1) // 2
FIRST_RIM = MOVING + PAIRS
WORDS = FIRST_RIM + (MOVING + 1 + 3) // 4


def pick(*choices):
    row = row_ids()
    out = choices[-1][-1]
    for rows, tile in choices[-2::-1]:
        mask = row == rows[0]
        for r in rows[1:]:
            mask = mask | (row == r)
        out = jnp.where(mask, tile, out)
    return out


def pack_message(message, first, second, rim, up):
    for k, i in enumerate(FORWARD if up else BACKWARD):
        f, s = [first(i, h) for h in range(2)], [second(i, h) for h in range(2)]
        if up:
            message[k] = pick(
                ((7, 0), roll_rows(f[0], 1)),
                ((1, 2), roll_rows(f[1], 3)),
                ((3, 4), roll_rows(s[0], -2)),
                (s[1],),
            )
        else:
            message[k] = pick(
                ((3, 4), roll_rows(f[0], 3)),
                ((5, 6), roll_rows(f[1], 5)),
                ((7, 0), roll_rows(s[0], -2)),
                (s[1],),
            )
    for k in range(PAIRS):
        shared = []
        for i in (LEVEL + [NPOP])[2 * k : 2 * k + 2]:
            f = [first(i, h) for h in range(2)]
            s = [second(i, h) for h in range(2)] if i < NPOP else f
            if up:
                shared.append(
                    pick(
                        ((7,), f[0]),
                        ((1,), roll_rows(f[1], 2)),
                        ((3,), roll_rows(s[0], -3)),
                        (roll_rows(s[1], -1),),
                    )
                )
            else:
                shared.append(
                    pick(
                        ((4,), roll_rows(f[0], 4)),
                        ((6,), roll_rows(f[1], -2)),
                        ((0,), roll_rows(s[0], -1)),
                        (roll_rows(s[1], 1),),
                    )
                )
        own_rows = (1, 3, 5, 7) if up else (0, 2, 4, 6)
        message[MOVING + k] = pick((own_rows, shared[0]), (roll_rows(shared[1], 1),))
    for j in range(WORDS - FIRST_RIM):
        tile = None
        for k, v in enumerate(rim[4 * j : 4 * j + 4]):
            v = roll_rows(v, k if up else -k)
            at = k if up else 3 - k
            tile = v if tile is None else jnp.where(row_ids() % 4 == at, v, tile)
        message[FIRST_RIM + j] = tile


def shared_tile(message, i):
    k = (LEVEL + [NPOP]).index(i)
    return roll_rows(message[MOVING + k // 2], -(k % 2))


def rim_row(message, k, h, up):
    row = 4 * (1 - h) + k % 4 if up else 4 * h + 3 - k % 4
    return jnp.broadcast_to(message[FIRST_RIM + k // 4, pl.ds(row, 1), :], TILE)


def pack_kernel(fine, solid, coarse, coarse_solid, slot, moved, second, high, low, slot_out, strip, rim, sem):
    planes = fine.shape[2]
    last = coarse.shape[2] - 1

    def bring(source, target, which):
        pltpu.make_async_copy(source, target, sem.at[which]).start()

    def arrive(target, which):
        pltpu.make_async_copy(target, target, sem.at[which]).wait()

    ends = ((0, 0), (planes - 4, 4))
    for half in (pl.ds(0, 10), pl.ds(10, 9)):
        for first, row in ends:
            bring(fine.at[0, half, pl.ds(first, 4), :], strip.at[half, pl.ds(row, 4), :], 0)
    for first, row in ends:
        bring(solid.at[0, pl.ds(first, 4), :], strip.at[NPOP, pl.ds(row, 4), :], 0)
    for plane, row in ((last, 0), (0, 3)):
        bring(coarse.at[0, :, pl.ds(plane, 1), :], rim.at[pl.ds(0, NPOP), pl.ds(row, 1), :], 1)
        bring(coarse_solid.at[0, pl.ds(plane, 1), :], rim.at[NPOP, pl.ds(row, 1), :], 1)
    bring(slot, slot_out, 2)
    arrive(strip, 0)
    solids = [strip[NPOP, :, half_lanes(h)] for h in range(2)]
    once = move_in_planes(
        [collide([strip[i, :, half_lanes(h)] for i in range(NPOP)], solids[h], TAU_FINE) for h in range(2)]
    )
    arrive(slot_out, 2)
    arrive(rim.at[:, pl.ds(0, 2), :], 1)

    def rim_tile(i):
        v = [rim[i, :, half_lanes(h)] for h in range(2)]
        return pick(((0,), v[1]), ((3,), v[0]), ((4,), roll_rows(v[0], 4)), (roll_rows(v[1], 4),))

    s = rim_tile(NPOP)
    outer = collide([rim_tile(i) for i in range(NPOP)], s, TAU_COARSE) + [s]
    ring = move_along([once])[0]
    twice = [collide(ring[h], solids[h], TAU_FINE) for h in range(2)]
    for h in range(2):
        for i in range(NPOP):
            moved[i, h] = once[h][i]
            second[i, h] = twice[h][i]
        moved[NPOP, h] = solids[h]

    def first_of(i, h):
        return moved[i, h]

    def second_of(i, h):
        return second[i, h]

    pack_message(high, first_of, second_of, [outer[i] for i in FORWARD + [NPOP]], True)
    high[WORDS] = jnp.zeros(TILE, jnp.float32)
    pack_message(low, first_of, second_of, [outer[i] for i in BACKWARD + [NPOP]], False)


def inner_steps(fine, solid, moved, inner, packed, work):
    upper = row_ids() < 4

    def middle(ref, h, *i):
        at = half_lanes(h)
        return jnp.where(upper, ref[(0, *i, pl.ds(ROWS, ROWS), at)], ref[(0, *i, pl.ds(0, ROWS), at)])

    outer = [[moved[i, h] for i in range(NPOP)] for h in range(2)]
    center = move_in_planes(
        [
            collide([middle(fine, h, i) for i in range(NPOP)], middle(solid, h), TAU_FINE)
            for h in range(2)
        ]
    )
    ring = move_along([merge(upper, outer, center), merge(upper, center, outer)])
    for t in range(2):
        for h in range(2):
            s = solid[0, pl.ds(ROWS * t, ROWS), half_lanes(h)]
            ring[t][h] = collide(ring[t][h], s, TAU_FINE)
        ring[t] = move_in_planes(ring[t])
    ring = move_along(ring)
    for i in range(NPOP):
        for h in range(2):
            for t in range(2):
                inner[i, h, pl.ds(ROWS * t, ROWS), :] = ring[t][h][i]
                work[i, h, pl.ds(ROWS * t, ROWS), :] = ring[t][h][i]
    sums = [
        [
            work[i, h, pl.ds(0, ROWS, stride=2), :] + work[i, h, pl.ds(1, ROWS, stride=2), :]
            for h in range(2)
        ]
        for i in range(NPOP)
    ]
    out = restrict(squeeze(sums, means())) + [None]
    for j in range((NPOP + 1) // 2):
        packed[j] = pair_up(out[2 * j], out[2 * j + 1])


def starts_early():
    return lax.axis_index("blk") == 0


def early_kernel(fine, solid, moved, low, inner, packed, low_out, work):
    low_out[...] = low[...]

    @pl.when(starts_early())
    def _():
        inner_steps(fine, solid, moved, inner, packed, work)


def inner_kernel(fine, solid, moved, early_inner, early_packed, slot, inner, packed, padded, chosen, matrix, work):
    groups = chosen.shape[1]
    matrix[...] = means()
    me = lax.axis_index("grp")
    codes = slot[...].reshape(1, groups)
    group_ids = lax.broadcasted_iota(jnp.int32, codes.shape, 1)
    for s in range(groups):
        code = jnp.sum(jnp.where(group_ids == me ^ s, codes, 0), axis=1, keepdims=True)
        for q in range(4):
            chosen[q, s] = jnp.where(lane_ids() * 0 + (4 * me + q) == code, 1.0, 0.0)

    @pl.when(starts_early())
    def _():
        inner[...] = early_inner[...]
        packed[...] = early_packed[...]

    @pl.when(jnp.logical_not(starts_early()))
    def _():
        inner_steps(fine, solid, moved, inner, packed, work)

    size = packed.shape[0]
    padded[pl.ds(0, size)] = packed[...]
    padded[size] = jnp.zeros(TILE, jnp.float32)


def edge_kernel(moved, second, below, above, matrix, coarse, coarse_solid, edges, packed):
    row = row_ids()

    def middle(i):
        v = [moved[i, h] for h in range(2)]
        if i in FORWARD:
            return pick(
                ((3, 4), roll_rows(v[0], -3)),
                ((5, 6), roll_rows(v[1], -1)),
                (below[FORWARD.index(i)],),
            )
        if i in BACKWARD:
            return pick(
                ((7, 0), roll_rows(v[0], -1)),
                ((1, 2), roll_rows(v[1], 1)),
                (above[BACKWARD.index(i)],),
            )
        return pick(
            ((0,), v[0]),
            ((2,), roll_rows(v[1], 2)),
            ((3,), roll_rows(v[0], 4)),
            ((5,), roll_rows(v[1], -2)),
            ((1, 7), shared_tile(below, i)),
            (shared_tile(above, i),),
        )

    twice = collide([middle(i) for i in range(NPOP)], middle(NPOP), TAU_FINE)
    both = [[], []]
    for h in range(2):
        for i in range(NPOP):
            cx = int(VEL[i, 0])
            v, mine = roll_rows(twice[i], cx - 2 * h), second[i, h]
            if cx > 0:
                v = pick(
                    ((0, 1, 4, 5), v),
                    ((2, 3), roll_rows(mine, -3)),
                    (roll_rows(below[FORWARD.index(i)], 3 - 2 * h),),
                )
            elif cx < 0:
                v = pick(
                    ((2, 3, 6, 7), v),
                    ((0, 1), roll_rows(mine, -1)),
                    (roll_rows(above[BACKWARD.index(i)], -3 - 2 * h),),
                )
            else:
                v = pick(
                    ((0, 3, 4, 7), v),
                    ((1,), mine),
                    ((2,), roll_rows(mine, 4)),
                    ((6,), roll_rows(shared_tile(below, i), 3 - 2 * h)),
                    (roll_rows(shared_tile(above, i), -3 - 2 * h),),
                )
            both[h].append(v)
    both = move_in_planes(both)
    sums = [[v + roll_rows(v, -1) for v in half] + [None] for half in both]
    odd = row % 2 == 1
    pairs = [
        [half[i] if half[i + 1] is None else jnp.where(odd, roll_rows(half[i + 1], 1), half[i]) for half in sums]
        for i in range(0, NPOP, 2)
    ]
    mean = []
    for pair in squeeze(pairs, matrix[...]):
        mean += [pair, roll_rows(pair, -1)]
    out = restrict(mean[:NPOP]) + [None]
    pairs = [
        out[i] if out[i + 1] is None else jnp.where(odd, roll_rows(out[i + 1], 1), out[i])
        for i in range(0, NPOP, 2)
    ]
    for j in range(len(pairs) // 2):
        packed[j] = pair_up(pairs[2 * j], pairs[2 * j + 1])
    packed[len(pairs) // 2] = jnp.zeros(TILE, jnp.float32)
    for i in range(NPOP):
        for h in range(2):
            edges[i, h] = both[h][i]


def write_kernel(inner, edges, out):
    row = row_ids()
    for i in range(NPOP):
        for h in range(2):
            edge = edges[i, h]
            out[0, i, pl.ds(0, ROWS), half_lanes(h)] = jnp.where(
                row < 2, edge, inner[i, h, pl.ds(0, ROWS), :]
            )
            out[0, i, pl.ds(ROWS, ROWS), half_lanes(h)] = jnp.where(
                row >= 6, roll_rows(edge, 4), inner[i, h, pl.ds(ROWS, ROWS), :]
            )


def split_kernel(after, tiles, first, second):
    half = first.shape[0]
    first[...] = tiles[pl.ds(0, half)]
    second[...] = tiles[pl.ds(half, half)]


def paste_inner(chosen, sources, tile, base, out):
    masks = [filled(chosen, h, sources) for h in range(2)]
    for j in range((NPOP + 1) // 2):
        tiles = [(s, tile(s, j)) for s in sources]
        for h in range(2):
            low, high = (choose(chosen, 2 * h + z, tiles) for z in range(2))
            for i in range(2 * j, min(2 * j + 2, NPOP)):
                out(i, h, jnp.where(masks[h], spread(low, high, i % 2), base(i, h)))


def paste_kernel(after, coarse, solid, chosen, below, above, *refs):
    *packed, out, ends = refs
    sources = [1, *range(0, chosen.shape[1], 2)]
    parts = dict(zip(sources, packed))

    def write(i, h, tile):
        out[i, h] = tile

    paste_inner(
        chosen, sources, lambda s, j: parts[s][j], lambda i, h: coarse[0, i, :, half_lanes(h)], write
    )
    for i in range(NPOP + 1):
        v = [coarse[0, i, :, half_lanes(h)] if i < NPOP else solid[0, :, half_lanes(h)] for h in range(2)]
        tile = pick(((0,), v[0]), ((1,), roll_rows(v[1], 1)), ((2,), roll_rows(v[0], 3)), (roll_rows(v[1], 4),))
        if i == NPOP:
            tile = pick(
                ((4,), rim_row(above, MOVING, 0, False)),
                ((5,), rim_row(above, MOVING, 1, False)),
                ((6,), rim_row(below, MOVING, 0, True)),
                ((7,), rim_row(below, MOVING, 1, True)),
                (tile,),
            )
        ends[i] = tile


def coarse_kernel(after, base, solid, chosen, *refs):
    relayed, out = refs[:-1], refs[-1]
    sources = [2 * k + 3 for k in range(len(relayed) // 2)]
    f = [[None] * NPOP, [None] * NPOP]

    def write(i, h, tile):
        f[h][i] = tile

    def tile(s, j):
        half, at = divmod(j, relayed[0].shape[0])
        return relayed[s - 3 + half][at]

    paste_inner(chosen, sources, tile, lambda i, h: base[i, h], write)
    f = move_in_planes([collide(f[h], solid[0, :, half_lanes(h)], TAU_COARSE) for h in range(2)])
    for h in range(2):
        for i in range(NPOP):
            out[i, h] = f[h][i]


CHUNKS = (0, 3, 6, 9, 12, 15, 17, NPOP)


def last_kernel(chosen, below, above, base, middle, *refs):
    *packed, result, out, sem = refs
    sources = [0, *others(len(packed))]
    row, lane = row_ids(), lane_ids()
    odd = row % 2 == 1
    pasted = [filled(chosen, h, sources) for h in range(2)]
    pasted = (odd & pasted[1]) | (~odd & pasted[0])
    f = []
    for j in range((NPOP + 1) // 4):
        tiles = [(s, part[j]) for s, part in zip(sources, packed)]
        quadrants = [choose(chosen, q, tiles) for q in range(4)]
        for which in range(2):
            v = [spread(quadrants[2 * h], quadrants[2 * h + 1], which) for h in range(2)]
            f.append(jnp.where(odd, roll_rows(v[1], 1), v[0]))
            f.append(jnp.where(odd, v[1], roll_rows(v[0], -1)))
    f = [jnp.where(pasted, f[i], base[i]) for i in range(NPOP)]
    f = collide(f, base[NPOP], TAU_COARSE)
    copied = 0
    for i in range(NPOP):
        cx, cy, cz = (int(c) for c in VEL[i])
        v = f[i]
        if cx:
            k = (FORWARD if cx > 0 else BACKWARD).index(i)
            rim = [rim_row(below if cx > 0 else above, k, h, cx > 0) for h in range(2)]
            at = row >= 6 if cx > 0 else (row == 4) | (row == 5)
            v = jnp.where(at & ~pasted, jnp.where(odd, rim[1], rim[0]), v)
        if cz:
            edge = lane % BX == (0 if cz > 0 else BX - 1)
            v = jnp.where(
                edge, roll_lanes(v, BX * cy + cz - BX * cz), roll_lanes(v, BX * cy + cz)
            )
        elif cy:
            v = roll_lanes(v, BX * cy)
        if cy:
            carried = lane < BX if cy > 0 else lane >= LANES - BX
            v = jnp.where(carried, jnp.where(odd, roll_rows(v, 1), roll_rows(v, -1)), v)
        for h in range(2):
            inside = middle[i, h]
            if cx > 0:
                tile = pick(
                    ((0,), roll_rows(v, 2 - h)), ((1,), roll_rows(v, 1 - h)), (roll_rows(inside, 1),)
                )
            elif cx < 0:
                tile = pick(
                    ((7,), roll_rows(v, 3 - h)), ((6,), roll_rows(v, 4 - h)), (roll_rows(inside, -1),)
                )
            else:
                tile = pick(((0,), roll_rows(v, -h)), ((7,), roll_rows(v, 5 - h)), (inside,))
            out[0, i, :, half_lanes(h)] = tile
        if i + 1 in CHUNKS:
            some = pl.ds(copied, i + 1 - copied)
            pltpu.make_async_copy(out.at[0, some], result.at[0, some], sem).start()
            copied = i + 1
    pltpu.make_async_copy(out, result, sem).wait()


def others(groups):
    return range(1, groups)


def exchange(array, distance):
    groups = lax.axis_size("grp")
    return lax.ppermute(array, "grp", [(i, i ^ distance) for i in range(groups)])


def held(array):
    return pltpu.with_memory_space_constraint(array, VMEM)


def left(array):
    return pltpu.with_memory_space_constraint(array, pltpu.HBM)


def in_vmem(*shape):
    return VMEM(shape, jnp.float32)


def call(kernel, args, specs, outs, scratch=(), flops=0, name=None, out_space=VMEM):
    single = not isinstance(outs, (list, tuple))
    outs = [outs] if single else list(outs)
    result = pl.pallas_call(
        kernel,
        in_specs=[pl.BlockSpec(memory_space=s) for s in specs],
        out_specs=[pl.BlockSpec(memory_space=out_space)] * len(outs),
        out_shape=outs,
        scratch_shapes=list(scratch),
        compiler_params=pltpu.CompilerParams(vmem_limit_bytes=24 << 20),
        cost_estimate=pl.CostEstimate(flops=flops, bytes_accessed=1, transcendentals=0),
        name=name,
    )(*args)
    return result[0] if single else result


def per_device(fine_pops, fine_solid, coarse_pops, coarse_solid, coarse_slot):
    groups = lax.axis_size("grp")
    blocks = lax.axis_size("blk")
    moved, second, high, low, slot = call(
        pack_kernel,
        tuple(map(left, (fine_pops, fine_solid, coarse_pops, coarse_solid, coarse_slot))),
        [pl.ANY] * 5,
        [
            in_vmem(NPOP + 1, 2, *TILE),
            in_vmem(NPOP, 2, *TILE),
            in_vmem(WORDS + 1, *TILE),
            in_vmem(WORDS, *TILE),
            VMEM((groups,), jnp.int32),
        ],
        [
            in_vmem(NPOP + 1, ROWS, 2 * LANES),
            in_vmem(NPOP + 1, ROWS, 2 * LANES),
            pltpu.SemaphoreType.DMA((3,)),
        ],
        name="pack",
    )
    fine_v, solid_v = held(fine_pops), held(fine_solid)
    coarse_v, coarse_solid_v = held(coarse_pops), held(coarse_solid)
    inner_shapes = [in_vmem(NPOP, 2, 2 * ROWS, LANES), in_vmem((NPOP + 1) // 2, *TILE)]
    early_inner, early_packed, low = call(
        early_kernel,
        (fine_v, solid_v, held(moved), held(low)),
        [VMEM] * 4,
        [*inner_shapes, in_vmem(WORDS, *TILE)],
        inner_shapes[:1],
        name="early",
    )
    forward = [(i, (i + 1) % blocks) for i in range(blocks)]
    backward = [(i, (i - 1) % blocks) for i in range(blocks)]
    below = lax.ppermute(high, "blk", forward)
    above = lax.ppermute(low, "blk", backward)
    inner, packed_inner, padded_inner, chosen, matrix = call(
        inner_kernel,
        (fine_v, solid_v, held(moved), held(early_inner), held(early_packed), held(slot)),
        [VMEM] * 6,
        [*inner_shapes, in_vmem((NPOP + 1) // 2 + 1, *TILE), in_vmem(4, groups, *TILE), VMEM((2 * LANES, LANES), jnp.bfloat16)],
        inner_shapes[:1],
        name="inner",
    )

    across = [exchange(packed_inner, s) for s in range(2, groups, 2)]
    beside = exchange(padded_inner, 1)
    edges, packed_edges = call(
        edge_kernel,
        (held(moved), held(second), held(below), held(above), held(matrix), coarse_v, coarse_solid_v),
        [VMEM] * 7,
        [in_vmem(NPOP, 2, *TILE), in_vmem((NPOP + 1) // 4 + 1, *TILE)],
        name="edge",
    )
    edge_parts = [packed_edges] + [exchange(packed_edges, s) for s in others(groups)]
    fine_out = call(
        write_kernel,
        (held(inner), held(edges)),
        [VMEM] * 2,
        jax.ShapeDtypeStruct(fine_pops.shape, jnp.float32),
        name="write",
    )
    inner_parts = [beside, packed_inner, *across]
    base, ends = call(
        paste_kernel,
        (
            held(edges),
            coarse_v,
            coarse_solid_v,
            held(chosen),
            held(below),
            held(above),
            *map(held, inner_parts),
        ),
        [VMEM] * (6 + len(inner_parts)),
        [in_vmem(NPOP, 2, *TILE), in_vmem(NPOP + 1, *TILE)],
        name="paste",
    )
    relayed = []
    for part in across:
        halves = call(
            split_kernel,
            (held(base), held(part)),
            [VMEM] * 2,
            [in_vmem(part.shape[0] // 2, *TILE)] * 2,
            name="split",
        )
        relayed += [exchange(half, 1) for half in halves]
    middle = call(
        coarse_kernel,
        (left(fine_out), held(base), coarse_solid_v, held(chosen), *map(held, relayed)),
        [pl.ANY] + [VMEM] * (3 + len(relayed)),
        in_vmem(NPOP, 2, *TILE),
        name="coarse",
    )
    coarse_out = call(
        last_kernel,
        (held(chosen), held(below), held(above), held(ends), held(middle), *map(held, edge_parts)),
        [VMEM] * (5 + len(edge_parts)),
        jax.ShapeDtypeStruct(coarse_pops.shape, jnp.float32),
        [in_vmem(*coarse_pops.shape), pltpu.SemaphoreType.DMA],
        out_space=pl.ANY,
        name="last",
    )
    return fine_out, coarse_out


def solution(mesh):
    placed = (
        P("grp", None, "blk", None),
        P("grp", "blk", None),
        P("grp", None, "blk", None),
        P("grp", "blk", None),
        P(),
    )
    return jax.shard_map(
        per_device,
        mesh=mesh,
        in_specs=placed,
        out_specs=(P("grp", None, "blk", None), P("grp", None, "blk", None)),
        check_vma=False,
    )
```

```python
import jax
import jax.numpy as jnp
import numpy as np
from jax import lax
from jax.experimental import pallas as pl
from jax.experimental.pallas import tpu as pltpu
from jax.sharding import PartitionSpec as P

VEL = np.array(
    [
        [0, 0, 0],
        [1, 0, 0],
        [-1, 0, 0],
        [0, 1, 0],
        [0, -1, 0],
        [0, 0, 1],
        [0, 0, -1],
        [1, 1, 0],
        [-1, -1, 0],
        [1, -1, 0],
        [-1, 1, 0],
        [1, 0, 1],
        [-1, 0, -1],
        [1, 0, -1],
        [-1, 0, 1],
        [0, 1, 1],
        [0, -1, -1],
        [0, 1, -1],
        [0, -1, 1],
    ]
)
NPOP = 19
BX = 16
TAU_FINE = 0.6
TAU_COARSE = 0.55
RESCALE = 2.0 * TAU_COARSE / TAU_FINE

ROWS, LANES = 8, 128
TILE = (ROWS, LANES)
VMEM = pltpu.VMEM


def row_ids():
    return lax.broadcasted_iota(jnp.int32, TILE, 0)


def lane_ids():
    return lax.broadcasted_iota(jnp.int32, TILE, 1)


def roll_rows(tile, shift):
    return pltpu.roll(tile, shift % ROWS, 0)


def roll_lanes(tile, shift):
    return pltpu.roll(tile, shift % LANES, 1)


def moments(f, scale):
    minus = [f[i] - f[i + 1] for i in range(1, NPOP, 2)]
    plus = [f[i] + f[i + 1] for i in range(1, NPOP, 2)]
    rho = ((f[0] + plus[0]) + (plus[1] + plus[2])) + (
        (plus[3] + plus[4]) + (plus[5] + plus[6])
    ) + (plus[7] + plus[8])
    jx = (minus[0] + minus[3]) + (minus[4] + minus[5]) + minus[6]
    jy = (minus[1] + minus[3]) - (minus[4] - minus[7]) + minus[8]
    jz = (minus[2] + minus[5]) - (minus[6] - minus[7]) - minus[8]
    inverse = 1.5 / rho
    ux, uy, uz = jx * inverse, jy * inverse, jz * inverse
    amount = scale(rho)
    base = amount * (1.0 - (2.0 / 3.0) * (ux * ux + uy * uy + uz * uz))
    directions = [ux, uy, uz, ux + uy, ux - uy, ux + uz, ux - uz, uy + uz, uy - uz]
    base_axis, base_diag = base * (1.0 / 18.0), base * (1.0 / 36.0)
    amount_axis, amount_diag = amount * (1.0 / 9.0), amount * (1.0 / 18.0)
    pairs = []
    for k, along in enumerate(directions):
        odd = (amount_axis if k < 3 else amount_diag) * along
        pairs.append(((base_axis if k < 3 else base_diag) + odd * along, odd))
    return base * (1.0 / 3.0), pairs, plus, minus


def collide(f, solid, tau):
    rate = (1.0 - solid) * (1.0 / tau)
    rest, pairs, plus, minus = moments(f, lambda rho: rate * rho)
    keep = 1.0 - rate
    half = 0.5 * keep
    half_odd = half - solid
    out = [keep * f[0] + rest]
    for (even, odd), p, m in zip(pairs, plus, minus):
        symmetric = half * p + even
        antisymmetric = half_odd * m + odd
        out += [symmetric + antisymmetric, symmetric - antisymmetric]
    return out


def restrict(f):
    rest, pairs, _, _ = moments(f, lambda rho: (1.0 - RESCALE) * rho)
    out = [RESCALE * f[0] + rest]
    for k, (even, odd) in enumerate(pairs):
        out += [RESCALE * f[2 * k + 1] + (even + odd), RESCALE * f[2 * k + 2] + (even - odd)]
    return out


def shift_plane(halves, cy, cz):
    lane = lane_ids()
    if cz:
        edge = lane % BX == (0 if cz > 0 else BX - 1)
        halves = [
            jnp.where(
                edge,
                roll_lanes(v, BX * cy + cz - BX * cz),
                roll_lanes(v, BX * cy + cz),
            )
            for v in halves
        ]
    elif cy:
        halves = [roll_lanes(v, BX * cy) for v in halves]
    if cy:
        carried = lane < BX if cy > 0 else lane >= LANES - BX
        halves = [
            jnp.where(carried, halves[1], halves[0]),
            jnp.where(carried, halves[0], halves[1]),
        ]
    return halves


def shift_ring(tiles, cx):
    if not cx:
        return tiles
    row = row_ids()
    turned = [roll_rows(t, cx) for t in tiles]
    if len(tiles) == 1:
        return turned
    edge = row == (0 if cx > 0 else ROWS - 1)
    n = len(tiles)
    return [jnp.where(edge, turned[(i - cx) % n], turned[i]) for i in range(n)]


def move_in_planes(halves):
    moved = [
        shift_plane([halves[0][i], halves[1][i]], int(VEL[i, 1]), int(VEL[i, 2]))
        for i in range(NPOP)
    ]
    return [[moved[i][h] for i in range(NPOP)] for h in range(2)]


def move_along(ring):
    out = [[[], []] for _ in ring]
    for h in range(2):
        for i in range(NPOP):
            for t, v in enumerate(shift_ring([tile[h][i] for tile in ring], int(VEL[i, 0]))):
                out[t][h].append(v)
    return out


def merge(mask, first, second):
    return [
        [jnp.where(mask, v, w) for v, w in zip(a, b)] for a, b in zip(first, second)
    ]


def means():
    shape = (2 * LANES, LANES)
    fine = lax.broadcasted_iota(jnp.int32, shape, 0)
    place = lax.broadcasted_iota(jnp.int32, shape, 1)
    same = (fine // (2 * BX) == place // BX) & (fine % BX // 2 == place % 8)
    return jnp.where(same, 0.125, 0.0).astype(jnp.bfloat16)


def squeeze(planes, matrix):
    cells = jnp.concatenate([jnp.concatenate(halves, axis=1) for halves in planes], axis=0)
    found = None
    for _ in range(3):
        part = cells.astype(jnp.bfloat16)
        product = jnp.dot(part, matrix, preferred_element_type=jnp.float32)
        found = product if found is None else found + product
        cells = cells - part.astype(jnp.float32)
    return [found[ROWS * k : ROWS * (k + 1)] for k in range(len(planes))]


INNER_TILES = (NPOP + 1) // 2 - 2


def fold(tiles):
    out = list(tiles[:INNER_TILES])
    for m in range(6):
        extra, at = tiles[INNER_TILES + m // 3], 2 * (m % 3)
        out[m] = pick(((0,), roll_rows(extra, -1 - at)), ((7,), roll_rows(extra, 5 - at)), (out[m],))
    return out


def unfold(tile, j):
    if j < INNER_TILES:
        return tile(j)
    rows = []
    for m in range(3):
        v = tile(3 * (j - INNER_TILES) + m)
        rows += [((1 + 2 * m,), roll_rows(v, 1 + 2 * m)), ((2 + 2 * m,), roll_rows(v, 2 * m - 5))]
    return pick(*rows, (rows[-1][1],))


def lower():
    return lane_ids() % BX < 8


def pair_up(first, second):
    return first if second is None else jnp.where(lower(), first, second)


def spread(first, second, which):
    if which:
        return jnp.where(lower(), roll_lanes(first, -8), second)
    return jnp.where(lower(), first, roll_lanes(second, 8))


def filled(chosen, h, sources):
    low, high = (sum(chosen[2 * h + z, s] for s in sources) for z in range(2))
    return jnp.where(lower(), low, high) > 0.5


def choose(chosen, quadrant, tiles):
    (_, out), *rest = tiles
    for s, tile in rest:
        out = jnp.where(chosen[quadrant, s] > 0.5, tile, out)
    return out


def half_lanes(h):
    return pl.ds(h * LANES, LANES)


FORWARD = [i for i in range(NPOP) if VEL[i, 0] > 0]
LEVEL = [i for i in range(NPOP) if VEL[i, 0] == 0]
BACKWARD = [i for i in range(NPOP) if VEL[i, 0] < 0]
MOVING = len(FORWARD)

PAIRS = (len(LEVEL) + 1) // 2
WORDS = MOVING + PAIRS


def pick(*choices):
    row = row_ids()
    out = choices[-1][-1]
    for rows, tile in choices[-2::-1]:
        mask = row == rows[0]
        for r in rows[1:]:
            mask = mask | (row == r)
        out = jnp.where(mask, tile, out)
    return out


def pack_message(message, first, second, rim, up):
    for k, i in enumerate(FORWARD if up else BACKWARD):
        f, s = [first(i, h) for h in range(2)], [second(i, h) for h in range(2)]
        s = [v + roll_rows(v, -1) for v in s]
        if up:
            message[k] = pick(
                ((7, 0), roll_rows(f[0], 1)),
                ((1, 2), roll_rows(f[1], 3)),
                ((3,), roll_rows(s[0], -2)),
                ((5,), s[1]),
                ((4,), rim[k]),
                (roll_rows(rim[k], -2),),
            )
        else:
            message[k] = pick(
                ((3, 4), roll_rows(f[0], 3)),
                ((5, 6), roll_rows(f[1], 5)),
                ((7,), roll_rows(s[0], -2)),
                ((1,), s[1]),
                ((0,), roll_rows(rim[k], -3)),
                (roll_rows(rim[k], 3),),
            )
    for k in range(PAIRS):
        shared = []
        for i in (LEVEL + [NPOP])[2 * k : 2 * k + 2]:
            f = [first(i, h) for h in range(2)]
            if up:
                if i < NPOP:
                    s = [roll_rows(second(i, 0), -3), roll_rows(second(i, 1), -1)]
                else:
                    s = [roll_rows(rim[MOVING], -1), roll_rows(rim[MOVING], 5)]
                shared.append(pick(((7,), f[0]), ((1,), roll_rows(f[1], 2)), ((3,), s[0]), (s[1],)))
            else:
                if i < NPOP:
                    s = [roll_rows(second(i, 0), -1), roll_rows(second(i, 1), 1)]
                else:
                    s = [roll_rows(rim[MOVING], -3), roll_rows(rim[MOVING], 3)]
                shared.append(
                    pick(((4,), roll_rows(f[0], 4)), ((6,), roll_rows(f[1], -2)), ((0,), s[0]), (s[1],))
                )
        own_rows = (1, 3, 5, 7) if up else (0, 2, 4, 6)
        message[MOVING + k] = pick((own_rows, shared[0]), (roll_rows(shared[1], 1),))


def shared_tile(message, i):
    k = (LEVEL + [NPOP]).index(i)
    return roll_rows(message[MOVING + k // 2], -(k % 2))


def rim_row(message, k, h, up):
    index, row = (k, 0) if k < MOVING else (WORDS - 1, 1)
    row = 4 + 2 * h if up else row + 2 * h
    return jnp.broadcast_to(message[index, pl.ds(row, 1), :], TILE)


def pack_kernel(fine, solid, coarse, coarse_solid, slot, moved, second, high, low, slot_out, strip, rim, sem):
    planes = fine.shape[2]
    last = coarse.shape[2] - 1

    def bring(source, target, which):
        pltpu.make_async_copy(source, target, sem.at[which]).start()

    def arrive(target, which):
        pltpu.make_async_copy(target, target, sem.at[which]).wait()

    ends = ((0, 0), (planes - 4, 4))
    for half in (pl.ds(0, 10), pl.ds(10, 9)):
        for first, row in ends:
            bring(fine.at[0, half, pl.ds(first, 4), :], strip.at[half, pl.ds(row, 4), :], 0)
    for first, row in ends:
        bring(solid.at[0, pl.ds(first, 4), :], strip.at[NPOP, pl.ds(row, 4), :], 0)
    for plane, row in ((last, 0), (0, 3)):
        bring(coarse.at[0, :, pl.ds(plane, 1), :], rim.at[pl.ds(0, NPOP), pl.ds(row, 1), :], 1)
        bring(coarse_solid.at[0, pl.ds(plane, 1), :], rim.at[NPOP, pl.ds(row, 1), :], 1)
    bring(slot, slot_out, 2)
    arrive(strip, 0)
    solids = [strip[NPOP, :, half_lanes(h)] for h in range(2)]
    once = move_in_planes(
        [collide([strip[i, :, half_lanes(h)] for i in range(NPOP)], solids[h], TAU_FINE) for h in range(2)]
    )
    arrive(slot_out, 2)
    arrive(rim.at[:, pl.ds(0, 2), :], 1)

    def rim_tile(i):
        v = [rim[i, :, half_lanes(h)] for h in range(2)]
        return pick(((0,), v[1]), ((3,), v[0]), ((4,), roll_rows(v[0], 4)), (roll_rows(v[1], 4),))

    s = rim_tile(NPOP)
    outer = collide([rim_tile(i) for i in range(NPOP)], s, TAU_COARSE) + [s]
    ring = move_along([once])[0]
    twice = [collide(ring[h], solids[h], TAU_FINE) for h in range(2)]
    for h in range(2):
        for i in range(NPOP):
            moved[i, h] = once[h][i]
            second[i, h] = twice[h][i]
        moved[NPOP, h] = solids[h]

    def first_of(i, h):
        return moved[i, h]

    def second_of(i, h):
        return second[i, h]

    pack_message(high, first_of, second_of, [outer[i] for i in FORWARD + [NPOP]], True)
    high[WORDS] = jnp.zeros(TILE, jnp.float32)
    pack_message(low, first_of, second_of, [outer[i] for i in BACKWARD + [NPOP]], False)


def inner_steps(fine, solid, moved, inner, packed, work):
    upper = row_ids() < 4

    def middle(ref, h, *i):
        at = half_lanes(h)
        return jnp.where(upper, ref[(0, *i, pl.ds(ROWS, ROWS), at)], ref[(0, *i, pl.ds(0, ROWS), at)])

    outer = [[moved[i, h] for i in range(NPOP)] for h in range(2)]
    center = move_in_planes(
        [
            collide([middle(fine, h, i) for i in range(NPOP)], middle(solid, h), TAU_FINE)
            for h in range(2)
        ]
    )
    ring = move_along([merge(upper, outer, center), merge(upper, center, outer)])
    for t in range(2):
        for h in range(2):
            s = solid[0, pl.ds(ROWS * t, ROWS), half_lanes(h)]
            ring[t][h] = collide(ring[t][h], s, TAU_FINE)
        ring[t] = move_in_planes(ring[t])
    ring = move_along(ring)
    for i in range(NPOP):
        for h in range(2):
            for t in range(2):
                inner[i, h, pl.ds(ROWS * t, ROWS), :] = ring[t][h][i]
                work[i, h, pl.ds(ROWS * t, ROWS), :] = ring[t][h][i]
    sums = [
        [
            work[i, h, pl.ds(0, ROWS, stride=2), :] + work[i, h, pl.ds(1, ROWS, stride=2), :]
            for h in range(2)
        ]
        for i in range(NPOP)
    ]
    out = restrict(squeeze(sums, means())) + [None]
    pairs = [pair_up(out[2 * j], out[2 * j + 1]) for j in range((NPOP + 1) // 2)]
    for j, tile in enumerate(fold(pairs)):
        packed[j] = tile


def starts_early():
    return lax.axis_index("blk") == 0


def early_kernel(fine, solid, moved, low, inner, packed, low_out, work):
    low_out[...] = low[...]

    @pl.when(starts_early())
    def _():
        inner_steps(fine, solid, moved, inner, packed, work)


def inner_kernel(fine, solid, moved, early_inner, early_packed, slot, inner, packed, padded, chosen, matrix, work):
    groups = chosen.shape[1]
    matrix[...] = means()
    me = lax.axis_index("grp")
    codes = slot[...].reshape(1, groups)
    group_ids = lax.broadcasted_iota(jnp.int32, codes.shape, 1)
    for s in range(groups):
        code = jnp.sum(jnp.where(group_ids == me ^ s, codes, 0), axis=1, keepdims=True)
        for q in range(4):
            chosen[q, s] = jnp.where(lane_ids() * 0 + (4 * me + q) == code, 1.0, 0.0)

    @pl.when(starts_early())
    def _():
        inner[...] = early_inner[...]
        packed[...] = early_packed[...]

    @pl.when(jnp.logical_not(starts_early()))
    def _():
        inner_steps(fine, solid, moved, inner, packed, work)

    size = packed.shape[0]
    padded[pl.ds(0, size)] = packed[...]
    padded[size] = jnp.zeros(TILE, jnp.float32)


def edge_kernel(moved, second, below, above, matrix, coarse, coarse_solid, edges, packed):
    row = row_ids()

    def middle(i):
        v = [moved[i, h] for h in range(2)]
        if i in FORWARD:
            return pick(
                ((3, 4), roll_rows(v[0], -3)),
                ((5, 6), roll_rows(v[1], -1)),
                (below[FORWARD.index(i)],),
            )
        if i in BACKWARD:
            return pick(
                ((7, 0), roll_rows(v[0], -1)),
                ((1, 2), roll_rows(v[1], 1)),
                (above[BACKWARD.index(i)],),
            )
        return pick(
            ((0,), v[0]),
            ((2,), roll_rows(v[1], 2)),
            ((3,), roll_rows(v[0], 4)),
            ((5,), roll_rows(v[1], -2)),
            ((1, 7), shared_tile(below, i)),
            (shared_tile(above, i),),
        )

    twice = collide([middle(i) for i in range(NPOP)], middle(NPOP), TAU_FINE)
    nothing = jnp.zeros(TILE, jnp.float32)
    both = [[], []]
    for h in range(2):
        for i in range(NPOP):
            cx = int(VEL[i, 0])
            v, mine = roll_rows(twice[i], cx - 2 * h), second[i, h]
            if cx > 0:
                v = pick(
                    ((0, 1, 4, 5), v),
                    ((2, 3), roll_rows(mine, -3)),
                    ((7,), nothing),
                    (roll_rows(below[FORWARD.index(i)], 3 - 2 * h),),
                )
            elif cx < 0:
                v = pick(
                    ((2, 3, 6, 7), v),
                    ((0, 1), roll_rows(mine, -1)),
                    ((5,), nothing),
                    (roll_rows(above[BACKWARD.index(i)], -3 - 2 * h),),
                )
            else:
                v = pick(
                    ((0, 3, 4, 7), v),
                    ((1,), mine),
                    ((2,), roll_rows(mine, 4)),
                    ((6,), roll_rows(shared_tile(below, i), 3 - 2 * h)),
                    (roll_rows(shared_tile(above, i), -3 - 2 * h),),
                )
            both[h].append(v)
    both = move_in_planes(both)
    sums = [[v + roll_rows(v, -1) for v in half] + [None] for half in both]
    odd = row % 2 == 1
    pairs = [
        [half[i] if half[i + 1] is None else jnp.where(odd, roll_rows(half[i + 1], 1), half[i]) for half in sums]
        for i in range(0, NPOP, 2)
    ]
    mean = []
    for pair in squeeze(pairs, matrix[...]):
        mean += [pair, roll_rows(pair, -1)]
    out = restrict(mean[:NPOP]) + [None]
    pairs = [
        out[i] if out[i + 1] is None else jnp.where(odd, roll_rows(out[i + 1], 1), out[i])
        for i in range(0, NPOP, 2)
    ]
    for j in range(len(pairs) // 2):
        packed[j] = pair_up(pairs[2 * j], pairs[2 * j + 1])
    for i in range(NPOP):
        for h in range(2):
            edges[i, h] = both[h][i]


def write_kernel(inner, edges, out):
    row = row_ids()
    for i in range(NPOP):
        for h in range(2):
            edge = edges[i, h]
            out[0, i, pl.ds(0, ROWS), half_lanes(h)] = jnp.where(
                row < 2, edge, inner[i, h, pl.ds(0, ROWS), :]
            )
            out[0, i, pl.ds(ROWS, ROWS), half_lanes(h)] = jnp.where(
                row >= 6, roll_rows(edge, 4), inner[i, h, pl.ds(ROWS, ROWS), :]
            )


def split_kernel(after, tiles, first, second):
    half = first.shape[0]
    first[...] = tiles[pl.ds(0, half)]
    second[...] = tiles[pl.ds(half, half)]


def paste_inner(chosen, sources, tile, base, out):
    masks = [filled(chosen, h, sources) for h in range(2)]
    for j in range((NPOP + 1) // 2):
        tiles = [(s, tile(s, j)) for s in sources]
        for h in range(2):
            low, high = (choose(chosen, 2 * h + z, tiles) for z in range(2))
            for i in range(2 * j, min(2 * j + 2, NPOP)):
                out(i, h, jnp.where(masks[h], spread(low, high, i % 2), base(i, h)))


def paste_kernel(after, coarse, solid, chosen, below, above, *refs):
    *packed, out, ends = refs
    sources = [1, *range(0, chosen.shape[1], 2)]
    parts = dict(zip(sources, packed))

    def write(i, h, tile):
        out[i, h] = tile

    paste_inner(
        chosen, sources, lambda s, j: unfold(lambda k: parts[s][k], j), lambda i, h: coarse[0, i, :, half_lanes(h)], write
    )
    for i in range(NPOP + 1):
        v = [coarse[0, i, :, half_lanes(h)] if i < NPOP else solid[0, :, half_lanes(h)] for h in range(2)]
        tile = pick(((0,), v[0]), ((1,), roll_rows(v[1], 1)), ((2,), roll_rows(v[0], 3)), (roll_rows(v[1], 4),))
        if i == NPOP:
            tile = pick(
                ((4,), rim_row(above, MOVING, 0, False)),
                ((5,), rim_row(above, MOVING, 1, False)),
                ((6,), rim_row(below, MOVING, 0, True)),
                ((7,), rim_row(below, MOVING, 1, True)),
                (tile,),
            )
        ends[i] = tile


def coarse_kernel(after, base, solid, chosen, *refs):
    relayed, out = refs[:-1], refs[-1]
    sources = [2 * k + 3 for k in range(len(relayed) // 2)]
    f = [[None] * NPOP, [None] * NPOP]

    def write(i, h, tile):
        f[h][i] = tile

    half = relayed[0].shape[0]

    def tile(s, j):
        return unfold(lambda k: relayed[s - 3 + k // half][k % half], j)

    paste_inner(chosen, sources, tile, lambda i, h: base[i, h], write)
    f = move_in_planes([collide(f[h], solid[0, :, half_lanes(h)], TAU_COARSE) for h in range(2)])
    for h in range(2):
        for i in range(NPOP):
            out[i, h] = f[h][i]


CHUNKS = (0, 3, 6, 9, 12, 15, 17, NPOP)


def last_kernel(chosen, below, above, base, middle, *refs):
    *packed, result, out, sem = refs
    sources = [0, *others(len(packed))]
    row, lane = row_ids(), lane_ids()
    odd = row % 2 == 1
    pasted = [filled(chosen, h, sources) for h in range(2)]
    pasted = (odd & pasted[1]) | (~odd & pasted[0])
    f = []
    for j in range((NPOP + 1) // 4):
        tiles = [(s, part[j]) for s, part in zip(sources, packed)]
        quadrants = [choose(chosen, q, tiles) for q in range(4)]
        for which in range(2):
            v = [spread(quadrants[2 * h], quadrants[2 * h + 1], which) for h in range(2)]
            f.append(jnp.where(odd, roll_rows(v[1], 1), v[0]))
            f.append(jnp.where(odd, v[1], roll_rows(v[0], -1)))
    f = [jnp.where(pasted, f[i], base[i]) for i in range(NPOP)]
    f = collide(f, base[NPOP], TAU_COARSE)
    copied = 0
    for i in range(NPOP):
        cx, cy, cz = (int(c) for c in VEL[i])
        v = f[i]
        if cx:
            k = (FORWARD if cx > 0 else BACKWARD).index(i)
            rim = [rim_row(below if cx > 0 else above, k, h, cx > 0) for h in range(2)]
            at = row >= 6 if cx > 0 else (row == 4) | (row == 5)
            v = jnp.where(at & ~pasted, jnp.where(odd, rim[1], rim[0]), v)
        if cz:
            edge = lane % BX == (0 if cz > 0 else BX - 1)
            v = jnp.where(
                edge, roll_lanes(v, BX * cy + cz - BX * cz), roll_lanes(v, BX * cy + cz)
            )
        elif cy:
            v = roll_lanes(v, BX * cy)
        if cy:
            carried = lane < BX if cy > 0 else lane >= LANES - BX
            v = jnp.where(carried, jnp.where(odd, roll_rows(v, 1), roll_rows(v, -1)), v)
        for h in range(2):
            inside = middle[i, h]
            if cx > 0:
                tile = pick(
                    ((0,), roll_rows(v, 2 - h)), ((1,), roll_rows(v, 1 - h)), (roll_rows(inside, 1),)
                )
            elif cx < 0:
                tile = pick(
                    ((7,), roll_rows(v, 3 - h)), ((6,), roll_rows(v, 4 - h)), (roll_rows(inside, -1),)
                )
            else:
                tile = pick(((0,), roll_rows(v, -h)), ((7,), roll_rows(v, 5 - h)), (inside,))
            out[0, i, :, half_lanes(h)] = tile
        if i + 1 in CHUNKS:
            some = pl.ds(copied, i + 1 - copied)
            pltpu.make_async_copy(out.at[0, some], result.at[0, some], sem).start()
            copied = i + 1
    pltpu.make_async_copy(out, result, sem).wait()


def others(groups):
    return range(1, groups)


def exchange(array, distance):
    groups = lax.axis_size("grp")
    return lax.ppermute(array, "grp", [(i, i ^ distance) for i in range(groups)])


def held(array):
    return pltpu.with_memory_space_constraint(array, VMEM)


def left(array):
    return pltpu.with_memory_space_constraint(array, pltpu.HBM)


def in_vmem(*shape):
    return VMEM(shape, jnp.float32)


def call(kernel, args, specs, outs, scratch=(), flops=0, name=None, out_space=VMEM):
    single = not isinstance(outs, (list, tuple))
    outs = [outs] if single else list(outs)
    result = pl.pallas_call(
        kernel,
        in_specs=[pl.BlockSpec(memory_space=s) for s in specs],
        out_specs=[pl.BlockSpec(memory_space=out_space)] * len(outs),
        out_shape=outs,
        scratch_shapes=list(scratch),
        compiler_params=pltpu.CompilerParams(vmem_limit_bytes=24 << 20),
        cost_estimate=pl.CostEstimate(flops=flops, bytes_accessed=1, transcendentals=0),
        name=name,
    )(*args)
    return result[0] if single else result


def per_device(fine_pops, fine_solid, coarse_pops, coarse_solid, coarse_slot):
    groups = lax.axis_size("grp")
    blocks = lax.axis_size("blk")
    moved, second, high, low, slot = call(
        pack_kernel,
        tuple(map(left, (fine_pops, fine_solid, coarse_pops, coarse_solid, coarse_slot))),
        [pl.ANY] * 5,
        [
            in_vmem(NPOP + 1, 2, *TILE),
            in_vmem(NPOP, 2, *TILE),
            in_vmem(WORDS + 1, *TILE),
            in_vmem(WORDS, *TILE),
            VMEM((groups,), jnp.int32),
        ],
        [
            in_vmem(NPOP + 1, ROWS, 2 * LANES),
            in_vmem(NPOP + 1, ROWS, 2 * LANES),
            pltpu.SemaphoreType.DMA((3,)),
        ],
        name="pack",
    )
    fine_v, solid_v = held(fine_pops), held(fine_solid)
    coarse_v, coarse_solid_v = held(coarse_pops), held(coarse_solid)
    inner_shapes = [in_vmem(NPOP, 2, 2 * ROWS, LANES), in_vmem(INNER_TILES, *TILE)]
    early_inner, early_packed, low = call(
        early_kernel,
        (fine_v, solid_v, held(moved), held(low)),
        [VMEM] * 4,
        [*inner_shapes, in_vmem(WORDS, *TILE)],
        inner_shapes[:1],
        name="early",
    )
    forward = [(i, (i + 1) % blocks) for i in range(blocks)]
    backward = [(i, (i - 1) % blocks) for i in range(blocks)]
    below = lax.ppermute(high, "blk", forward)
    above = lax.ppermute(low, "blk", backward)
    inner, packed_inner, padded_inner, chosen, matrix = call(
        inner_kernel,
        (fine_v, solid_v, held(moved), held(early_inner), held(early_packed), held(slot)),
        [VMEM] * 6,
        [*inner_shapes, in_vmem(INNER_TILES + 1, *TILE), in_vmem(4, groups, *TILE), VMEM((2 * LANES, LANES), jnp.bfloat16)],
        inner_shapes[:1],
        name="inner",
    )

    across = [exchange(packed_inner, s) for s in range(2, groups, 2)]
    beside = exchange(padded_inner, 1)
    edges, packed_edges = call(
        edge_kernel,
        (held(moved), held(second), held(below), held(above), held(matrix), coarse_v, coarse_solid_v),
        [VMEM] * 7,
        [in_vmem(NPOP, 2, *TILE), in_vmem((NPOP + 1) // 4, *TILE)],
        name="edge",
    )
    edge_parts = [packed_edges] + [exchange(packed_edges, s) for s in others(groups)]
    fine_out = call(
        write_kernel,
        (held(inner), held(edges)),
        [VMEM] * 2,
        jax.ShapeDtypeStruct(fine_pops.shape, jnp.float32),
        name="write",
    )
    inner_parts = [beside, packed_inner, *across]
    base, ends = call(
        paste_kernel,
        (
            held(edges),
            coarse_v,
            coarse_solid_v,
            held(chosen),
            held(below),
            held(above),
            *map(held, inner_parts),
        ),
        [VMEM] * (6 + len(inner_parts)),
        [in_vmem(NPOP, 2, *TILE), in_vmem(NPOP + 1, *TILE)],
        name="paste",
    )
    relayed = []
    for part in across:
        halves = call(
            split_kernel,
            (held(base), held(part)),
            [VMEM] * 2,
            [in_vmem(part.shape[0] // 2, *TILE)] * 2,
            name="split",
        )
        relayed += [exchange(half, 1) for half in halves]
    middle = call(
        coarse_kernel,
        (left(fine_out), held(base), coarse_solid_v, held(chosen), *map(held, relayed)),
        [pl.ANY] + [VMEM] * (3 + len(relayed)),
        in_vmem(NPOP, 2, *TILE),
        name="coarse",
    )
    coarse_out = call(
        last_kernel,
        (held(chosen), held(below), held(above), held(ends), held(middle), *map(held, edge_parts)),
        [VMEM] * (5 + len(edge_parts)),
        jax.ShapeDtypeStruct(coarse_pops.shape, jnp.float32),
        [in_vmem(*coarse_pops.shape), pltpu.SemaphoreType.DMA],
        out_space=pl.ANY,
        name="last",
    )
    return fine_out, coarse_out


def solution(mesh):
    placed = (
        P("grp", None, "blk", None),
        P("grp", "blk", None),
        P("grp", None, "blk", None),
        P("grp", "blk", None),
        P(),
    )
    return jax.shard_map(
        per_device,
        mesh=mesh,
        in_specs=placed,
        out_specs=(P("grp", None, "blk", None), P("grp", None, "blk", None)),
        check_vma=False,
    )
```

```python
import jax
import jax.numpy as jnp
import numpy as np
from jax import lax
from jax.experimental import pallas as pl
from jax.experimental.pallas import tpu as pltpu
from jax.sharding import PartitionSpec as P

VEL = np.array(
    [
        [0, 0, 0],
        [1, 0, 0],
        [-1, 0, 0],
        [0, 1, 0],
        [0, -1, 0],
        [0, 0, 1],
        [0, 0, -1],
        [1, 1, 0],
        [-1, -1, 0],
        [1, -1, 0],
        [-1, 1, 0],
        [1, 0, 1],
        [-1, 0, -1],
        [1, 0, -1],
        [-1, 0, 1],
        [0, 1, 1],
        [0, -1, -1],
        [0, 1, -1],
        [0, -1, 1],
    ]
)
NPOP = 19
BX = 16
TAU_FINE = 0.6
TAU_COARSE = 0.55
RESCALE = 2.0 * TAU_COARSE / TAU_FINE

ROWS, LANES = 8, 128
TILE = (ROWS, LANES)
VMEM = pltpu.VMEM


def row_ids():
    return lax.broadcasted_iota(jnp.int32, TILE, 0)


def lane_ids():
    return lax.broadcasted_iota(jnp.int32, TILE, 1)


def roll_rows(tile, shift):
    return pltpu.roll(tile, shift % ROWS, 0)


def roll_lanes(tile, shift):
    return pltpu.roll(tile, shift % LANES, 1)


def moments(f, scale):
    minus = [f[i] - f[i + 1] for i in range(1, NPOP, 2)]
    plus = [f[i] + f[i + 1] for i in range(1, NPOP, 2)]
    rho = ((f[0] + plus[0]) + (plus[1] + plus[2])) + (
        (plus[3] + plus[4]) + (plus[5] + plus[6])
    ) + (plus[7] + plus[8])
    jx = (minus[0] + minus[3]) + (minus[4] + minus[5]) + minus[6]
    jy = (minus[1] + minus[3]) - (minus[4] - minus[7]) + minus[8]
    jz = (minus[2] + minus[5]) - (minus[6] - minus[7]) - minus[8]
    inverse = 1.5 / rho
    ux, uy, uz = jx * inverse, jy * inverse, jz * inverse
    amount = scale(rho)
    base = amount * (1.0 - (2.0 / 3.0) * (ux * ux + uy * uy + uz * uz))
    directions = [ux, uy, uz, ux + uy, ux - uy, ux + uz, ux - uz, uy + uz, uy - uz]
    base_axis, base_diag = base * (1.0 / 18.0), base * (1.0 / 36.0)
    amount_axis, amount_diag = amount * (1.0 / 9.0), amount * (1.0 / 18.0)
    pairs = []
    for k, along in enumerate(directions):
        odd = (amount_axis if k < 3 else amount_diag) * along
        pairs.append(((base_axis if k < 3 else base_diag) + odd * along, odd))
    return base * (1.0 / 3.0), pairs, plus, minus


def collide(f, solid, tau):
    rate = (1.0 - solid) * (1.0 / tau)
    rest, pairs, plus, minus = moments(f, lambda rho: rate * rho)
    keep = 1.0 - rate
    half = 0.5 * keep
    half_odd = half - solid
    out = [keep * f[0] + rest]
    for (even, odd), p, m in zip(pairs, plus, minus):
        symmetric = half * p + even
        antisymmetric = half_odd * m + odd
        out += [symmetric + antisymmetric, symmetric - antisymmetric]
    return out


def restrict(f):
    rest, pairs, _, _ = moments(f, lambda rho: (1.0 - RESCALE) * rho)
    out = [RESCALE * f[0] + rest]
    for k, (even, odd) in enumerate(pairs):
        out += [RESCALE * f[2 * k + 1] + (even + odd), RESCALE * f[2 * k + 2] + (even - odd)]
    return out


def shift_plane(halves, cy, cz):
    lane = lane_ids()
    if cz:
        edge = lane % BX == (0 if cz > 0 else BX - 1)
        halves = [
            jnp.where(
                edge,
                roll_lanes(v, BX * cy + cz - BX * cz),
                roll_lanes(v, BX * cy + cz),
            )
            for v in halves
        ]
    elif cy:
        halves = [roll_lanes(v, BX * cy) for v in halves]
    if cy:
        carried = lane < BX if cy > 0 else lane >= LANES - BX
        halves = [
            jnp.where(carried, halves[1], halves[0]),
            jnp.where(carried, halves[0], halves[1]),
        ]
    return halves


def shift_ring(tiles, cx):
    if not cx:
        return tiles
    row = row_ids()
    turned = [roll_rows(t, cx) for t in tiles]
    if len(tiles) == 1:
        return turned
    edge = row == (0 if cx > 0 else ROWS - 1)
    n = len(tiles)
    return [jnp.where(edge, turned[(i - cx) % n], turned[i]) for i in range(n)]


def move_in_planes(halves):
    moved = [
        shift_plane([halves[0][i], halves[1][i]], int(VEL[i, 1]), int(VEL[i, 2]))
        for i in range(NPOP)
    ]
    return [[moved[i][h] for i in range(NPOP)] for h in range(2)]


def move_along(ring):
    out = [[[], []] for _ in ring]
    for h in range(2):
        for i in range(NPOP):
            for t, v in enumerate(shift_ring([tile[h][i] for tile in ring], int(VEL[i, 0]))):
                out[t][h].append(v)
    return out


def merge(mask, first, second):
    return [
        [jnp.where(mask, v, w) for v, w in zip(a, b)] for a, b in zip(first, second)
    ]


def means():
    shape = (2 * LANES, LANES)
    fine = lax.broadcasted_iota(jnp.int32, shape, 0)
    place = lax.broadcasted_iota(jnp.int32, shape, 1)
    same = (fine // (2 * BX) == place // BX) & (fine % BX // 2 == place % 8)
    return jnp.where(same, 0.125, 0.0).astype(jnp.bfloat16)


def squeeze(planes, matrix):
    cells = jnp.concatenate([jnp.concatenate(halves, axis=1) for halves in planes], axis=0)
    found = None
    for _ in range(3):
        part = cells.astype(jnp.bfloat16)
        product = jnp.dot(part, matrix, preferred_element_type=jnp.float32)
        found = product if found is None else found + product
        cells = cells - part.astype(jnp.float32)
    return [found[ROWS * k : ROWS * (k + 1)] for k in range(len(planes))]


INNER_TILES = (NPOP + 1) // 2 - 2


def fold(tiles):
    out = list(tiles[:INNER_TILES])
    for m in range(6):
        extra, at = tiles[INNER_TILES + m // 3], 2 * (m % 3)
        out[m] = pick(((0,), roll_rows(extra, -1 - at)), ((7,), roll_rows(extra, 5 - at)), (out[m],))
    return out


def unfold(tile, j):
    if j < INNER_TILES:
        return tile(j)
    rows = []
    for m in range(3):
        v = tile(3 * (j - INNER_TILES) + m)
        rows += [((1 + 2 * m,), roll_rows(v, 1 + 2 * m)), ((2 + 2 * m,), roll_rows(v, 2 * m - 5))]
    return pick(*rows, (rows[-1][1],))


def lower():
    return lane_ids() % BX < 8


def pair_up(first, second):
    return first if second is None else jnp.where(lower(), first, second)


def spread(first, second, which):
    if which:
        return jnp.where(lower(), roll_lanes(first, -8), second)
    return jnp.where(lower(), first, roll_lanes(second, 8))


def filled(chosen, h, sources):
    low, high = (sum(chosen[2 * h + z, s] for s in sources) for z in range(2))
    return jnp.where(lower(), low, high) > 0.5


def choose(chosen, quadrant, tiles):
    (_, out), *rest = tiles
    for s, tile in rest:
        out = jnp.where(chosen[quadrant, s] > 0.5, tile, out)
    return out


def half_lanes(h):
    return pl.ds(h * LANES, LANES)


FORWARD = [i for i in range(NPOP) if VEL[i, 0] > 0]
LEVEL = [i for i in range(NPOP) if VEL[i, 0] == 0]
BACKWARD = [i for i in range(NPOP) if VEL[i, 0] < 0]
MOVING = len(FORWARD)

PAIRS = (len(LEVEL) + 1) // 2
WORDS = MOVING + PAIRS


def pick(*choices):
    row = row_ids()
    out = choices[-1][-1]
    for rows, tile in choices[-2::-1]:
        mask = row == rows[0]
        for r in rows[1:]:
            mask = mask | (row == r)
        out = jnp.where(mask, tile, out)
    return out


def pack_message(message, first, second, rim, up):
    for k, i in enumerate(FORWARD if up else BACKWARD):
        f, s = [first(i, h) for h in range(2)], [second(i, h) for h in range(2)]
        s = [v + roll_rows(v, -1) for v in s]
        if up:
            message[k] = pick(
                ((7, 0), roll_rows(f[0], 1)),
                ((1, 2), roll_rows(f[1], 3)),
                ((3,), roll_rows(s[0], -2)),
                ((5,), s[1]),
                ((4,), rim[k]),
                (roll_rows(rim[k], -2),),
            )
        else:
            message[k] = pick(
                ((3, 4), roll_rows(f[0], 3)),
                ((5, 6), roll_rows(f[1], 5)),
                ((7,), roll_rows(s[0], -2)),
                ((1,), s[1]),
                ((0,), roll_rows(rim[k], -3)),
                (roll_rows(rim[k], 3),),
            )
    for k in range(PAIRS):
        shared = []
        for i in (LEVEL + [NPOP])[2 * k : 2 * k + 2]:
            f = [first(i, h) for h in range(2)]
            if up:
                if i < NPOP:
                    s = [roll_rows(second(i, 0), -3), roll_rows(second(i, 1), -1)]
                else:
                    s = [roll_rows(rim[MOVING], -1), roll_rows(rim[MOVING], 5)]
                shared.append(pick(((7,), f[0]), ((1,), roll_rows(f[1], 2)), ((3,), s[0]), (s[1],)))
            else:
                if i < NPOP:
                    s = [roll_rows(second(i, 0), -1), roll_rows(second(i, 1), 1)]
                else:
                    s = [roll_rows(rim[MOVING], -3), roll_rows(rim[MOVING], 3)]
                shared.append(
                    pick(((4,), roll_rows(f[0], 4)), ((6,), roll_rows(f[1], -2)), ((0,), s[0]), (s[1],))
                )
        own_rows = (1, 3, 5, 7) if up else (0, 2, 4, 6)
        message[MOVING + k] = pick((own_rows, shared[0]), (roll_rows(shared[1], 1),))


def shared_tile(message, i):
    k = (LEVEL + [NPOP]).index(i)
    return roll_rows(message[MOVING + k // 2], -(k % 2))


def rim_row(message, k, h, up):
    index, row = (k, 0) if k < MOVING else (WORDS - 1, 1)
    row = 4 + 2 * h if up else row + 2 * h
    return jnp.broadcast_to(message[index, pl.ds(row, 1), :], TILE)


def pack_kernel(fine, solid, coarse, coarse_solid, slot, moved, second, high, low, slot_out, strip, shade, rim, sem):
    planes = fine.shape[2]
    last = coarse.shape[2] - 1

    def bring(source, target, which):
        pltpu.make_async_copy(source, target, sem.at[which]).start()

    def arrive(target, which):
        pltpu.make_async_copy(target, target, sem.at[which]).wait()

    ends = ((0, 0), (planes - 4, 4))
    for half in (pl.ds(0, 7), pl.ds(7, 6), pl.ds(13, 6)):
        for first, row in ends:
            bring(fine.at[0, half, pl.ds(first, 4), :], strip.at[half, pl.ds(row, 4), :], 0)
    bring(solid.at[0], shade, 0)
    for plane, row in ((last, 0), (0, 3)):
        bring(coarse.at[0, :, pl.ds(plane, 1), :], rim.at[pl.ds(0, NPOP), pl.ds(row, 1), :], 1)
        bring(coarse_solid.at[0, pl.ds(plane, 1), :], rim.at[NPOP, pl.ds(row, 1), :], 1)
    bring(slot, slot_out, 2)
    arrive(strip, 0)
    upper = row_ids() < 4
    solids = [
        jnp.where(upper, shade[pl.ds(0, ROWS), half_lanes(h)], shade[pl.ds(planes - ROWS, ROWS), half_lanes(h)])
        for h in range(2)
    ]
    once = move_in_planes(
        [collide([strip[i, :, half_lanes(h)] for i in range(NPOP)], solids[h], TAU_FINE) for h in range(2)]
    )
    arrive(slot_out, 2)
    arrive(rim.at[:, pl.ds(0, 2), :], 1)

    def rim_tile(i):
        v = [rim[i, :, half_lanes(h)] for h in range(2)]
        return pick(((0,), v[1]), ((3,), v[0]), ((4,), roll_rows(v[0], 4)), (roll_rows(v[1], 4),))

    s = rim_tile(NPOP)
    outer = collide([rim_tile(i) for i in range(NPOP)], s, TAU_COARSE) + [s]
    ring = move_along([once])[0]
    twice = [collide(ring[h], solids[h], TAU_FINE) for h in range(2)]
    for h in range(2):
        for i in range(NPOP):
            moved[i, h] = once[h][i]
            second[i, h] = twice[h][i]
        moved[NPOP, h] = solids[h]

    def first_of(i, h):
        return moved[i, h]

    def second_of(i, h):
        return second[i, h]

    pack_message(high, first_of, second_of, [outer[i] for i in FORWARD + [NPOP]], True)
    high[WORDS] = jnp.zeros(TILE, jnp.float32)
    pack_message(low, first_of, second_of, [outer[i] for i in BACKWARD + [NPOP]], False)


def inner_steps(fine, solid, moved, inner, packed, work):
    upper = row_ids() < 4

    def middle(ref, h, *i):
        at = half_lanes(h)
        return jnp.where(upper, ref[(0, *i, pl.ds(ROWS, ROWS), at)], ref[(0, *i, pl.ds(0, ROWS), at)])

    outer = [[moved[i, h] for i in range(NPOP)] for h in range(2)]
    center = move_in_planes(
        [
            collide([middle(fine, h, i) for i in range(NPOP)], middle(solid, h), TAU_FINE)
            for h in range(2)
        ]
    )
    ring = move_along([merge(upper, outer, center), merge(upper, center, outer)])
    for t in range(2):
        for h in range(2):
            s = solid[0, pl.ds(ROWS * t, ROWS), half_lanes(h)]
            ring[t][h] = collide(ring[t][h], s, TAU_FINE)
        ring[t] = move_in_planes(ring[t])
    ring = move_along(ring)
    for i in range(NPOP):
        for h in range(2):
            for t in range(2):
                inner[i, h, pl.ds(ROWS * t, ROWS), :] = ring[t][h][i]
                work[i, h, pl.ds(ROWS * t, ROWS), :] = ring[t][h][i]
    sums = [
        [
            work[i, h, pl.ds(0, ROWS, stride=2), :] + work[i, h, pl.ds(1, ROWS, stride=2), :]
            for h in range(2)
        ]
        for i in range(NPOP)
    ]
    out = restrict(squeeze(sums, means())) + [None]
    pairs = [pair_up(out[2 * j], out[2 * j + 1]) for j in range((NPOP + 1) // 2)]
    for j, tile in enumerate(fold(pairs)):
        packed[j] = tile


def starts_early():
    return lax.axis_index("blk") == 0


def prepare(slot, chosen, matrix):
    groups = chosen.shape[1]
    matrix[...] = means()
    me = lax.axis_index("grp")
    codes = slot[...].reshape(1, groups)
    group_ids = lax.broadcasted_iota(jnp.int32, codes.shape, 1)
    for s in range(groups):
        code = jnp.sum(jnp.where(group_ids == me ^ s, codes, 0), axis=1, keepdims=True)
        for q in range(4):
            chosen[q, s] = jnp.where(lane_ids() * 0 + (4 * me + q) == code, 1.0, 0.0)


def early_kernel(fine, solid, moved, slot, low, inner, packed, chosen, matrix, low_out, work):
    low_out[...] = low[...]

    @pl.when(starts_early())
    def _():
        inner_steps(fine, solid, moved, inner, packed, work)
        prepare(slot, chosen, matrix)


def inner_kernel(fine, solid, moved, slot, *refs):
    *refs, padded, work = refs
    done, (inner, packed, chosen, matrix) = refs[:4], refs[4:]

    @pl.when(starts_early())
    def _():
        for source, target in zip(done, (inner, packed, chosen, matrix)):
            target[...] = source[...]

    @pl.when(jnp.logical_not(starts_early()))
    def _():
        inner_steps(fine, solid, moved, inner, packed, work)
        prepare(slot, chosen, matrix)

    size = packed.shape[0]
    padded[pl.ds(0, size)] = packed[...]
    padded[size] = jnp.zeros(TILE, jnp.float32)


def edge_kernel(moved, second, below, above, matrix, coarse, coarse_solid, edges, packed):
    row = row_ids()

    def middle(i):
        v = [moved[i, h] for h in range(2)]
        if i in FORWARD:
            return pick(
                ((3, 4), roll_rows(v[0], -3)),
                ((5, 6), roll_rows(v[1], -1)),
                (below[FORWARD.index(i)],),
            )
        if i in BACKWARD:
            return pick(
                ((7, 0), roll_rows(v[0], -1)),
                ((1, 2), roll_rows(v[1], 1)),
                (above[BACKWARD.index(i)],),
            )
        return pick(
            ((0,), v[0]),
            ((2,), roll_rows(v[1], 2)),
            ((3,), roll_rows(v[0], 4)),
            ((5,), roll_rows(v[1], -2)),
            ((1, 7), shared_tile(below, i)),
            (shared_tile(above, i),),
        )

    twice = collide([middle(i) for i in range(NPOP)], middle(NPOP), TAU_FINE)
    nothing = jnp.zeros(TILE, jnp.float32)
    both = [[], []]
    for h in range(2):
        for i in range(NPOP):
            cx = int(VEL[i, 0])
            v, mine = roll_rows(twice[i], cx - 2 * h), second[i, h]
            if cx > 0:
                v = pick(
                    ((0, 1, 4, 5), v),
                    ((2, 3), roll_rows(mine, -3)),
                    ((7,), nothing),
                    (roll_rows(below[FORWARD.index(i)], 3 - 2 * h),),
                )
            elif cx < 0:
                v = pick(
                    ((2, 3, 6, 7), v),
                    ((0, 1), roll_rows(mine, -1)),
                    ((5,), nothing),
                    (roll_rows(above[BACKWARD.index(i)], -3 - 2 * h),),
                )
            else:
                v = pick(
                    ((0, 3, 4, 7), v),
                    ((1,), mine),
                    ((2,), roll_rows(mine, 4)),
                    ((6,), roll_rows(shared_tile(below, i), 3 - 2 * h)),
                    (roll_rows(shared_tile(above, i), -3 - 2 * h),),
                )
            both[h].append(v)
    both = move_in_planes(both)
    sums = [[v + roll_rows(v, -1) for v in half] + [None] for half in both]
    odd = row % 2 == 1
    pairs = [
        [half[i] if half[i + 1] is None else jnp.where(odd, roll_rows(half[i + 1], 1), half[i]) for half in sums]
        for i in range(0, NPOP, 2)
    ]
    mean = []
    for pair in squeeze(pairs, matrix[...]):
        mean += [pair, roll_rows(pair, -1)]
    out = restrict(mean[:NPOP]) + [None]
    pairs = [
        out[i] if out[i + 1] is None else jnp.where(odd, roll_rows(out[i + 1], 1), out[i])
        for i in range(0, NPOP, 2)
    ]
    for j in range(len(pairs) // 2):
        packed[j] = pair_up(pairs[2 * j], pairs[2 * j + 1])
    for i in range(NPOP):
        for h in range(2):
            edges[i, h] = both[h][i]


def write_kernel(inner, edges, out):
    row = row_ids()
    for i in range(NPOP):
        for h in range(2):
            edge = edges[i, h]
            out[0, i, pl.ds(0, ROWS), half_lanes(h)] = jnp.where(
                row < 2, edge, inner[i, h, pl.ds(0, ROWS), :]
            )
            out[0, i, pl.ds(ROWS, ROWS), half_lanes(h)] = jnp.where(
                row >= 6, roll_rows(edge, 4), inner[i, h, pl.ds(ROWS, ROWS), :]
            )


def split_kernel(after, tiles, first, second):
    half = first.shape[0]
    first[...] = tiles[pl.ds(0, half)]
    second[...] = tiles[pl.ds(half, half)]


def paste_inner(chosen, sources, tile, base, out):
    masks = [filled(chosen, h, sources) for h in range(2)]
    for j in range((NPOP + 1) // 2):
        tiles = [(s, tile(s, j)) for s in sources]
        for h in range(2):
            low, high = (choose(chosen, 2 * h + z, tiles) for z in range(2))
            for i in range(2 * j, min(2 * j + 2, NPOP)):
                out(i, h, jnp.where(masks[h], spread(low, high, i % 2), base(i, h)))


def paste_kernel(after, coarse, solid, chosen, below, above, *refs):
    *packed, out, ends = refs
    sources = [1, *range(0, chosen.shape[1], 2)]
    parts = dict(zip(sources, packed))

    def write(i, h, tile):
        out[i, h] = tile

    paste_inner(
        chosen, sources, lambda s, j: unfold(lambda k: parts[s][k], j), lambda i, h: coarse[0, i, :, half_lanes(h)], write
    )
    for i in range(NPOP + 1):
        v = [coarse[0, i, :, half_lanes(h)] if i < NPOP else solid[0, :, half_lanes(h)] for h in range(2)]
        tile = pick(((0,), v[0]), ((1,), roll_rows(v[1], 1)), ((2,), roll_rows(v[0], 3)), (roll_rows(v[1], 4),))
        if i == NPOP:
            tile = pick(
                ((4,), rim_row(above, MOVING, 0, False)),
                ((5,), rim_row(above, MOVING, 1, False)),
                ((6,), rim_row(below, MOVING, 0, True)),
                ((7,), rim_row(below, MOVING, 1, True)),
                (tile,),
            )
        ends[i] = tile


def coarse_kernel(after, base, solid, chosen, *refs):
    relayed, out = refs[:-1], refs[-1]
    sources = [2 * k + 3 for k in range(len(relayed) // 2)]
    f = [[None] * NPOP, [None] * NPOP]

    def write(i, h, tile):
        f[h][i] = tile

    half = relayed[0].shape[0]

    def tile(s, j):
        return unfold(lambda k: relayed[s - 3 + k // half][k % half], j)

    paste_inner(chosen, sources, tile, lambda i, h: base[i, h], write)
    f = move_in_planes([collide(f[h], solid[0, :, half_lanes(h)], TAU_COARSE) for h in range(2)])
    for h in range(2):
        for i in range(NPOP):
            out[i, h] = f[h][i]


CHUNKS = (0, 3, 6, 9, 12, 15, 17, NPOP)


def last_kernel(chosen, below, above, base, middle, *refs):
    *packed, result, out, sem = refs
    sources = [0, *others(len(packed))]
    row, lane = row_ids(), lane_ids()
    odd = row % 2 == 1
    pasted = [filled(chosen, h, sources) for h in range(2)]
    pasted = (odd & pasted[1]) | (~odd & pasted[0])
    f = []
    for j in range((NPOP + 1) // 4):
        tiles = [(s, part[j]) for s, part in zip(sources, packed)]
        quadrants = [choose(chosen, q, tiles) for q in range(4)]
        for which in range(2):
            v = [spread(quadrants[2 * h], quadrants[2 * h + 1], which) for h in range(2)]
            f.append(jnp.where(odd, roll_rows(v[1], 1), v[0]))
            f.append(jnp.where(odd, v[1], roll_rows(v[0], -1)))
    f = [jnp.where(pasted, f[i], base[i]) for i in range(NPOP)]
    f = collide(f, base[NPOP], TAU_COARSE)
    copied = 0
    for i in range(NPOP):
        cx, cy, cz = (int(c) for c in VEL[i])
        v = f[i]
        if cx:
            k = (FORWARD if cx > 0 else BACKWARD).index(i)
            rim = [rim_row(below if cx > 0 else above, k, h, cx > 0) for h in range(2)]
            at = row >= 6 if cx > 0 else (row == 4) | (row == 5)
            v = jnp.where(at & ~pasted, jnp.where(odd, rim[1], rim[0]), v)
        if cz:
            edge = lane % BX == (0 if cz > 0 else BX - 1)
            v = jnp.where(
                edge, roll_lanes(v, BX * cy + cz - BX * cz), roll_lanes(v, BX * cy + cz)
            )
        elif cy:
            v = roll_lanes(v, BX * cy)
        if cy:
            carried = lane < BX if cy > 0 else lane >= LANES - BX
            v = jnp.where(carried, jnp.where(odd, roll_rows(v, 1), roll_rows(v, -1)), v)
        for h in range(2):
            inside = middle[i, h]
            if cx > 0:
                tile = pick(
                    ((0,), roll_rows(v, 2 - h)), ((1,), roll_rows(v, 1 - h)), (roll_rows(inside, 1),)
                )
            elif cx < 0:
                tile = pick(
                    ((7,), roll_rows(v, 3 - h)), ((6,), roll_rows(v, 4 - h)), (roll_rows(inside, -1),)
                )
            else:
                tile = pick(((0,), roll_rows(v, -h)), ((7,), roll_rows(v, 5 - h)), (inside,))
            out[0, i, :, half_lanes(h)] = tile
        if i + 1 in CHUNKS:
            some = pl.ds(copied, i + 1 - copied)
            pltpu.make_async_copy(out.at[0, some], result.at[0, some], sem).start()
            copied = i + 1
    pltpu.make_async_copy(out, result, sem).wait()


def others(groups):
    return range(1, groups)


def exchange(array, distance):
    groups = lax.axis_size("grp")
    return lax.ppermute(array, "grp", [(i, i ^ distance) for i in range(groups)])


def held(array):
    return pltpu.with_memory_space_constraint(array, VMEM)


def left(array):
    return pltpu.with_memory_space_constraint(array, pltpu.HBM)


def in_vmem(*shape):
    return VMEM(shape, jnp.float32)


def call(kernel, args, specs, outs, scratch=(), flops=0, name=None, out_space=VMEM):
    single = not isinstance(outs, (list, tuple))
    outs = [outs] if single else list(outs)
    result = pl.pallas_call(
        kernel,
        in_specs=[pl.BlockSpec(memory_space=s) for s in specs],
        out_specs=[pl.BlockSpec(memory_space=out_space)] * len(outs),
        out_shape=outs,
        scratch_shapes=list(scratch),
        compiler_params=pltpu.CompilerParams(vmem_limit_bytes=24 << 20),
        cost_estimate=pl.CostEstimate(flops=flops, bytes_accessed=1, transcendentals=0),
        name=name,
    )(*args)
    return result[0] if single else result


def per_device(fine_pops, fine_solid, coarse_pops, coarse_solid, coarse_slot):
    groups = lax.axis_size("grp")
    blocks = lax.axis_size("blk")
    moved, second, high, low, slot = call(
        pack_kernel,
        tuple(map(left, (fine_pops, fine_solid, coarse_pops, coarse_solid, coarse_slot))),
        [pl.ANY] * 5,
        [
            in_vmem(NPOP + 1, 2, *TILE),
            in_vmem(NPOP, 2, *TILE),
            in_vmem(WORDS + 1, *TILE),
            in_vmem(WORDS, *TILE),
            VMEM((groups,), jnp.int32),
        ],
        [
            in_vmem(NPOP + 2, ROWS, 2 * LANES),
            in_vmem(*fine_solid.shape[1:]),
            in_vmem(NPOP + 1, ROWS, 2 * LANES),
            pltpu.SemaphoreType.DMA((3,)),
        ],
        name="pack",
    )
    fine_v, solid_v = held(fine_pops), held(fine_solid)
    coarse_v, coarse_solid_v = held(coarse_pops), held(coarse_solid)
    inner_shapes = [
        in_vmem(NPOP, 2, 2 * ROWS, LANES),
        in_vmem(INNER_TILES, *TILE),
        in_vmem(4, groups, *TILE),
        VMEM((2 * LANES, LANES), jnp.bfloat16),
    ]
    inner_args = (fine_v, solid_v, held(moved), held(slot))
    *done, low = call(
        early_kernel,
        (*inner_args, held(low)),
        [VMEM] * 5,
        [*inner_shapes, in_vmem(WORDS, *TILE)],
        inner_shapes[:1],
        name="early",
    )
    forward = [(i, (i + 1) % blocks) for i in range(blocks)]
    backward = [(i, (i - 1) % blocks) for i in range(blocks)]
    below = lax.ppermute(high, "blk", forward)
    above = lax.ppermute(low, "blk", backward)
    inner, packed_inner, chosen, matrix, padded_inner = call(
        inner_kernel,
        (*inner_args, *map(held, done)),
        [VMEM] * 8,
        [*inner_shapes, in_vmem(INNER_TILES + 1, *TILE)],
        inner_shapes[:1],
        name="inner",
    )

    across = [exchange(packed_inner, s) for s in range(2, groups, 2)]
    beside = exchange(padded_inner, 1)
    edges, packed_edges = call(
        edge_kernel,
        (held(moved), held(second), held(below), held(above), held(matrix), coarse_v, coarse_solid_v),
        [VMEM] * 7,
        [in_vmem(NPOP, 2, *TILE), in_vmem((NPOP + 1) // 4, *TILE)],
        name="edge",
    )
    edge_parts = [packed_edges] + [exchange(packed_edges, s) for s in others(groups)]
    fine_out = call(
        write_kernel,
        (held(inner), held(edges)),
        [VMEM] * 2,
        jax.ShapeDtypeStruct(fine_pops.shape, jnp.float32),
        name="write",
    )
    inner_parts = [beside, packed_inner, *across]
    base, ends = call(
        paste_kernel,
        (
            held(edges),
            coarse_v,
            coarse_solid_v,
            held(chosen),
            held(below),
            held(above),
            *map(held, inner_parts),
        ),
        [VMEM] * (6 + len(inner_parts)),
        [in_vmem(NPOP, 2, *TILE), in_vmem(NPOP + 1, *TILE)],
        name="paste",
    )
    relayed = []
    for part in across:
        halves = call(
            split_kernel,
            (held(base), held(part)),
            [VMEM] * 2,
            [in_vmem(part.shape[0] // 2, *TILE)] * 2,
            name="split",
        )
        relayed += [exchange(half, 1) for half in halves]
    middle = call(
        coarse_kernel,
        (left(fine_out), held(base), coarse_solid_v, held(chosen), *map(held, relayed)),
        [pl.ANY] + [VMEM] * (3 + len(relayed)),
        in_vmem(NPOP, 2, *TILE),
        name="coarse",
    )
    coarse_out = call(
        last_kernel,
        (held(chosen), held(below), held(above), held(ends), held(middle), *map(held, edge_parts)),
        [VMEM] * (5 + len(edge_parts)),
        jax.ShapeDtypeStruct(coarse_pops.shape, jnp.float32),
        [in_vmem(*coarse_pops.shape), pltpu.SemaphoreType.DMA],
        out_space=pl.ANY,
        name="last",
    )
    return fine_out, coarse_out


def solution(mesh):
    placed = (
        P("grp", None, "blk", None),
        P("grp", "blk", None),
        P("grp", None, "blk", None),
        P("grp", "blk", None),
        P(),
    )
    return jax.shard_map(
        per_device,
        mesh=mesh,
        in_specs=placed,
        out_specs=(P("grp", None, "blk", None), P("grp", None, "blk", None)),
        check_vma=False,
    )
```

```python
import jax
import jax.numpy as jnp
import numpy as np
from jax import lax
from jax.experimental import pallas as pl
from jax.experimental.pallas import tpu as pltpu
from jax.sharding import PartitionSpec as P

VEL = np.array(
    [
        [0, 0, 0],
        [1, 0, 0],
        [-1, 0, 0],
        [0, 1, 0],
        [0, -1, 0],
        [0, 0, 1],
        [0, 0, -1],
        [1, 1, 0],
        [-1, -1, 0],
        [1, -1, 0],
        [-1, 1, 0],
        [1, 0, 1],
        [-1, 0, -1],
        [1, 0, -1],
        [-1, 0, 1],
        [0, 1, 1],
        [0, -1, -1],
        [0, 1, -1],
        [0, -1, 1],
    ]
)
NPOP = 19
BX = 16
TAU_FINE = 0.6
TAU_COARSE = 0.55
RESCALE = 2.0 * TAU_COARSE / TAU_FINE

ROWS, LANES = 8, 128
TILE = (ROWS, LANES)
VMEM = pltpu.VMEM


def row_ids():
    return lax.broadcasted_iota(jnp.int32, TILE, 0)


def lane_ids():
    return lax.broadcasted_iota(jnp.int32, TILE, 1)


def roll_rows(tile, shift):
    return pltpu.roll(tile, shift % ROWS, 0)


def roll_lanes(tile, shift):
    return pltpu.roll(tile, shift % LANES, 1)


def moments(f, scale):
    minus = [f[i] - f[i + 1] for i in range(1, NPOP, 2)]
    plus = [f[i] + f[i + 1] for i in range(1, NPOP, 2)]
    rho = ((f[0] + plus[0]) + (plus[1] + plus[2])) + (
        (plus[3] + plus[4]) + (plus[5] + plus[6])
    ) + (plus[7] + plus[8])
    jx = (minus[0] + minus[3]) + (minus[4] + minus[5]) + minus[6]
    jy = (minus[1] + minus[3]) - (minus[4] - minus[7]) + minus[8]
    jz = (minus[2] + minus[5]) - (minus[6] - minus[7]) - minus[8]
    inverse = 1.5 / rho
    ux, uy, uz = jx * inverse, jy * inverse, jz * inverse
    amount = scale(rho)
    base = amount * (1.0 - (2.0 / 3.0) * (ux * ux + uy * uy + uz * uz))
    directions = [ux, uy, uz, ux + uy, ux - uy, ux + uz, ux - uz, uy + uz, uy - uz]
    base_axis, base_diag = base * (1.0 / 18.0), base * (1.0 / 36.0)
    amount_axis, amount_diag = amount * (1.0 / 9.0), amount * (1.0 / 18.0)
    pairs = []
    for k, along in enumerate(directions):
        odd = (amount_axis if k < 3 else amount_diag) * along
        pairs.append(((base_axis if k < 3 else base_diag) + odd * along, odd))
    return base * (1.0 / 3.0), pairs, plus, minus


def collide(f, solid, tau):
    rate = (1.0 - solid) * (1.0 / tau)
    rest, pairs, plus, minus = moments(f, lambda rho: rate * rho)
    keep = 1.0 - rate
    half = 0.5 * keep
    half_odd = half - solid
    out = [keep * f[0] + rest]
    for (even, odd), p, m in zip(pairs, plus, minus):
        symmetric = half * p + even
        antisymmetric = half_odd * m + odd
        out += [symmetric + antisymmetric, symmetric - antisymmetric]
    return out


def restrict(f):
    rest, pairs, _, _ = moments(f, lambda rho: (1.0 - RESCALE) * rho)
    out = [RESCALE * f[0] + rest]
    for k, (even, odd) in enumerate(pairs):
        out += [RESCALE * f[2 * k + 1] + (even + odd), RESCALE * f[2 * k + 2] + (even - odd)]
    return out


def shift_plane(halves, cy, cz):
    lane = lane_ids()
    if cz:
        edge = lane % BX == (0 if cz > 0 else BX - 1)
        halves = [
            jnp.where(
                edge,
                roll_lanes(v, BX * cy + cz - BX * cz),
                roll_lanes(v, BX * cy + cz),
            )
            for v in halves
        ]
    elif cy:
        halves = [roll_lanes(v, BX * cy) for v in halves]
    if cy:
        carried = lane < BX if cy > 0 else lane >= LANES - BX
        halves = [
            jnp.where(carried, halves[1], halves[0]),
            jnp.where(carried, halves[0], halves[1]),
        ]
    return halves


def shift_ring(tiles, cx):
    if not cx:
        return tiles
    row = row_ids()
    turned = [roll_rows(t, cx) for t in tiles]
    if len(tiles) == 1:
        return turned
    edge = row == (0 if cx > 0 else ROWS - 1)
    n = len(tiles)
    return [jnp.where(edge, turned[(i - cx) % n], turned[i]) for i in range(n)]


def move_in_planes(halves):
    moved = [
        shift_plane([halves[0][i], halves[1][i]], int(VEL[i, 1]), int(VEL[i, 2]))
        for i in range(NPOP)
    ]
    return [[moved[i][h] for i in range(NPOP)] for h in range(2)]


def move_along(ring):
    out = [[[], []] for _ in ring]
    for h in range(2):
        for i in range(NPOP):
            for t, v in enumerate(shift_ring([tile[h][i] for tile in ring], int(VEL[i, 0]))):
                out[t][h].append(v)
    return out


def merge(mask, first, second):
    return [
        [jnp.where(mask, v, w) for v, w in zip(a, b)] for a, b in zip(first, second)
    ]


def means():
    shape = (2 * LANES, LANES)
    fine = lax.broadcasted_iota(jnp.int32, shape, 0)
    place = lax.broadcasted_iota(jnp.int32, shape, 1)
    same = (fine // (2 * BX) == place // BX) & (fine % BX // 2 == place % 8)
    return jnp.where(same, 0.125, 0.0).astype(jnp.bfloat16)


def squeeze(planes, matrix):
    cells = jnp.concatenate([jnp.concatenate(halves, axis=1) for halves in planes], axis=0)
    found = None
    for _ in range(3):
        part = cells.astype(jnp.bfloat16)
        product = jnp.dot(part, matrix, preferred_element_type=jnp.float32)
        found = product if found is None else found + product
        cells = cells - part.astype(jnp.float32)
    return [found[ROWS * k : ROWS * (k + 1)] for k in range(len(planes))]


INNER_TILES = (NPOP + 1) // 2 - 2


def fold(tiles):
    out = list(tiles[:INNER_TILES])
    for m in range(6):
        extra, at = tiles[INNER_TILES + m // 3], 2 * (m % 3)
        out[m] = pick(((0,), roll_rows(extra, -1 - at)), ((7,), roll_rows(extra, 5 - at)), (out[m],))
    return out


def unfold(tile, j):
    if j < INNER_TILES:
        return tile(j)
    rows = []
    for m in range(3):
        v = tile(3 * (j - INNER_TILES) + m)
        rows += [((1 + 2 * m,), roll_rows(v, 1 + 2 * m)), ((2 + 2 * m,), roll_rows(v, 2 * m - 5))]
    return pick(*rows, (rows[-1][1],))


def lower():
    return lane_ids() % BX < 8


def pair_up(first, second):
    return first if second is None else jnp.where(lower(), first, second)


def spread(first, second, which):
    if which:
        return jnp.where(lower(), roll_lanes(first, -8), second)
    return jnp.where(lower(), first, roll_lanes(second, 8))


def filled(chosen, h, sources):
    low, high = (sum(chosen[2 * h + z, s] for s in sources) for z in range(2))
    return jnp.where(lower(), low, high) > 0.5


def choose(chosen, quadrant, tiles):
    (_, out), *rest = tiles
    for s, tile in rest:
        out = jnp.where(chosen[quadrant, s] > 0.5, tile, out)
    return out


def half_lanes(h):
    return pl.ds(h * LANES, LANES)


FORWARD = [i for i in range(NPOP) if VEL[i, 0] > 0]
LEVEL = [i for i in range(NPOP) if VEL[i, 0] == 0]
BACKWARD = [i for i in range(NPOP) if VEL[i, 0] < 0]
MOVING = len(FORWARD)

PAIRS = (len(LEVEL) + 1) // 2
WORDS = MOVING + PAIRS


def pick(*choices):
    row = row_ids()
    out = choices[-1][-1]
    for rows, tile in choices[-2::-1]:
        mask = row == rows[0]
        for r in rows[1:]:
            mask = mask | (row == r)
        out = jnp.where(mask, tile, out)
    return out


def pack_message(message, first, second, rim, up):
    for k, i in enumerate(FORWARD if up else BACKWARD):
        f, s = [first(i, h) for h in range(2)], [second(i, h) for h in range(2)]
        s = [v + roll_rows(v, -1) for v in s]
        if up:
            message[k] = pick(
                ((7, 0), roll_rows(f[0], 1)),
                ((1, 2), roll_rows(f[1], 3)),
                ((3,), roll_rows(s[0], -2)),
                ((5,), s[1]),
                ((4,), rim[k]),
                (roll_rows(rim[k], -2),),
            )
        else:
            message[k] = pick(
                ((3, 4), roll_rows(f[0], 3)),
                ((5, 6), roll_rows(f[1], 5)),
                ((7,), roll_rows(s[0], -2)),
                ((1,), s[1]),
                ((0,), roll_rows(rim[k], -3)),
                (roll_rows(rim[k], 3),),
            )
    for k in range(PAIRS):
        shared = []
        for i in (LEVEL + [NPOP])[2 * k : 2 * k + 2]:
            f = [first(i, h) for h in range(2)]
            if up:
                if i < NPOP:
                    s = [roll_rows(second(i, 0), -3), roll_rows(second(i, 1), -1)]
                else:
                    s = [roll_rows(rim[MOVING], -1), roll_rows(rim[MOVING], 5)]
                shared.append(pick(((7,), f[0]), ((1,), roll_rows(f[1], 2)), ((3,), s[0]), (s[1],)))
            else:
                if i < NPOP:
                    s = [roll_rows(second(i, 0), -1), roll_rows(second(i, 1), 1)]
                else:
                    s = [roll_rows(rim[MOVING], -3), roll_rows(rim[MOVING], 3)]
                shared.append(
                    pick(((4,), roll_rows(f[0], 4)), ((6,), roll_rows(f[1], -2)), ((0,), s[0]), (s[1],))
                )
        own_rows = (1, 3, 5, 7) if up else (0, 2, 4, 6)
        message[MOVING + k] = pick((own_rows, shared[0]), (roll_rows(shared[1], 1),))


def shared_tile(message, i):
    k = (LEVEL + [NPOP]).index(i)
    return roll_rows(message[MOVING + k // 2], -(k % 2))


def rim_row(message, k, h, up):
    index, row = (k, 0) if k < MOVING else (WORDS - 1, 1)
    row = 4 + 2 * h if up else row + 2 * h
    return jnp.broadcast_to(message[index, pl.ds(row, 1), :], TILE)


def pack_kernel(
    fine, solid, coarse, coarse_solid, slot, moved, second, high, low, center, shade, slot_out, strip, rim, sem
):
    planes = fine.shape[2]
    last = coarse.shape[2] - 1

    def bring(source, target, which):
        pltpu.make_async_copy(source, target, sem.at[which]).start()

    def arrive(target, which):
        pltpu.make_async_copy(target, target, sem.at[which]).wait()

    ends = ((0, 0), (planes - 4, 4))
    for half in (pl.ds(0, 7), pl.ds(7, 6), pl.ds(13, 6)):
        for first, row in ends:
            bring(fine.at[0, half, pl.ds(first, 4), :], strip.at[half, pl.ds(row, 4), :], 0)
    bring(solid.at[0], shade, 0)
    for plane, row in ((last, 0), (0, 3)):
        bring(coarse.at[0, :, pl.ds(plane, 1), :], rim.at[pl.ds(0, NPOP), pl.ds(row, 1), :], 1)
        bring(coarse_solid.at[0, pl.ds(plane, 1), :], rim.at[NPOP, pl.ds(row, 1), :], 1)
    bring(slot, slot_out, 2)
    for first, row in ((4, 4), (8, 0)):
        bring(fine.at[0, :, pl.ds(first, 4), :], center.at[:, pl.ds(row, 4), :], 3)
    arrive(strip, 0)
    upper = row_ids() < 4
    solids = [
        jnp.where(upper, shade[pl.ds(0, ROWS), half_lanes(h)], shade[pl.ds(planes - ROWS, ROWS), half_lanes(h)])
        for h in range(2)
    ]
    once = move_in_planes(
        [collide([strip[i, :, half_lanes(h)] for i in range(NPOP)], solids[h], TAU_FINE) for h in range(2)]
    )
    arrive(slot_out, 2)
    arrive(rim.at[:, pl.ds(0, 2), :], 1)

    def rim_tile(i):
        v = [rim[i, :, half_lanes(h)] for h in range(2)]
        return pick(((0,), v[1]), ((3,), v[0]), ((4,), roll_rows(v[0], 4)), (roll_rows(v[1], 4),))

    s = rim_tile(NPOP)
    outer = collide([rim_tile(i) for i in range(NPOP)], s, TAU_COARSE) + [s]
    ring = move_along([once])[0]
    twice = [collide(ring[h], solids[h], TAU_FINE) for h in range(2)]
    for h in range(2):
        for i in range(NPOP):
            moved[i, h] = once[h][i]
            second[i, h] = twice[h][i]
        moved[NPOP, h] = solids[h]

    def first_of(i, h):
        return moved[i, h]

    def second_of(i, h):
        return second[i, h]

    pack_message(high, first_of, second_of, [outer[i] for i in FORWARD + [NPOP]], True)
    high[WORDS] = jnp.zeros(TILE, jnp.float32)
    pack_message(low, first_of, second_of, [outer[i] for i in BACKWARD + [NPOP]], False)
    arrive(center, 3)


def inner_steps(center, solid, moved, inner, packed, work):
    upper = row_ids() < 4
    solids = [
        [solid[pl.ds(ROWS * t, ROWS), half_lanes(h)] for h in range(2)] for t in range(2)
    ]
    outer = [[moved[i, h] for i in range(NPOP)] for h in range(2)]
    between = move_in_planes(
        [
            collide(
                [center[i, :, half_lanes(h)] for i in range(NPOP)],
                jnp.where(upper, solids[1][h], solids[0][h]),
                TAU_FINE,
            )
            for h in range(2)
        ]
    )
    ring = move_along([merge(upper, outer, between), merge(upper, between, outer)])
    for t in range(2):
        for h in range(2):
            ring[t][h] = collide(ring[t][h], solids[t][h], TAU_FINE)
        ring[t] = move_in_planes(ring[t])
    ring = move_along(ring)
    for i in range(NPOP):
        for h in range(2):
            for t in range(2):
                inner[i, h, pl.ds(ROWS * t, ROWS), :] = ring[t][h][i]
                work[i, h, pl.ds(ROWS * t, ROWS), :] = ring[t][h][i]
    sums = [
        [
            work[i, h, pl.ds(0, ROWS, stride=2), :] + work[i, h, pl.ds(1, ROWS, stride=2), :]
            for h in range(2)
        ]
        for i in range(NPOP)
    ]
    out = restrict(squeeze(sums, means())) + [None]
    pairs = [pair_up(out[2 * j], out[2 * j + 1]) for j in range((NPOP + 1) // 2)]
    for j, tile in enumerate(fold(pairs)):
        packed[j] = tile


def starts_early():
    return lax.axis_index("blk") == 0


def prepare(slot, chosen, matrix):
    groups = chosen.shape[1]
    matrix[...] = means()
    me = lax.axis_index("grp")
    codes = slot[...].reshape(1, groups)
    group_ids = lax.broadcasted_iota(jnp.int32, codes.shape, 1)
    for s in range(groups):
        code = jnp.sum(jnp.where(group_ids == me ^ s, codes, 0), axis=1, keepdims=True)
        for q in range(4):
            chosen[q, s] = jnp.where(lane_ids() * 0 + (4 * me + q) == code, 1.0, 0.0)


def early_kernel(center, solid, moved, slot, low, inner, packed, chosen, matrix, low_out, work):
    low_out[...] = low[...]

    @pl.when(starts_early())
    def _():
        inner_steps(center, solid, moved, inner, packed, work)
        prepare(slot, chosen, matrix)


def inner_kernel(center, solid, moved, slot, *refs):
    *refs, padded, work = refs
    done, (inner, packed, chosen, matrix) = refs[:4], refs[4:]

    @pl.when(starts_early())
    def _():
        for source, target in zip(done, (inner, packed, chosen, matrix)):
            target[...] = source[...]

    @pl.when(jnp.logical_not(starts_early()))
    def _():
        inner_steps(center, solid, moved, inner, packed, work)
        prepare(slot, chosen, matrix)

    size = packed.shape[0]
    padded[pl.ds(0, size)] = packed[...]
    padded[size] = jnp.zeros(TILE, jnp.float32)


def edge_kernel(moved, second, below, above, matrix, coarse, coarse_solid, edges, packed):
    row = row_ids()

    def middle(i):
        v = [moved[i, h] for h in range(2)]
        if i in FORWARD:
            return pick(
                ((3, 4), roll_rows(v[0], -3)),
                ((5, 6), roll_rows(v[1], -1)),
                (below[FORWARD.index(i)],),
            )
        if i in BACKWARD:
            return pick(
                ((7, 0), roll_rows(v[0], -1)),
                ((1, 2), roll_rows(v[1], 1)),
                (above[BACKWARD.index(i)],),
            )
        return pick(
            ((0,), v[0]),
            ((2,), roll_rows(v[1], 2)),
            ((3,), roll_rows(v[0], 4)),
            ((5,), roll_rows(v[1], -2)),
            ((1, 7), shared_tile(below, i)),
            (shared_tile(above, i),),
        )

    twice = collide([middle(i) for i in range(NPOP)], middle(NPOP), TAU_FINE)
    nothing = jnp.zeros(TILE, jnp.float32)
    both = [[], []]
    for h in range(2):
        for i in range(NPOP):
            cx = int(VEL[i, 0])
            v, mine = roll_rows(twice[i], cx - 2 * h), second[i, h]
            if cx > 0:
                v = pick(
                    ((0, 1, 4, 5), v),
                    ((2, 3), roll_rows(mine, -3)),
                    ((7,), nothing),
                    (roll_rows(below[FORWARD.index(i)], 3 - 2 * h),),
                )
            elif cx < 0:
                v = pick(
                    ((2, 3, 6, 7), v),
                    ((0, 1), roll_rows(mine, -1)),
                    ((5,), nothing),
                    (roll_rows(above[BACKWARD.index(i)], -3 - 2 * h),),
                )
            else:
                v = pick(
                    ((0, 3, 4, 7), v),
                    ((1,), mine),
                    ((2,), roll_rows(mine, 4)),
                    ((6,), roll_rows(shared_tile(below, i), 3 - 2 * h)),
                    (roll_rows(shared_tile(above, i), -3 - 2 * h),),
                )
            both[h].append(v)
    both = move_in_planes(both)
    sums = [[v + roll_rows(v, -1) for v in half] + [None] for half in both]
    odd = row % 2 == 1
    pairs = [
        [half[i] if half[i + 1] is None else jnp.where(odd, roll_rows(half[i + 1], 1), half[i]) for half in sums]
        for i in range(0, NPOP, 2)
    ]
    mean = []
    for pair in squeeze(pairs, matrix[...]):
        mean += [pair, roll_rows(pair, -1)]
    out = restrict(mean[:NPOP]) + [None]
    pairs = [
        out[i] if out[i + 1] is None else jnp.where(odd, roll_rows(out[i + 1], 1), out[i])
        for i in range(0, NPOP, 2)
    ]
    for j in range(len(pairs) // 2):
        packed[j] = pair_up(pairs[2 * j], pairs[2 * j + 1])
    for i in range(NPOP):
        for h in range(2):
            edges[i, h] = both[h][i]


def write_kernel(inner, edges, out):
    row = row_ids()
    for i in range(NPOP):
        for h in range(2):
            edge = edges[i, h]
            out[0, i, pl.ds(0, ROWS), half_lanes(h)] = jnp.where(
                row < 2, edge, inner[i, h, pl.ds(0, ROWS), :]
            )
            out[0, i, pl.ds(ROWS, ROWS), half_lanes(h)] = jnp.where(
                row >= 6, roll_rows(edge, 4), inner[i, h, pl.ds(ROWS, ROWS), :]
            )


def split_kernel(after, tiles, first, second):
    half = first.shape[0]
    first[...] = tiles[pl.ds(0, half)]
    second[...] = tiles[pl.ds(half, half)]


def paste_inner(chosen, sources, tile, base, out):
    masks = [filled(chosen, h, sources) for h in range(2)]
    for j in range((NPOP + 1) // 2):
        tiles = [(s, tile(s, j)) for s in sources]
        for h in range(2):
            low, high = (choose(chosen, 2 * h + z, tiles) for z in range(2))
            for i in range(2 * j, min(2 * j + 2, NPOP)):
                out(i, h, jnp.where(masks[h], spread(low, high, i % 2), base(i, h)))


def paste_kernel(after, coarse, solid, chosen, below, above, *refs):
    *packed, out, ends = refs
    sources = [1, *range(0, chosen.shape[1], 2)]
    parts = dict(zip(sources, packed))

    def write(i, h, tile):
        out[i, h] = tile

    paste_inner(
        chosen, sources, lambda s, j: unfold(lambda k: parts[s][k], j), lambda i, h: coarse[0, i, :, half_lanes(h)], write
    )
    for i in range(NPOP + 1):
        v = [coarse[0, i, :, half_lanes(h)] if i < NPOP else solid[0, :, half_lanes(h)] for h in range(2)]
        tile = pick(((0,), v[0]), ((1,), roll_rows(v[1], 1)), ((2,), roll_rows(v[0], 3)), (roll_rows(v[1], 4),))
        if i == NPOP:
            tile = pick(
                ((4,), rim_row(above, MOVING, 0, False)),
                ((5,), rim_row(above, MOVING, 1, False)),
                ((6,), rim_row(below, MOVING, 0, True)),
                ((7,), rim_row(below, MOVING, 1, True)),
                (tile,),
            )
        ends[i] = tile


def coarse_kernel(after, base, solid, chosen, *refs):
    relayed, out = refs[:-1], refs[-1]
    sources = [2 * k + 3 for k in range(len(relayed) // 2)]
    f = [[None] * NPOP, [None] * NPOP]

    def write(i, h, tile):
        f[h][i] = tile

    half = relayed[0].shape[0]

    def tile(s, j):
        return unfold(lambda k: relayed[s - 3 + k // half][k % half], j)

    paste_inner(chosen, sources, tile, lambda i, h: base[i, h], write)
    f = move_in_planes([collide(f[h], solid[0, :, half_lanes(h)], TAU_COARSE) for h in range(2)])
    for h in range(2):
        for i in range(NPOP):
            out[i, h] = f[h][i]


CHUNKS = (0, 3, 6, 9, 12, 15, 17, NPOP)


def last_kernel(chosen, below, above, base, middle, *refs):
    *packed, result, out, sem = refs
    sources = [0, *others(len(packed))]
    row, lane = row_ids(), lane_ids()
    odd = row % 2 == 1
    pasted = [filled(chosen, h, sources) for h in range(2)]
    pasted = (odd & pasted[1]) | (~odd & pasted[0])
    f = []
    for j in range((NPOP + 1) // 4):
        tiles = [(s, part[j]) for s, part in zip(sources, packed)]
        quadrants = [choose(chosen, q, tiles) for q in range(4)]
        for which in range(2):
            v = [spread(quadrants[2 * h], quadrants[2 * h + 1], which) for h in range(2)]
            f.append(jnp.where(odd, roll_rows(v[1], 1), v[0]))
            f.append(jnp.where(odd, v[1], roll_rows(v[0], -1)))
    f = [jnp.where(pasted, f[i], base[i]) for i in range(NPOP)]
    f = collide(f, base[NPOP], TAU_COARSE)
    copied = 0
    for i in range(NPOP):
        cx, cy, cz = (int(c) for c in VEL[i])
        v = f[i]
        if cx:
            k = (FORWARD if cx > 0 else BACKWARD).index(i)
            rim = [rim_row(below if cx > 0 else above, k, h, cx > 0) for h in range(2)]
            at = row >= 6 if cx > 0 else (row == 4) | (row == 5)
            v = jnp.where(at & ~pasted, jnp.where(odd, rim[1], rim[0]), v)
        if cz:
            edge = lane % BX == (0 if cz > 0 else BX - 1)
            v = jnp.where(
                edge, roll_lanes(v, BX * cy + cz - BX * cz), roll_lanes(v, BX * cy + cz)
            )
        elif cy:
            v = roll_lanes(v, BX * cy)
        if cy:
            carried = lane < BX if cy > 0 else lane >= LANES - BX
            v = jnp.where(carried, jnp.where(odd, roll_rows(v, 1), roll_rows(v, -1)), v)
        for h in range(2):
            inside = middle[i, h]
            if cx > 0:
                tile = pick(
                    ((0,), roll_rows(v, 2 - h)), ((1,), roll_rows(v, 1 - h)), (roll_rows(inside, 1),)
                )
            elif cx < 0:
                tile = pick(
                    ((7,), roll_rows(v, 3 - h)), ((6,), roll_rows(v, 4 - h)), (roll_rows(inside, -1),)
                )
            else:
                tile = pick(((0,), roll_rows(v, -h)), ((7,), roll_rows(v, 5 - h)), (inside,))
            out[0, i, :, half_lanes(h)] = tile
        if i + 1 in CHUNKS:
            some = pl.ds(copied, i + 1 - copied)
            pltpu.make_async_copy(out.at[0, some], result.at[0, some], sem).start()
            copied = i + 1
    pltpu.make_async_copy(out, result, sem).wait()


def others(groups):
    return range(1, groups)


def exchange(array, distance):
    groups = lax.axis_size("grp")
    return lax.ppermute(array, "grp", [(i, i ^ distance) for i in range(groups)])


def held(array):
    return pltpu.with_memory_space_constraint(array, VMEM)


def left(array):
    return pltpu.with_memory_space_constraint(array, pltpu.HBM)


def in_vmem(*shape):
    return VMEM(shape, jnp.float32)


def call(kernel, args, specs, outs, scratch=(), flops=0, name=None, out_space=VMEM):
    single = not isinstance(outs, (list, tuple))
    outs = [outs] if single else list(outs)
    result = pl.pallas_call(
        kernel,
        in_specs=[pl.BlockSpec(memory_space=s) for s in specs],
        out_specs=[pl.BlockSpec(memory_space=out_space)] * len(outs),
        out_shape=outs,
        scratch_shapes=list(scratch),
        compiler_params=pltpu.CompilerParams(vmem_limit_bytes=24 << 20),
        cost_estimate=pl.CostEstimate(flops=flops, bytes_accessed=1, transcendentals=0),
        name=name,
    )(*args)
    return result[0] if single else result


def per_device(fine_pops, fine_solid, coarse_pops, coarse_solid, coarse_slot):
    groups = lax.axis_size("grp")
    blocks = lax.axis_size("blk")
    moved, second, high, low, center, shade, slot = call(
        pack_kernel,
        tuple(map(left, (fine_pops, fine_solid, coarse_pops, coarse_solid, coarse_slot))),
        [pl.ANY] * 5,
        [
            in_vmem(NPOP + 1, 2, *TILE),
            in_vmem(NPOP, 2, *TILE),
            in_vmem(WORDS + 1, *TILE),
            in_vmem(WORDS, *TILE),
            in_vmem(NPOP, ROWS, 2 * LANES),
            in_vmem(*fine_solid.shape[1:]),
            VMEM((groups,), jnp.int32),
        ],
        [
            in_vmem(NPOP + 2, ROWS, 2 * LANES),
            in_vmem(NPOP + 1, ROWS, 2 * LANES),
            pltpu.SemaphoreType.DMA((4,)),
        ],
        name="pack",
    )
    coarse_v, coarse_solid_v = held(coarse_pops), held(coarse_solid)
    inner_shapes = [
        in_vmem(NPOP, 2, 2 * ROWS, LANES),
        in_vmem(INNER_TILES, *TILE),
        in_vmem(4, groups, *TILE),
        VMEM((2 * LANES, LANES), jnp.bfloat16),
    ]
    inner_args = (held(center), held(shade), held(moved), held(slot))
    *done, low = call(
        early_kernel,
        (*inner_args, held(low)),
        [VMEM] * 5,
        [*inner_shapes, in_vmem(WORDS, *TILE)],
        inner_shapes[:1],
        name="early",
    )
    forward = [(i, (i + 1) % blocks) for i in range(blocks)]
    backward = [(i, (i - 1) % blocks) for i in range(blocks)]
    below = lax.ppermute(high, "blk", forward)
    above = lax.ppermute(low, "blk", backward)
    inner, packed_inner, chosen, matrix, padded_inner = call(
        inner_kernel,
        (*inner_args, *map(held, done)),
        [VMEM] * 8,
        [*inner_shapes, in_vmem(INNER_TILES + 1, *TILE)],
        inner_shapes[:1],
        name="inner",
    )

    across = [exchange(packed_inner, s) for s in range(2, groups, 2)]
    beside = exchange(padded_inner, 1)
    edges, packed_edges = call(
        edge_kernel,
        (held(moved), held(second), held(below), held(above), held(matrix), coarse_v, coarse_solid_v),
        [VMEM] * 7,
        [in_vmem(NPOP, 2, *TILE), in_vmem((NPOP + 1) // 4, *TILE)],
        name="edge",
    )
    edge_parts = [packed_edges] + [exchange(packed_edges, s) for s in others(groups)]
    fine_out = call(
        write_kernel,
        (held(inner), held(edges)),
        [VMEM] * 2,
        jax.ShapeDtypeStruct(fine_pops.shape, jnp.float32),
        name="write",
    )
    inner_parts = [beside, packed_inner, *across]
    base, ends = call(
        paste_kernel,
        (
            held(edges),
            coarse_v,
            coarse_solid_v,
            held(chosen),
            held(below),
            held(above),
            *map(held, inner_parts),
        ),
        [VMEM] * (6 + len(inner_parts)),
        [in_vmem(NPOP, 2, *TILE), in_vmem(NPOP + 1, *TILE)],
        name="paste",
    )
    relayed = []
    for part in across:
        halves = call(
            split_kernel,
            (held(base), held(part)),
            [VMEM] * 2,
            [in_vmem(part.shape[0] // 2, *TILE)] * 2,
            name="split",
        )
        relayed += [exchange(half, 1) for half in halves]
    middle = call(
        coarse_kernel,
        (left(fine_out), held(base), coarse_solid_v, held(chosen), *map(held, relayed)),
        [pl.ANY] + [VMEM] * (3 + len(relayed)),
        in_vmem(NPOP, 2, *TILE),
        name="coarse",
    )
    coarse_out = call(
        last_kernel,
        (held(chosen), held(below), held(above), held(ends), held(middle), *map(held, edge_parts)),
        [VMEM] * (5 + len(edge_parts)),
        jax.ShapeDtypeStruct(coarse_pops.shape, jnp.float32),
        [in_vmem(*coarse_pops.shape), pltpu.SemaphoreType.DMA],
        out_space=pl.ANY,
        name="last",
    )
    return fine_out, coarse_out


def solution(mesh):
    placed = (
        P("grp", None, "blk", None),
        P("grp", "blk", None),
        P("grp", None, "blk", None),
        P("grp", "blk", None),
        P(),
    )
    return jax.shard_map(
        per_device,
        mesh=mesh,
        in_specs=placed,
        out_specs=(P("grp", None, "blk", None), P("grp", None, "blk", None)),
        check_vma=False,
    )
```

```python
import jax
import jax.numpy as jnp
import numpy as np
from jax import lax
from jax.experimental import pallas as pl
from jax.experimental.pallas import tpu as pltpu
from jax.sharding import PartitionSpec as P

VEL = np.array(
    [
        [0, 0, 0],
        [1, 0, 0],
        [-1, 0, 0],
        [0, 1, 0],
        [0, -1, 0],
        [0, 0, 1],
        [0, 0, -1],
        [1, 1, 0],
        [-1, -1, 0],
        [1, -1, 0],
        [-1, 1, 0],
        [1, 0, 1],
        [-1, 0, -1],
        [1, 0, -1],
        [-1, 0, 1],
        [0, 1, 1],
        [0, -1, -1],
        [0, 1, -1],
        [0, -1, 1],
    ]
)
NPOP = 19
BX = 16
TAU_FINE = 0.6
TAU_COARSE = 0.55
RESCALE = 2.0 * TAU_COARSE / TAU_FINE

ROWS, LANES = 8, 128
TILE = (ROWS, LANES)
VMEM = pltpu.VMEM


def row_ids():
    return lax.broadcasted_iota(jnp.int32, TILE, 0)


def lane_ids():
    return lax.broadcasted_iota(jnp.int32, TILE, 1)


def roll_rows(tile, shift):
    return pltpu.roll(tile, shift % ROWS, 0)


def roll_lanes(tile, shift):
    return pltpu.roll(tile, shift % LANES, 1)


def moments(f, scale):
    minus = [f[i] - f[i + 1] for i in range(1, NPOP, 2)]
    plus = [f[i] + f[i + 1] for i in range(1, NPOP, 2)]
    rho = ((f[0] + plus[0]) + (plus[1] + plus[2])) + (
        (plus[3] + plus[4]) + (plus[5] + plus[6])
    ) + (plus[7] + plus[8])
    jx = (minus[0] + minus[3]) + (minus[4] + minus[5]) + minus[6]
    jy = (minus[1] + minus[3]) - (minus[4] - minus[7]) + minus[8]
    jz = (minus[2] + minus[5]) - (minus[6] - minus[7]) - minus[8]
    inverse = 1.5 / rho
    ux, uy, uz = jx * inverse, jy * inverse, jz * inverse
    amount = scale(rho)
    base = amount * (1.0 - (2.0 / 3.0) * (ux * ux + uy * uy + uz * uz))
    directions = [ux, uy, uz, ux + uy, ux - uy, ux + uz, ux - uz, uy + uz, uy - uz]
    base_axis, base_diag = base * (1.0 / 18.0), base * (1.0 / 36.0)
    amount_axis, amount_diag = amount * (1.0 / 9.0), amount * (1.0 / 18.0)
    pairs = []
    for k, along in enumerate(directions):
        odd = (amount_axis if k < 3 else amount_diag) * along
        pairs.append(((base_axis if k < 3 else base_diag) + odd * along, odd))
    return base * (1.0 / 3.0), pairs, plus, minus


def collide(f, solid, tau):
    rate = (1.0 - solid) * (1.0 / tau)
    rest, pairs, plus, minus = moments(f, lambda rho: rate * rho)
    keep = 1.0 - rate
    half = 0.5 * keep
    half_odd = half - solid
    out = [keep * f[0] + rest]
    for (even, odd), p, m in zip(pairs, plus, minus):
        symmetric = half * p + even
        antisymmetric = half_odd * m + odd
        out += [symmetric + antisymmetric, symmetric - antisymmetric]
    return out


def restrict(f):
    rest, pairs, _, _ = moments(f, lambda rho: (1.0 - RESCALE) * rho)
    out = [RESCALE * f[0] + rest]
    for k, (even, odd) in enumerate(pairs):
        out += [RESCALE * f[2 * k + 1] + (even + odd), RESCALE * f[2 * k + 2] + (even - odd)]
    return out


def shift_plane(halves, cy, cz):
    lane = lane_ids()
    if cz:
        edge = lane % BX == (0 if cz > 0 else BX - 1)
        halves = [
            jnp.where(
                edge,
                roll_lanes(v, BX * cy + cz - BX * cz),
                roll_lanes(v, BX * cy + cz),
            )
            for v in halves
        ]
    elif cy:
        halves = [roll_lanes(v, BX * cy) for v in halves]
    if cy:
        carried = lane < BX if cy > 0 else lane >= LANES - BX
        halves = [
            jnp.where(carried, halves[1], halves[0]),
            jnp.where(carried, halves[0], halves[1]),
        ]
    return halves


def shift_ring(tiles, cx):
    if not cx:
        return tiles
    row = row_ids()
    turned = [roll_rows(t, cx) for t in tiles]
    if len(tiles) == 1:
        return turned
    edge = row == (0 if cx > 0 else ROWS - 1)
    n = len(tiles)
    return [jnp.where(edge, turned[(i - cx) % n], turned[i]) for i in range(n)]


def move_in_planes(halves):
    moved = [
        shift_plane([halves[0][i], halves[1][i]], int(VEL[i, 1]), int(VEL[i, 2]))
        for i in range(NPOP)
    ]
    return [[moved[i][h] for i in range(NPOP)] for h in range(2)]


def move_along(ring):
    out = [[[], []] for _ in ring]
    for h in range(2):
        for i in range(NPOP):
            for t, v in enumerate(shift_ring([tile[h][i] for tile in ring], int(VEL[i, 0]))):
                out[t][h].append(v)
    return out


def merge(mask, first, second):
    return [
        [jnp.where(mask, v, w) for v, w in zip(a, b)] for a, b in zip(first, second)
    ]


def means():
    shape = (2 * LANES, LANES)
    fine = lax.broadcasted_iota(jnp.int32, shape, 0)
    place = lax.broadcasted_iota(jnp.int32, shape, 1)
    same = (fine // (2 * BX) == place // BX) & (fine % BX // 2 == place % 8)
    return jnp.where(same, 0.125, 0.0).astype(jnp.bfloat16)


def squeeze(planes, matrix):
    cells = jnp.concatenate([jnp.concatenate(halves, axis=1) for halves in planes], axis=0)
    found = None
    for _ in range(3):
        part = cells.astype(jnp.bfloat16)
        product = jnp.dot(part, matrix, preferred_element_type=jnp.float32)
        found = product if found is None else found + product
        cells = cells - part.astype(jnp.float32)
    return [found[ROWS * k : ROWS * (k + 1)] for k in range(len(planes))]


INNER_TILES = (NPOP + 1) // 2 - 2


def fold(tiles):
    out = list(tiles[:INNER_TILES])
    for m in range(6):
        extra, at = tiles[INNER_TILES + m // 3], 2 * (m % 3)
        out[m] = pick(((0,), roll_rows(extra, -1 - at)), ((7,), roll_rows(extra, 5 - at)), (out[m],))
    return out


def unfold(tile, j):
    if j < INNER_TILES:
        return tile(j)
    rows = []
    for m in range(3):
        v = tile(3 * (j - INNER_TILES) + m)
        rows += [((1 + 2 * m,), roll_rows(v, 1 + 2 * m)), ((2 + 2 * m,), roll_rows(v, 2 * m - 5))]
    return pick(*rows, (rows[-1][1],))


def lower():
    return lane_ids() % BX < 8


def pair_up(first, second):
    return first if second is None else jnp.where(lower(), first, second)


def spread(first, second, which):
    if which:
        return jnp.where(lower(), roll_lanes(first, -8), second)
    return jnp.where(lower(), first, roll_lanes(second, 8))


def filled(chosen, h, sources):
    low, high = (sum(chosen[2 * h + z, s] for s in sources) for z in range(2))
    return jnp.where(lower(), low, high) > 0.5


def choose(chosen, quadrant, tiles):
    (_, out), *rest = tiles
    for s, tile in rest:
        out = jnp.where(chosen[quadrant, s] > 0.5, tile, out)
    return out


def half_lanes(h):
    return pl.ds(h * LANES, LANES)


FORWARD = [i for i in range(NPOP) if VEL[i, 0] > 0]
LEVEL = [i for i in range(NPOP) if VEL[i, 0] == 0]
BACKWARD = [i for i in range(NPOP) if VEL[i, 0] < 0]
MOVING = len(FORWARD)

PAIRS = (len(LEVEL) + 1) // 2
WORDS = MOVING + PAIRS


def pick(*choices):
    row = row_ids()
    out = choices[-1][-1]
    for rows, tile in choices[-2::-1]:
        mask = row == rows[0]
        for r in rows[1:]:
            mask = mask | (row == r)
        out = jnp.where(mask, tile, out)
    return out


def pack_message(message, first, second, rim, up):
    for k, i in enumerate(FORWARD if up else BACKWARD):
        f, s = [first(i, h) for h in range(2)], [second(i, h) for h in range(2)]
        s = [v + roll_rows(v, -1) for v in s]
        if up:
            message[k] = pick(
                ((7, 0), roll_rows(f[0], 1)),
                ((1, 2), roll_rows(f[1], 3)),
                ((3,), roll_rows(s[0], -2)),
                ((5,), s[1]),
                ((4,), rim[k]),
                (roll_rows(rim[k], -2),),
            )
        else:
            message[k] = pick(
                ((3, 4), roll_rows(f[0], 3)),
                ((5, 6), roll_rows(f[1], 5)),
                ((7,), roll_rows(s[0], -2)),
                ((1,), s[1]),
                ((0,), roll_rows(rim[k], -3)),
                (roll_rows(rim[k], 3),),
            )
    for k in range(PAIRS):
        shared = []
        for i in (LEVEL + [NPOP])[2 * k : 2 * k + 2]:
            f = [first(i, h) for h in range(2)]
            if up:
                if i < NPOP:
                    s = [roll_rows(second(i, 0), -3), roll_rows(second(i, 1), -1)]
                else:
                    s = [roll_rows(rim[MOVING], -1), roll_rows(rim[MOVING], 5)]
                shared.append(pick(((7,), f[0]), ((1,), roll_rows(f[1], 2)), ((3,), s[0]), (s[1],)))
            else:
                if i < NPOP:
                    s = [roll_rows(second(i, 0), -1), roll_rows(second(i, 1), 1)]
                else:
                    s = [roll_rows(rim[MOVING], -3), roll_rows(rim[MOVING], 3)]
                shared.append(
                    pick(((4,), roll_rows(f[0], 4)), ((6,), roll_rows(f[1], -2)), ((0,), s[0]), (s[1],))
                )
        own_rows = (1, 3, 5, 7) if up else (0, 2, 4, 6)
        message[MOVING + k] = pick((own_rows, shared[0]), (roll_rows(shared[1], 1),))


def shared_tile(message, i):
    k = (LEVEL + [NPOP]).index(i)
    return roll_rows(message[MOVING + k // 2], -(k % 2))


def rim_row(message, k, h, up):
    index, row = (k, 0) if k < MOVING else (WORDS - 1, 1)
    row = 4 + 2 * h if up else row + 2 * h
    return jnp.broadcast_to(message[index, pl.ds(row, 1), :], TILE)


def pack_kernel(
    fine, solid, coarse, coarse_solid, slot, moved, second, high, low, center, shade, slot_out, strip, rim, sem
):
    planes = fine.shape[2]
    last = coarse.shape[2] - 1

    def bring(source, target, which):
        pltpu.make_async_copy(source, target, sem.at[which]).start()

    def arrive(target, which):
        pltpu.make_async_copy(target, target, sem.at[which]).wait()

    ends = ((0, 0), (planes - 4, 4))
    for half in (pl.ds(0, 7), pl.ds(7, 6), pl.ds(13, 6)):
        for first, row in ends:
            bring(fine.at[0, half, pl.ds(first, 4), :], strip.at[half, pl.ds(row, 4), :], 0)
    bring(solid.at[0], shade, 0)
    for plane, row in ((last, 0), (0, 3)):
        bring(coarse.at[0, :, pl.ds(plane, 1), :], rim.at[pl.ds(0, NPOP), pl.ds(row, 1), :], 1)
        bring(coarse_solid.at[0, pl.ds(plane, 1), :], rim.at[NPOP, pl.ds(row, 1), :], 1)
    bring(slot, slot_out, 2)
    for first, row in ((4, 4), (8, 0)):
        bring(fine.at[0, :, pl.ds(first, 4), :], center.at[:, pl.ds(row, 4), :], 3)
    arrive(strip, 0)
    upper = row_ids() < 4
    solids = [
        jnp.where(upper, shade[pl.ds(0, ROWS), half_lanes(h)], shade[pl.ds(planes - ROWS, ROWS), half_lanes(h)])
        for h in range(2)
    ]
    once = move_in_planes(
        [collide([strip[i, :, half_lanes(h)] for i in range(NPOP)], solids[h], TAU_FINE) for h in range(2)]
    )
    arrive(slot_out, 2)
    arrive(rim.at[:, pl.ds(0, 2), :], 1)

    def rim_tile(i):
        v = [rim[i, :, half_lanes(h)] for h in range(2)]
        return pick(((0,), v[1]), ((3,), v[0]), ((4,), roll_rows(v[0], 4)), (roll_rows(v[1], 4),))

    s = rim_tile(NPOP)
    outer = collide([rim_tile(i) for i in range(NPOP)], s, TAU_COARSE) + [s]
    ring = move_along([once])[0]
    twice = [collide(ring[h], solids[h], TAU_FINE) for h in range(2)]
    for h in range(2):
        for i in range(NPOP):
            moved[i, h] = once[h][i]
            second[i, h] = twice[h][i]
        moved[NPOP, h] = solids[h]

    def first_of(i, h):
        return moved[i, h]

    def second_of(i, h):
        return second[i, h]

    pack_message(high, first_of, second_of, [outer[i] for i in FORWARD + [NPOP]], True)
    high[WORDS] = jnp.zeros(TILE, jnp.float32)
    pack_message(low, first_of, second_of, [outer[i] for i in BACKWARD + [NPOP]], False)
    arrive(center, 3)


def inner_steps(center, solid, moved, inner, packed):
    upper = row_ids() < 4
    solids = [
        [solid[pl.ds(ROWS * t, ROWS), half_lanes(h)] for h in range(2)] for t in range(2)
    ]
    outer = [[moved[i, h] for i in range(NPOP)] for h in range(2)]
    between = move_in_planes(
        [
            collide(
                [center[i, :, half_lanes(h)] for i in range(NPOP)],
                jnp.where(upper, solids[1][h], solids[0][h]),
                TAU_FINE,
            )
            for h in range(2)
        ]
    )
    ring = move_along([merge(upper, outer, between), merge(upper, between, outer)])
    for t in range(2):
        for h in range(2):
            ring[t][h] = collide(ring[t][h], solids[t][h], TAU_FINE)
        ring[t] = move_in_planes(ring[t])
    ring = move_along(ring)
    for i in range(NPOP):
        for h in range(2):
            for t in range(2):
                inner[i, h, pl.ds(ROWS * t, ROWS), :] = ring[t][h][i]
    sums = [
        [
            inner[i, h, pl.ds(0, ROWS, stride=2), :] + inner[i, h, pl.ds(1, ROWS, stride=2), :]
            for h in range(2)
        ]
        for i in range(NPOP)
    ]
    out = restrict(squeeze(sums, means())) + [None]
    pairs = [pair_up(out[2 * j], out[2 * j + 1]) for j in range((NPOP + 1) // 2)]
    for j, tile in enumerate(fold(pairs)):
        packed[j] = tile


def starts_early():
    return lax.axis_index("blk") == 0


def prepare(slot, chosen, matrix):
    groups = chosen.shape[1]
    matrix[...] = means()
    me = lax.axis_index("grp")
    codes = slot[...].reshape(1, groups)
    group_ids = lax.broadcasted_iota(jnp.int32, codes.shape, 1)
    for s in range(groups):
        code = jnp.sum(jnp.where(group_ids == me ^ s, codes, 0), axis=1, keepdims=True)
        for q in range(4):
            chosen[q, s] = jnp.where(lane_ids() * 0 + (4 * me + q) == code, 1.0, 0.0)


def early_kernel(center, solid, moved, slot, low, inner, packed, chosen, matrix, low_out):
    low_out[...] = low[...]

    @pl.when(starts_early())
    def _():
        inner_steps(center, solid, moved, inner, packed)
        prepare(slot, chosen, matrix)


def inner_kernel(center, solid, moved, slot, *refs):
    *refs, padded = refs
    done, (inner, packed, chosen, matrix) = refs[:4], refs[4:]

    @pl.when(starts_early())
    def _():
        for source, target in zip(done, (inner, packed, chosen, matrix)):
            target[...] = source[...]

    @pl.when(jnp.logical_not(starts_early()))
    def _():
        inner_steps(center, solid, moved, inner, packed)
        prepare(slot, chosen, matrix)

    size = packed.shape[0]
    padded[pl.ds(0, size)] = packed[...]
    padded[size] = jnp.zeros(TILE, jnp.float32)


def edge_kernel(moved, second, below, above, matrix, coarse, coarse_solid, edges, packed):
    row = row_ids()

    def middle(i):
        v = [moved[i, h] for h in range(2)]
        if i in FORWARD:
            return pick(
                ((3, 4), roll_rows(v[0], -3)),
                ((5, 6), roll_rows(v[1], -1)),
                (below[FORWARD.index(i)],),
            )
        if i in BACKWARD:
            return pick(
                ((7, 0), roll_rows(v[0], -1)),
                ((1, 2), roll_rows(v[1], 1)),
                (above[BACKWARD.index(i)],),
            )
        return pick(
            ((0,), v[0]),
            ((2,), roll_rows(v[1], 2)),
            ((3,), roll_rows(v[0], 4)),
            ((5,), roll_rows(v[1], -2)),
            ((1, 7), shared_tile(below, i)),
            (shared_tile(above, i),),
        )

    twice = collide([middle(i) for i in range(NPOP)], middle(NPOP), TAU_FINE)
    nothing = jnp.zeros(TILE, jnp.float32)
    both = [[], []]
    for h in range(2):
        for i in range(NPOP):
            cx = int(VEL[i, 0])
            v, mine = roll_rows(twice[i], cx - 2 * h), second[i, h]
            if cx > 0:
                v = pick(
                    ((0, 1, 4, 5), v),
                    ((2, 3), roll_rows(mine, -3)),
                    ((7,), nothing),
                    (roll_rows(below[FORWARD.index(i)], 3 - 2 * h),),
                )
            elif cx < 0:
                v = pick(
                    ((2, 3, 6, 7), v),
                    ((0, 1), roll_rows(mine, -1)),
                    ((5,), nothing),
                    (roll_rows(above[BACKWARD.index(i)], -3 - 2 * h),),
                )
            else:
                v = pick(
                    ((0, 3, 4, 7), v),
                    ((1,), mine),
                    ((2,), roll_rows(mine, 4)),
                    ((6,), roll_rows(shared_tile(below, i), 3 - 2 * h)),
                    (roll_rows(shared_tile(above, i), -3 - 2 * h),),
                )
            both[h].append(v)
    both = move_in_planes(both)
    sums = [[v + roll_rows(v, -1) for v in half] + [None] for half in both]
    odd = row % 2 == 1
    pairs = [
        [half[i] if half[i + 1] is None else jnp.where(odd, roll_rows(half[i + 1], 1), half[i]) for half in sums]
        for i in range(0, NPOP, 2)
    ]
    mean = []
    for pair in squeeze(pairs, matrix[...]):
        mean += [pair, roll_rows(pair, -1)]
    out = restrict(mean[:NPOP]) + [None]
    pairs = [
        out[i] if out[i + 1] is None else jnp.where(odd, roll_rows(out[i + 1], 1), out[i])
        for i in range(0, NPOP, 2)
    ]
    for j in range(len(pairs) // 2):
        packed[j] = pair_up(pairs[2 * j], pairs[2 * j + 1])
    for i in range(NPOP):
        for h in range(2):
            edges[i, h] = both[h][i]


def write_kernel(inner, edges, out):
    row = row_ids()
    for i in range(NPOP):
        for h in range(2):
            edge = edges[i, h]
            out[0, i, pl.ds(0, ROWS), half_lanes(h)] = jnp.where(
                row < 2, edge, inner[i, h, pl.ds(0, ROWS), :]
            )
            out[0, i, pl.ds(ROWS, ROWS), half_lanes(h)] = jnp.where(
                row >= 6, roll_rows(edge, 4), inner[i, h, pl.ds(ROWS, ROWS), :]
            )


def split_kernel(after, tiles, first, second):
    half = first.shape[0]
    first[...] = tiles[pl.ds(0, half)]
    second[...] = tiles[pl.ds(half, half)]


def paste_inner(chosen, sources, tile, base, out):
    masks = [filled(chosen, h, sources) for h in range(2)]
    for j in range((NPOP + 1) // 2):
        tiles = [(s, tile(s, j)) for s in sources]
        for h in range(2):
            low, high = (choose(chosen, 2 * h + z, tiles) for z in range(2))
            for i in range(2 * j, min(2 * j + 2, NPOP)):
                out(i, h, jnp.where(masks[h], spread(low, high, i % 2), base(i, h)))


def paste_kernel(after, coarse, solid, chosen, below, above, *refs):
    *packed, out, ends = refs
    sources = [1, *range(0, chosen.shape[1], 2)]
    parts = dict(zip(sources, packed))

    def write(i, h, tile):
        out[i, h] = tile

    paste_inner(
        chosen, sources, lambda s, j: unfold(lambda k: parts[s][k], j), lambda i, h: coarse[0, i, :, half_lanes(h)], write
    )
    for i in range(NPOP + 1):
        v = [coarse[0, i, :, half_lanes(h)] if i < NPOP else solid[0, :, half_lanes(h)] for h in range(2)]
        tile = pick(((0,), v[0]), ((1,), roll_rows(v[1], 1)), ((2,), roll_rows(v[0], 3)), (roll_rows(v[1], 4),))
        if i == NPOP:
            tile = pick(
                ((4,), rim_row(above, MOVING, 0, False)),
                ((5,), rim_row(above, MOVING, 1, False)),
                ((6,), rim_row(below, MOVING, 0, True)),
                ((7,), rim_row(below, MOVING, 1, True)),
                (tile,),
            )
        ends[i] = tile


def coarse_kernel(after, base, solid, chosen, *refs):
    relayed, out = refs[:-1], refs[-1]
    sources = [2 * k + 3 for k in range(len(relayed) // 2)]
    f = [[None] * NPOP, [None] * NPOP]

    def write(i, h, tile):
        f[h][i] = tile

    half = relayed[0].shape[0]

    def tile(s, j):
        return unfold(lambda k: relayed[s - 3 + k // half][k % half], j)

    paste_inner(chosen, sources, tile, lambda i, h: base[i, h], write)
    f = move_in_planes([collide(f[h], solid[0, :, half_lanes(h)], TAU_COARSE) for h in range(2)])
    for h in range(2):
        for i in range(NPOP):
            out[i, h] = f[h][i]


CHUNKS = (0, 3, 6, 9, 12, 15, 17, NPOP)


def last_kernel(chosen, below, above, base, middle, *refs):
    *packed, result, out, sem = refs
    sources = [0, *others(len(packed))]
    row, lane = row_ids(), lane_ids()
    odd = row % 2 == 1
    pasted = [filled(chosen, h, sources) for h in range(2)]
    pasted = (odd & pasted[1]) | (~odd & pasted[0])
    f = []
    for j in range((NPOP + 1) // 4):
        tiles = [(s, part[j]) for s, part in zip(sources, packed)]
        quadrants = [choose(chosen, q, tiles) for q in range(4)]
        for which in range(2):
            v = [spread(quadrants[2 * h], quadrants[2 * h + 1], which) for h in range(2)]
            f.append(jnp.where(odd, roll_rows(v[1], 1), v[0]))
            f.append(jnp.where(odd, v[1], roll_rows(v[0], -1)))
    f = [jnp.where(pasted, f[i], base[i]) for i in range(NPOP)]
    f = collide(f, base[NPOP], TAU_COARSE)
    copied = 0
    for i in range(NPOP):
        cx, cy, cz = (int(c) for c in VEL[i])
        v = f[i]
        if cx:
            k = (FORWARD if cx > 0 else BACKWARD).index(i)
            rim = [rim_row(below if cx > 0 else above, k, h, cx > 0) for h in range(2)]
            at = row >= 6 if cx > 0 else (row == 4) | (row == 5)
            v = jnp.where(at & ~pasted, jnp.where(odd, rim[1], rim[0]), v)
        if cz:
            edge = lane % BX == (0 if cz > 0 else BX - 1)
            v = jnp.where(
                edge, roll_lanes(v, BX * cy + cz - BX * cz), roll_lanes(v, BX * cy + cz)
            )
        elif cy:
            v = roll_lanes(v, BX * cy)
        if cy:
            carried = lane < BX if cy > 0 else lane >= LANES - BX
            v = jnp.where(carried, jnp.where(odd, roll_rows(v, 1), roll_rows(v, -1)), v)
        for h in range(2):
            inside = middle[i, h]
            if cx > 0:
                tile = pick(
                    ((0,), roll_rows(v, 2 - h)), ((1,), roll_rows(v, 1 - h)), (roll_rows(inside, 1),)
                )
            elif cx < 0:
                tile = pick(
                    ((7,), roll_rows(v, 3 - h)), ((6,), roll_rows(v, 4 - h)), (roll_rows(inside, -1),)
                )
            else:
                tile = pick(((0,), roll_rows(v, -h)), ((7,), roll_rows(v, 5 - h)), (inside,))
            out[0, i, :, half_lanes(h)] = tile
        if i + 1 in CHUNKS:
            some = pl.ds(copied, i + 1 - copied)
            pltpu.make_async_copy(out.at[0, some], result.at[0, some], sem).start()
            copied = i + 1
    pltpu.make_async_copy(out, result, sem).wait()


def others(groups):
    return range(1, groups)


def exchange(array, distance):
    groups = lax.axis_size("grp")
    return lax.ppermute(array, "grp", [(i, i ^ distance) for i in range(groups)])


def held(array):
    return pltpu.with_memory_space_constraint(array, VMEM)


def left(array):
    return pltpu.with_memory_space_constraint(array, pltpu.HBM)


def in_vmem(*shape):
    return VMEM(shape, jnp.float32)


def call(kernel, args, specs, outs, scratch=(), flops=0, name=None, out_space=VMEM):
    single = not isinstance(outs, (list, tuple))
    outs = [outs] if single else list(outs)
    result = pl.pallas_call(
        kernel,
        in_specs=[pl.BlockSpec(memory_space=s) for s in specs],
        out_specs=[pl.BlockSpec(memory_space=out_space)] * len(outs),
        out_shape=outs,
        scratch_shapes=list(scratch),
        compiler_params=pltpu.CompilerParams(vmem_limit_bytes=24 << 20),
        cost_estimate=pl.CostEstimate(flops=flops, bytes_accessed=1, transcendentals=0),
        name=name,
    )(*args)
    return result[0] if single else result


def per_device(fine_pops, fine_solid, coarse_pops, coarse_solid, coarse_slot):
    groups = lax.axis_size("grp")
    blocks = lax.axis_size("blk")
    moved, second, high, low, center, shade, slot = call(
        pack_kernel,
        tuple(map(left, (fine_pops, fine_solid, coarse_pops, coarse_solid, coarse_slot))),
        [pl.ANY] * 5,
        [
            in_vmem(NPOP + 1, 2, *TILE),
            in_vmem(NPOP, 2, *TILE),
            in_vmem(WORDS + 1, *TILE),
            in_vmem(WORDS, *TILE),
            in_vmem(NPOP, ROWS, 2 * LANES),
            in_vmem(*fine_solid.shape[1:]),
            VMEM((groups,), jnp.int32),
        ],
        [
            in_vmem(NPOP + 2, ROWS, 2 * LANES),
            in_vmem(NPOP + 1, ROWS, 2 * LANES),
            pltpu.SemaphoreType.DMA((4,)),
        ],
        name="pack",
    )
    coarse_v, coarse_solid_v = held(coarse_pops), held(coarse_solid)
    inner_shapes = [
        in_vmem(NPOP, 2, 2 * ROWS, LANES),
        in_vmem(INNER_TILES, *TILE),
        in_vmem(4, groups, *TILE),
        VMEM((2 * LANES, LANES), jnp.bfloat16),
    ]
    inner_args = (held(center), held(shade), held(moved), held(slot))
    *done, low = call(
        early_kernel,
        (*inner_args, held(low)),
        [VMEM] * 5,
        [*inner_shapes, in_vmem(WORDS, *TILE)],
        name="early",
    )
    forward = [(i, (i + 1) % blocks) for i in range(blocks)]
    backward = [(i, (i - 1) % blocks) for i in range(blocks)]
    below = lax.ppermute(high, "blk", forward)
    above = lax.ppermute(low, "blk", backward)
    inner, packed_inner, chosen, matrix, padded_inner = call(
        inner_kernel,
        (*inner_args, *map(held, done)),
        [VMEM] * 8,
        [*inner_shapes, in_vmem(INNER_TILES + 1, *TILE)],
        name="inner",
    )

    across = [exchange(packed_inner, s) for s in range(2, groups, 2)]
    beside = exchange(padded_inner, 1)
    edges, packed_edges = call(
        edge_kernel,
        (held(moved), held(second), held(below), held(above), held(matrix), coarse_v, coarse_solid_v),
        [VMEM] * 7,
        [in_vmem(NPOP, 2, *TILE), in_vmem((NPOP + 1) // 4, *TILE)],
        name="edge",
    )
    edge_parts = [packed_edges] + [exchange(packed_edges, s) for s in others(groups)]
    fine_out = call(
        write_kernel,
        (held(inner), held(edges)),
        [VMEM] * 2,
        jax.ShapeDtypeStruct(fine_pops.shape, jnp.float32),
        name="write",
    )
    inner_parts = [beside, packed_inner, *across]
    base, ends = call(
        paste_kernel,
        (
            held(edges),
            coarse_v,
            coarse_solid_v,
            held(chosen),
            held(below),
            held(above),
            *map(held, inner_parts),
        ),
        [VMEM] * (6 + len(inner_parts)),
        [in_vmem(NPOP, 2, *TILE), in_vmem(NPOP + 1, *TILE)],
        name="paste",
    )
    relayed = []
    for part in across:
        halves = call(
            split_kernel,
            (held(base), held(part)),
            [VMEM] * 2,
            [in_vmem(part.shape[0] // 2, *TILE)] * 2,
            name="split",
        )
        relayed += [exchange(half, 1) for half in halves]
    middle = call(
        coarse_kernel,
        (left(fine_out), held(base), coarse_solid_v, held(chosen), *map(held, relayed)),
        [pl.ANY] + [VMEM] * (3 + len(relayed)),
        in_vmem(NPOP, 2, *TILE),
        name="coarse",
    )
    coarse_out = call(
        last_kernel,
        (held(chosen), held(below), held(above), held(ends), held(middle), *map(held, edge_parts)),
        [VMEM] * (5 + len(edge_parts)),
        jax.ShapeDtypeStruct(coarse_pops.shape, jnp.float32),
        [in_vmem(*coarse_pops.shape), pltpu.SemaphoreType.DMA],
        out_space=pl.ANY,
        name="last",
    )
    return fine_out, coarse_out


def solution(mesh):
    placed = (
        P("grp", None, "blk", None),
        P("grp", "blk", None),
        P("grp", None, "blk", None),
        P("grp", "blk", None),
        P(),
    )
    return jax.shard_map(
        per_device,
        mesh=mesh,
        in_specs=placed,
        out_specs=(P("grp", None, "blk", None), P("grp", None, "blk", None)),
        check_vma=False,
    )
```

```python
import jax
import jax.numpy as jnp
import numpy as np
from jax import lax
from jax.experimental import pallas as pl
from jax.experimental.pallas import tpu as pltpu
from jax.sharding import PartitionSpec as P

VEL = np.array(
    [
        [0, 0, 0],
        [1, 0, 0],
        [-1, 0, 0],
        [0, 1, 0],
        [0, -1, 0],
        [0, 0, 1],
        [0, 0, -1],
        [1, 1, 0],
        [-1, -1, 0],
        [1, -1, 0],
        [-1, 1, 0],
        [1, 0, 1],
        [-1, 0, -1],
        [1, 0, -1],
        [-1, 0, 1],
        [0, 1, 1],
        [0, -1, -1],
        [0, 1, -1],
        [0, -1, 1],
    ]
)
NPOP = 19
BX = 16
TAU_FINE = 0.6
TAU_COARSE = 0.55
RESCALE = 2.0 * TAU_COARSE / TAU_FINE

ROWS, LANES = 8, 128
TILE = (ROWS, LANES)
VMEM = pltpu.VMEM


def row_ids():
    return lax.broadcasted_iota(jnp.int32, TILE, 0)


def lane_ids():
    return lax.broadcasted_iota(jnp.int32, TILE, 1)


def roll_rows(tile, shift):
    return pltpu.roll(tile, shift % ROWS, 0)


def roll_lanes(tile, shift):
    return pltpu.roll(tile, shift % LANES, 1)


def moments(f, scale):
    minus = [f[i] - f[i + 1] for i in range(1, NPOP, 2)]
    plus = [f[i] + f[i + 1] for i in range(1, NPOP, 2)]
    rho = ((f[0] + plus[0]) + (plus[1] + plus[2])) + (
        (plus[3] + plus[4]) + (plus[5] + plus[6])
    ) + (plus[7] + plus[8])
    jx = (minus[0] + minus[3]) + (minus[4] + minus[5]) + minus[6]
    jy = (minus[1] + minus[3]) - (minus[4] - minus[7]) + minus[8]
    jz = (minus[2] + minus[5]) - (minus[6] - minus[7]) - minus[8]
    inverse = 1.5 / rho
    ux, uy, uz = jx * inverse, jy * inverse, jz * inverse
    amount = scale(rho)
    base = amount * (1.0 - (2.0 / 3.0) * (ux * ux + uy * uy + uz * uz))
    directions = [ux, uy, uz, ux + uy, ux - uy, ux + uz, ux - uz, uy + uz, uy - uz]
    base_axis, base_diag = base * (1.0 / 18.0), base * (1.0 / 36.0)
    amount_axis, amount_diag = amount * (1.0 / 9.0), amount * (1.0 / 18.0)
    pairs = []
    for k, along in enumerate(directions):
        odd = (amount_axis if k < 3 else amount_diag) * along
        pairs.append(((base_axis if k < 3 else base_diag) + odd * along, odd))
    return base * (1.0 / 3.0), pairs, plus, minus


def collide(f, solid, tau):
    rate = (1.0 - solid) * (1.0 / tau)
    rest, pairs, plus, minus = moments(f, lambda rho: rate * rho)
    keep = 1.0 - rate
    half = 0.5 * keep
    half_odd = half - solid
    out = [keep * f[0] + rest]
    for (even, odd), p, m in zip(pairs, plus, minus):
        symmetric = half * p + even
        antisymmetric = half_odd * m + odd
        out += [symmetric + antisymmetric, symmetric - antisymmetric]
    return out


def restrict(f):
    rest, pairs, _, _ = moments(f, lambda rho: (1.0 - RESCALE) * rho)
    out = [RESCALE * f[0] + rest]
    for k, (even, odd) in enumerate(pairs):
        out += [RESCALE * f[2 * k + 1] + (even + odd), RESCALE * f[2 * k + 2] + (even - odd)]
    return out


def shift_plane(halves, cy, cz):
    lane = lane_ids()
    if cz:
        edge = lane % BX == (0 if cz > 0 else BX - 1)
        halves = [
            jnp.where(
                edge,
                roll_lanes(v, BX * cy + cz - BX * cz),
                roll_lanes(v, BX * cy + cz),
            )
            for v in halves
        ]
    elif cy:
        halves = [roll_lanes(v, BX * cy) for v in halves]
    if cy:
        carried = lane < BX if cy > 0 else lane >= LANES - BX
        halves = [
            jnp.where(carried, halves[1], halves[0]),
            jnp.where(carried, halves[0], halves[1]),
        ]
    return halves


def shift_ring(tiles, cx):
    if not cx:
        return tiles
    row = row_ids()
    turned = [roll_rows(t, cx) for t in tiles]
    if len(tiles) == 1:
        return turned
    edge = row == (0 if cx > 0 else ROWS - 1)
    n = len(tiles)
    return [jnp.where(edge, turned[(i - cx) % n], turned[i]) for i in range(n)]


def move_in_planes(halves):
    moved = [
        shift_plane([halves[0][i], halves[1][i]], int(VEL[i, 1]), int(VEL[i, 2]))
        for i in range(NPOP)
    ]
    return [[moved[i][h] for i in range(NPOP)] for h in range(2)]


def move_along(ring):
    out = [[[], []] for _ in ring]
    for h in range(2):
        for i in range(NPOP):
            for t, v in enumerate(shift_ring([tile[h][i] for tile in ring], int(VEL[i, 0]))):
                out[t][h].append(v)
    return out


def merge(mask, first, second):
    return [
        [jnp.where(mask, v, w) for v, w in zip(a, b)] for a, b in zip(first, second)
    ]


def means():
    shape = (2 * LANES, LANES)
    fine = lax.broadcasted_iota(jnp.int32, shape, 0)
    place = lax.broadcasted_iota(jnp.int32, shape, 1)
    same = (fine // (2 * BX) == place // BX) & (fine % BX // 2 == place % 8)
    return jnp.where(same, 0.125, 0.0).astype(jnp.bfloat16)


def squeeze(planes, matrix):
    cells = jnp.concatenate([jnp.concatenate(halves, axis=1) for halves in planes], axis=0)
    found = None
    for _ in range(3):
        part = cells.astype(jnp.bfloat16)
        product = jnp.dot(part, matrix, preferred_element_type=jnp.float32)
        found = product if found is None else found + product
        cells = cells - part.astype(jnp.float32)
    return [found[ROWS * k : ROWS * (k + 1)] for k in range(len(planes))]


INNER_TILES = (NPOP + 1) // 2 - 2


def fold(tiles):
    out = list(tiles[:INNER_TILES])
    for m in range(6):
        extra, at = tiles[INNER_TILES + m // 3], 2 * (m % 3)
        out[m] = pick(((0,), roll_rows(extra, -1 - at)), ((7,), roll_rows(extra, 5 - at)), (out[m],))
    return out


def unfold(tile, j):
    if j < INNER_TILES:
        return tile(j)
    rows = []
    for m in range(3):
        v = tile(3 * (j - INNER_TILES) + m)
        rows += [((1 + 2 * m,), roll_rows(v, 1 + 2 * m)), ((2 + 2 * m,), roll_rows(v, 2 * m - 5))]
    return pick(*rows, (rows[-1][1],))


def lower():
    return lane_ids() % BX < 8


def pair_up(first, second):
    return first if second is None else jnp.where(lower(), first, second)


def spread(first, second, which):
    if which:
        return jnp.where(lower(), roll_lanes(first, -8), second)
    return jnp.where(lower(), first, roll_lanes(second, 8))


def filled(chosen, h, sources):
    low, high = (sum(chosen[2 * h + z, s] for s in sources) for z in range(2))
    return jnp.where(lower(), low, high) > 0.5


def choose(chosen, quadrant, tiles):
    (_, out), *rest = tiles
    for s, tile in rest:
        out = jnp.where(chosen[quadrant, s] > 0.5, tile, out)
    return out


def half_lanes(h):
    return pl.ds(h * LANES, LANES)


FORWARD = [i for i in range(NPOP) if VEL[i, 0] > 0]
LEVEL = [i for i in range(NPOP) if VEL[i, 0] == 0]
BACKWARD = [i for i in range(NPOP) if VEL[i, 0] < 0]
MOVING = len(FORWARD)

PAIRS = (len(LEVEL) + 1) // 2
WORDS = MOVING + PAIRS


def pick(*choices):
    row = row_ids()
    out = choices[-1][-1]
    for rows, tile in choices[-2::-1]:
        mask = row == rows[0]
        for r in rows[1:]:
            mask = mask | (row == r)
        out = jnp.where(mask, tile, out)
    return out


def pack_message(message, first, second, rim, up):
    for k, i in enumerate(FORWARD if up else BACKWARD):
        f, s = [first(i, h) for h in range(2)], [second(i, h) for h in range(2)]
        s = [v + roll_rows(v, -1) for v in s]
        if up:
            message[k] = pick(
                ((7, 0), roll_rows(f[0], 1)),
                ((1, 2), roll_rows(f[1], 3)),
                ((3,), roll_rows(s[0], -2)),
                ((5,), s[1]),
                ((4,), rim[k]),
                (roll_rows(rim[k], -2),),
            )
        else:
            message[k] = pick(
                ((3, 4), roll_rows(f[0], 3)),
                ((5, 6), roll_rows(f[1], 5)),
                ((7,), roll_rows(s[0], -2)),
                ((1,), s[1]),
                ((0,), roll_rows(rim[k], -3)),
                (roll_rows(rim[k], 3),),
            )
    for k in range(PAIRS):
        shared = []
        for i in (LEVEL + [NPOP])[2 * k : 2 * k + 2]:
            f = [first(i, h) for h in range(2)]
            if up:
                if i < NPOP:
                    s = [roll_rows(second(i, 0), -3), roll_rows(second(i, 1), -1)]
                else:
                    s = [roll_rows(rim[MOVING], -1), roll_rows(rim[MOVING], 5)]
                shared.append(pick(((7,), f[0]), ((1,), roll_rows(f[1], 2)), ((3,), s[0]), (s[1],)))
            else:
                if i < NPOP:
                    s = [roll_rows(second(i, 0), -1), roll_rows(second(i, 1), 1)]
                else:
                    s = [roll_rows(rim[MOVING], -3), roll_rows(rim[MOVING], 3)]
                shared.append(
                    pick(((4,), roll_rows(f[0], 4)), ((6,), roll_rows(f[1], -2)), ((0,), s[0]), (s[1],))
                )
        own_rows = (1, 3, 5, 7) if up else (0, 2, 4, 6)
        message[MOVING + k] = pick((own_rows, shared[0]), (roll_rows(shared[1], 1),))


def shared_tile(message, i):
    k = (LEVEL + [NPOP]).index(i)
    return roll_rows(message[MOVING + k // 2], -(k % 2))


def rim_row(message, k, h, up):
    index, row = (k, 0) if k < MOVING else (WORDS - 1, 1)
    row = 4 + 2 * h if up else row + 2 * h
    return jnp.broadcast_to(message[index, pl.ds(row, 1), :], TILE)


def pack_kernel(
    fine, solid, coarse, coarse_solid, slot, moved, second, high, low, center, shade, slot_out, strip, rim, sem
):
    planes = fine.shape[2]
    last = coarse.shape[2] - 1

    def bring(source, target, which):
        pltpu.make_async_copy(source, target, sem.at[which]).start()

    def arrive(target, which):
        pltpu.make_async_copy(target, target, sem.at[which]).wait()

    ends = ((0, 0), (planes - 4, 4))
    for half in (pl.ds(0, 7), pl.ds(7, 6), pl.ds(13, 6)):
        for first, row in ends:
            bring(fine.at[0, half, pl.ds(first, 4), :], strip.at[half, pl.ds(row, 4), :], 0)
    bring(solid.at[0], shade, 0)
    for plane, row in ((last, 0), (0, 3)):
        bring(coarse.at[0, :, pl.ds(plane, 1), :], rim.at[pl.ds(0, NPOP), pl.ds(row, 1), :], 1)
        bring(coarse_solid.at[0, pl.ds(plane, 1), :], rim.at[NPOP, pl.ds(row, 1), :], 1)
    bring(slot, slot_out, 2)
    for first, row in ((4, 4), (8, 0)):
        bring(fine.at[0, :, pl.ds(first, 4), :], center.at[:, pl.ds(row, 4), :], 3)
    arrive(strip, 0)
    upper = row_ids() < 4
    solids = [
        jnp.where(upper, shade[pl.ds(0, ROWS), half_lanes(h)], shade[pl.ds(planes - ROWS, ROWS), half_lanes(h)])
        for h in range(2)
    ]
    once = move_in_planes(
        [collide([strip[i, :, half_lanes(h)] for i in range(NPOP)], solids[h], TAU_FINE) for h in range(2)]
    )
    arrive(slot_out, 2)
    arrive(rim.at[:, pl.ds(0, 2), :], 1)

    def rim_tile(i):
        v = [rim[i, :, half_lanes(h)] for h in range(2)]
        return pick(((0,), v[1]), ((3,), v[0]), ((4,), roll_rows(v[0], 4)), (roll_rows(v[1], 4),))

    s = rim_tile(NPOP)
    outer = collide([rim_tile(i) for i in range(NPOP)], s, TAU_COARSE) + [s]
    ring = move_along([once])[0]
    twice = [collide(ring[h], solids[h], TAU_FINE) for h in range(2)]
    for h in range(2):
        for i in range(NPOP):
            moved[i, h] = once[h][i]
            second[i, h] = twice[h][i]
        moved[NPOP, h] = solids[h]

    def first_of(i, h):
        return moved[i, h]

    def second_of(i, h):
        return second[i, h]

    pack_message(high, first_of, second_of, [outer[i] for i in FORWARD + [NPOP]], True)
    high[WORDS] = jnp.zeros(TILE, jnp.float32)
    pack_message(low, first_of, second_of, [outer[i] for i in BACKWARD + [NPOP]], False)
    arrive(center, 3)


def inner_steps(center, solid, moved, inner, packed):
    upper = row_ids() < 4
    solids = [
        [solid[pl.ds(ROWS * t, ROWS), half_lanes(h)] for h in range(2)] for t in range(2)
    ]
    outer = [[moved[i, h] for i in range(NPOP)] for h in range(2)]
    between = move_in_planes(
        [
            collide(
                [center[i, :, half_lanes(h)] for i in range(NPOP)],
                jnp.where(upper, solids[1][h], solids[0][h]),
                TAU_FINE,
            )
            for h in range(2)
        ]
    )
    ring = move_along([merge(upper, outer, between), merge(upper, between, outer)])
    for t in range(2):
        for h in range(2):
            ring[t][h] = collide(ring[t][h], solids[t][h], TAU_FINE)
        ring[t] = move_in_planes(ring[t])
    ring = move_along(ring)
    for i in range(NPOP):
        for h in range(2):
            for t in range(2):
                inner[i, h, pl.ds(ROWS * t, ROWS), :] = ring[t][h][i]
    sums = [
        [
            inner[i, h, pl.ds(0, ROWS, stride=2), :] + inner[i, h, pl.ds(1, ROWS, stride=2), :]
            for h in range(2)
        ]
        for i in range(NPOP)
    ]
    out = restrict(squeeze(sums, means())) + [None]
    pairs = [pair_up(out[2 * j], out[2 * j + 1]) for j in range((NPOP + 1) // 2)]
    for j, tile in enumerate(fold(pairs)):
        packed[j] = tile


def starts_early():
    return lax.axis_index("blk") == 0


def prepare(slot, chosen, matrix):
    groups = chosen.shape[1]
    matrix[...] = means()
    me = lax.axis_index("grp")
    codes = slot[...].reshape(1, groups)
    group_ids = lax.broadcasted_iota(jnp.int32, codes.shape, 1)
    for s in range(groups):
        code = jnp.sum(jnp.where(group_ids == me ^ s, codes, 0), axis=1, keepdims=True)
        for q in range(4):
            chosen[q, s] = jnp.where(lane_ids() * 0 + (4 * me + q) == code, 1.0, 0.0)


def early_kernel(center, solid, moved, slot, low, inner, packed, chosen, matrix, low_out):
    low_out[...] = low[...]

    @pl.when(starts_early())
    def _():
        inner_steps(center, solid, moved, inner, packed)
        prepare(slot, chosen, matrix)


def inner_kernel(center, solid, moved, slot, *refs):
    *refs, padded = refs
    done, (inner, packed, chosen, matrix) = refs[:4], refs[4:]

    @pl.when(starts_early())
    def _():
        for source, target in zip(done, (inner, packed, chosen, matrix)):
            target[...] = source[...]

    @pl.when(jnp.logical_not(starts_early()))
    def _():
        inner_steps(center, solid, moved, inner, packed)
        prepare(slot, chosen, matrix)

    size = packed.shape[0]
    padded[pl.ds(0, size)] = packed[...]
    padded[size] = jnp.zeros(TILE, jnp.float32)


def edge_kernel(moved, second, below, above, matrix, coarse, coarse_solid, edges, packed):
    row = row_ids()

    def middle(i):
        v = [moved[i, h] for h in range(2)]
        if i in FORWARD:
            return pick(
                ((3, 4), roll_rows(v[0], -3)),
                ((5, 6), roll_rows(v[1], -1)),
                (below[FORWARD.index(i)],),
            )
        if i in BACKWARD:
            return pick(
                ((7, 0), roll_rows(v[0], -1)),
                ((1, 2), roll_rows(v[1], 1)),
                (above[BACKWARD.index(i)],),
            )
        return pick(
            ((0,), v[0]),
            ((2,), roll_rows(v[1], 2)),
            ((3,), roll_rows(v[0], 4)),
            ((5,), roll_rows(v[1], -2)),
            ((1, 7), shared_tile(below, i)),
            (shared_tile(above, i),),
        )

    twice = collide([middle(i) for i in range(NPOP)], middle(NPOP), TAU_FINE)
    nothing = jnp.zeros(TILE, jnp.float32)
    both = [[], []]
    for h in range(2):
        for i in range(NPOP):
            cx = int(VEL[i, 0])
            v, mine = roll_rows(twice[i], cx - 2 * h), second[i, h]
            if cx > 0:
                v = pick(
                    ((0, 1, 4, 5), v),
                    ((2, 3), roll_rows(mine, -3)),
                    ((7,), nothing),
                    (roll_rows(below[FORWARD.index(i)], 3 - 2 * h),),
                )
            elif cx < 0:
                v = pick(
                    ((2, 3, 6, 7), v),
                    ((0, 1), roll_rows(mine, -1)),
                    ((5,), nothing),
                    (roll_rows(above[BACKWARD.index(i)], -3 - 2 * h),),
                )
            else:
                v = pick(
                    ((0, 3, 4, 7), v),
                    ((1,), mine),
                    ((2,), roll_rows(mine, 4)),
                    ((6,), roll_rows(shared_tile(below, i), 3 - 2 * h)),
                    (roll_rows(shared_tile(above, i), -3 - 2 * h),),
                )
            both[h].append(v)
    both = move_in_planes(both)
    sums = [[v + roll_rows(v, -1) for v in half] + [None] for half in both]
    odd = row % 2 == 1
    pairs = [
        [half[i] if half[i + 1] is None else jnp.where(odd, roll_rows(half[i + 1], 1), half[i]) for half in sums]
        for i in range(0, NPOP, 2)
    ]
    mean = []
    for pair in squeeze(pairs, matrix[...]):
        mean += [pair, roll_rows(pair, -1)]
    out = restrict(mean[:NPOP]) + [None]
    pairs = [
        out[i] if out[i + 1] is None else jnp.where(odd, roll_rows(out[i + 1], 1), out[i])
        for i in range(0, NPOP, 2)
    ]
    for j in range(len(pairs) // 2):
        packed[j] = pair_up(pairs[2 * j], pairs[2 * j + 1])
    for i in range(NPOP):
        for h in range(2):
            edges[i, h] = both[h][i]


def write_kernel(inner, edges, out):
    row = row_ids()
    for i in range(NPOP):
        for h in range(2):
            edge = edges[i, h]
            out[0, i, pl.ds(0, ROWS), half_lanes(h)] = jnp.where(
                row < 2, edge, inner[i, h, pl.ds(0, ROWS), :]
            )
            out[0, i, pl.ds(ROWS, ROWS), half_lanes(h)] = jnp.where(
                row >= 6, roll_rows(edge, 4), inner[i, h, pl.ds(ROWS, ROWS), :]
            )


def split_kernel(after, tiles, first, second):
    half = first.shape[0]
    first[...] = tiles[pl.ds(0, half)]
    second[...] = tiles[pl.ds(half, half)]


def paste_inner(chosen, sources, tile, base, out):
    masks = [filled(chosen, h, sources) for h in range(2)]
    for j in range((NPOP + 1) // 2):
        tiles = [(s, tile(s, j)) for s in sources]
        for h in range(2):
            low, high = (choose(chosen, 2 * h + z, tiles) for z in range(2))
            for i in range(2 * j, min(2 * j + 2, NPOP)):
                out(i, h, jnp.where(masks[h], spread(low, high, i % 2), base(i, h)))


def paste_kernel(after, coarse, solid, chosen, below, above, *refs):
    *packed, out, ends = refs
    sources = [1, *range(0, chosen.shape[1], 2)]
    parts = dict(zip(sources, packed))

    def write(i, h, tile):
        out[i, h] = tile

    paste_inner(
        chosen, sources, lambda s, j: unfold(lambda k: parts[s][k], j), lambda i, h: coarse[0, i, :, half_lanes(h)], write
    )
    for i in range(NPOP + 1):
        v = [coarse[0, i, :, half_lanes(h)] if i < NPOP else solid[0, :, half_lanes(h)] for h in range(2)]
        tile = pick(((0,), v[0]), ((1,), roll_rows(v[1], 1)), ((2,), roll_rows(v[0], 3)), (roll_rows(v[1], 4),))
        if i == NPOP:
            tile = pick(
                ((4,), rim_row(above, MOVING, 0, False)),
                ((5,), rim_row(above, MOVING, 1, False)),
                ((6,), rim_row(below, MOVING, 0, True)),
                ((7,), rim_row(below, MOVING, 1, True)),
                (tile,),
            )
        ends[i] = tile


def coarse_kernel(after, base, solid, chosen, *refs):
    relayed, out = refs[:-1], refs[-1]
    sources = [2 * k + 3 for k in range(len(relayed) // 2)]
    f = [[None] * NPOP, [None] * NPOP]

    def write(i, h, tile):
        f[h][i] = tile

    half = relayed[0].shape[0]

    def tile(s, j):
        return unfold(lambda k: relayed[s - 3 + k // half][k % half], j)

    paste_inner(chosen, sources, tile, lambda i, h: base[i, h], write)
    f = move_in_planes([collide(f[h], solid[0, :, half_lanes(h)], TAU_COARSE) for h in range(2)])
    for h in range(2):
        for i in range(NPOP):
            out[i, h] = f[h][i]


CHUNKS = (0, 3, 6, 9, 12, 15, 17, NPOP)


def last_kernel(chosen, below, above, base, middle, *refs):
    *packed, result, out, sem = refs
    sources = [0, *others(len(packed))]
    row, lane = row_ids(), lane_ids()
    odd = row % 2 == 1
    pasted = [filled(chosen, h, sources) for h in range(2)]
    pasted = (odd & pasted[1]) | (~odd & pasted[0])
    f = []
    for j in range((NPOP + 1) // 4):
        tiles = [(s, part[j]) for s, part in zip(sources, packed)]
        quadrants = [choose(chosen, q, tiles) for q in range(4)]
        for which in range(2):
            v = [spread(quadrants[2 * h], quadrants[2 * h + 1], which) for h in range(2)]
            f.append(jnp.where(odd, roll_rows(v[1], 1), v[0]))
            f.append(jnp.where(odd, v[1], roll_rows(v[0], -1)))
    f = [jnp.where(pasted, f[i], base[i]) for i in range(NPOP)]
    f = collide(f, base[NPOP], TAU_COARSE)
    copied = 0
    for i in range(NPOP):
        cx, cy, cz = (int(c) for c in VEL[i])
        v = f[i]
        if cx:
            k = (FORWARD if cx > 0 else BACKWARD).index(i)
            rim = [rim_row(below if cx > 0 else above, k, h, cx > 0) for h in range(2)]
            at = row >= 6 if cx > 0 else (row == 4) | (row == 5)
            v = jnp.where(at & ~pasted, jnp.where(odd, rim[1], rim[0]), v)
        if cz:
            edge = lane % BX == (0 if cz > 0 else BX - 1)
            v = jnp.where(
                edge, roll_lanes(v, BX * cy + cz - BX * cz), roll_lanes(v, BX * cy + cz)
            )
        elif cy:
            v = roll_lanes(v, BX * cy)
        if cy:
            carried = lane < BX if cy > 0 else lane >= LANES - BX
            v = jnp.where(carried, jnp.where(odd, roll_rows(v, 1), roll_rows(v, -1)), v)
        for h in range(2):
            inside = middle[i, h]
            if cx > 0:
                tile = pick(
                    ((0,), roll_rows(v, 2 - h)), ((1,), roll_rows(v, 1 - h)), (roll_rows(inside, 1),)
                )
            elif cx < 0:
                tile = pick(
                    ((7,), roll_rows(v, 3 - h)), ((6,), roll_rows(v, 4 - h)), (roll_rows(inside, -1),)
                )
            else:
                tile = pick(((0,), roll_rows(v, -h)), ((7,), roll_rows(v, 5 - h)), (inside,))
            out[0, i, :, half_lanes(h)] = tile
        if i + 1 in CHUNKS:
            some = pl.ds(copied, i + 1 - copied)
            pltpu.make_async_copy(out.at[0, some], result.at[0, some], sem).start()
            copied = i + 1
    pltpu.make_async_copy(out, result, sem).wait()


def others(groups):
    return range(1, groups)


def exchange(array, distance):
    groups = lax.axis_size("grp")
    return lax.ppermute(array, "grp", [(i, i ^ distance) for i in range(groups)])


def held(array):
    return pltpu.with_memory_space_constraint(array, VMEM)


def left(array):
    return pltpu.with_memory_space_constraint(array, pltpu.HBM)


def in_vmem(*shape):
    return VMEM(shape, jnp.float32)


def call(kernel, args, specs, outs, scratch=(), flops=0, name=None, out_space=VMEM):
    single = not isinstance(outs, (list, tuple))
    outs = [outs] if single else list(outs)
    result = pl.pallas_call(
        kernel,
        in_specs=[pl.BlockSpec(memory_space=s) for s in specs],
        out_specs=[pl.BlockSpec(memory_space=out_space)] * len(outs),
        out_shape=outs,
        scratch_shapes=list(scratch),
        compiler_params=pltpu.CompilerParams(vmem_limit_bytes=24 << 20),
        cost_estimate=pl.CostEstimate(flops=flops, bytes_accessed=1, transcendentals=0),
        name=name,
    )(*args)
    return result[0] if single else result


def per_device(fine_pops, fine_solid, coarse_pops, coarse_solid, coarse_slot):
    groups = lax.axis_size("grp")
    blocks = lax.axis_size("blk")
    moved, second, high, low, center, shade, slot = call(
        pack_kernel,
        tuple(map(left, (fine_pops, fine_solid, coarse_pops, coarse_solid, coarse_slot))),
        [pl.ANY] * 5,
        [
            in_vmem(NPOP + 1, 2, *TILE),
            in_vmem(NPOP, 2, *TILE),
            in_vmem(WORDS + 1, *TILE),
            in_vmem(WORDS, *TILE),
            in_vmem(NPOP, ROWS, 2 * LANES),
            in_vmem(*fine_solid.shape[1:]),
            VMEM((groups,), jnp.int32),
        ],
        [
            in_vmem(NPOP + 2, ROWS, 2 * LANES),
            in_vmem(NPOP + 1, ROWS, 2 * LANES),
            pltpu.SemaphoreType.DMA((4,)),
        ],
        name="pack",
    )
    coarse_v, coarse_solid_v = held(coarse_pops), held(coarse_solid)
    inner_shapes = [
        in_vmem(NPOP, 2, 2 * ROWS, LANES),
        in_vmem(INNER_TILES, *TILE),
        in_vmem(4, groups, *TILE),
        VMEM((2 * LANES, LANES), jnp.bfloat16),
    ]
    inner_args = (held(center), held(shade), held(moved), held(slot))
    *done, low = call(
        early_kernel,
        (*inner_args, held(low)),
        [VMEM] * 5,
        [*inner_shapes, in_vmem(WORDS, *TILE)],
        name="early",
    )
    forward = [(i, (i + 1) % blocks) for i in range(blocks)]
    backward = [(i, (i - 1) % blocks) for i in range(blocks)]
    below = lax.ppermute(high, "blk", forward)
    above = lax.ppermute(low, "blk", backward)
    inner, packed_inner, chosen, matrix, padded_inner = call(
        inner_kernel,
        (*inner_args, *map(held, done)),
        [VMEM] * 8,
        [*inner_shapes, in_vmem(INNER_TILES + 1, *TILE)],
        name="inner",
    )

    across = [exchange(packed_inner, s) for s in range(2, groups, 2)]
    beside = exchange(padded_inner, 1)
    edges, packed_edges = call(
        edge_kernel,
        (held(moved), held(second), held(below), held(above), held(matrix), coarse_v, coarse_solid_v),
        [VMEM] * 7,
        [in_vmem(NPOP, 2, *TILE), in_vmem((NPOP + 1) // 4, *TILE)],
        name="edge",
    )
    edge_parts = [packed_edges] + [exchange(packed_edges, s) for s in others(groups)]
    fine_out = call(
        write_kernel,
        (held(inner), held(edges)),
        [VMEM] * 2,
        jax.ShapeDtypeStruct(fine_pops.shape, jnp.float32),
        name="write",
    )
    inner_parts = [beside, packed_inner, *across]
    base, ends = call(
        paste_kernel,
        (
            held(edges),
            coarse_v,
            coarse_solid_v,
            held(chosen),
            held(below),
            held(above),
            *map(held, inner_parts),
        ),
        [VMEM] * (6 + len(inner_parts)),
        [in_vmem(NPOP, 2, *TILE), in_vmem(NPOP + 1, *TILE)],
        name="paste",
    )
    relayed = []
    for part in across:
        halves = call(
            split_kernel,
            (held(edges), held(part)),
            [VMEM] * 2,
            [in_vmem(part.shape[0] // 2, *TILE)] * 2,
            name="split",
        )
        relayed += [exchange(half, 1) for half in halves]
    middle = call(
        coarse_kernel,
        (left(fine_out), held(base), coarse_solid_v, held(chosen), *map(held, relayed)),
        [pl.ANY] + [VMEM] * (3 + len(relayed)),
        in_vmem(NPOP, 2, *TILE),
        name="coarse",
    )
    coarse_out = call(
        last_kernel,
        (held(chosen), held(below), held(above), held(ends), held(middle), *map(held, edge_parts)),
        [VMEM] * (5 + len(edge_parts)),
        jax.ShapeDtypeStruct(coarse_pops.shape, jnp.float32),
        [in_vmem(*coarse_pops.shape), pltpu.SemaphoreType.DMA],
        out_space=pl.ANY,
        name="last",
    )
    return fine_out, coarse_out


def solution(mesh):
    placed = (
        P("grp", None, "blk", None),
        P("grp", "blk", None),
        P("grp", None, "blk", None),
        P("grp", "blk", None),
        P(),
    )
    return jax.shard_map(
        per_device,
        mesh=mesh,
        in_specs=placed,
        out_specs=(P("grp", None, "blk", None), P("grp", None, "blk", None)),
        check_vma=False,
    )
```

```python
import jax
import jax.numpy as jnp
import numpy as np
from jax import lax
from jax.experimental import pallas as pl
from jax.experimental.pallas import tpu as pltpu
from jax.sharding import PartitionSpec as P

VEL = np.array(
    [
        [0, 0, 0],
        [1, 0, 0],
        [-1, 0, 0],
        [0, 1, 0],
        [0, -1, 0],
        [0, 0, 1],
        [0, 0, -1],
        [1, 1, 0],
        [-1, -1, 0],
        [1, -1, 0],
        [-1, 1, 0],
        [1, 0, 1],
        [-1, 0, -1],
        [1, 0, -1],
        [-1, 0, 1],
        [0, 1, 1],
        [0, -1, -1],
        [0, 1, -1],
        [0, -1, 1],
    ]
)
NPOP = 19
BX = 16
TAU_FINE = 0.6
TAU_COARSE = 0.55
RESCALE = 2.0 * TAU_COARSE / TAU_FINE

ROWS, LANES = 8, 128
TILE = (ROWS, LANES)
VMEM = pltpu.VMEM


def row_ids():
    return lax.broadcasted_iota(jnp.int32, TILE, 0)


def lane_ids():
    return lax.broadcasted_iota(jnp.int32, TILE, 1)


def roll_rows(tile, shift):
    return pltpu.roll(tile, shift % ROWS, 0)


def roll_lanes(tile, shift):
    return pltpu.roll(tile, shift % LANES, 1)


def moments(f, scale):
    minus = [f[i] - f[i + 1] for i in range(1, NPOP, 2)]
    plus = [f[i] + f[i + 1] for i in range(1, NPOP, 2)]
    rho = ((f[0] + plus[0]) + (plus[1] + plus[2])) + (
        (plus[3] + plus[4]) + (plus[5] + plus[6])
    ) + (plus[7] + plus[8])
    jx = (minus[0] + minus[3]) + (minus[4] + minus[5]) + minus[6]
    jy = (minus[1] + minus[3]) - (minus[4] - minus[7]) + minus[8]
    jz = (minus[2] + minus[5]) - (minus[6] - minus[7]) - minus[8]
    inverse = 1.5 / rho
    ux, uy, uz = jx * inverse, jy * inverse, jz * inverse
    amount = scale(rho)
    base = amount * (1.0 - (2.0 / 3.0) * (ux * ux + uy * uy + uz * uz))
    directions = [ux, uy, uz, ux + uy, ux - uy, ux + uz, ux - uz, uy + uz, uy - uz]
    base_axis, base_diag = base * (1.0 / 18.0), base * (1.0 / 36.0)
    amount_axis, amount_diag = amount * (1.0 / 9.0), amount * (1.0 / 18.0)
    pairs = []
    for k, along in enumerate(directions):
        odd = (amount_axis if k < 3 else amount_diag) * along
        pairs.append(((base_axis if k < 3 else base_diag) + odd * along, odd))
    return base * (1.0 / 3.0), pairs, plus, minus


def collide(f, solid, tau):
    rate = (1.0 - solid) * (1.0 / tau)
    rest, pairs, plus, minus = moments(f, lambda rho: rate * rho)
    keep = 1.0 - rate
    half = 0.5 * keep
    half_odd = half - solid
    out = [keep * f[0] + rest]
    for (even, odd), p, m in zip(pairs, plus, minus):
        symmetric = half * p + even
        antisymmetric = half_odd * m + odd
        out += [symmetric + antisymmetric, symmetric - antisymmetric]
    return out


def restrict(f):
    rest, pairs, _, _ = moments(f, lambda rho: (1.0 - RESCALE) * rho)
    out = [RESCALE * f[0] + rest]
    for k, (even, odd) in enumerate(pairs):
        out += [RESCALE * f[2 * k + 1] + (even + odd), RESCALE * f[2 * k + 2] + (even - odd)]
    return out


def shift_plane(halves, cy, cz):
    lane = lane_ids()
    if cz:
        edge = lane % BX == (0 if cz > 0 else BX - 1)
        halves = [
            jnp.where(
                edge,
                roll_lanes(v, BX * cy + cz - BX * cz),
                roll_lanes(v, BX * cy + cz),
            )
            for v in halves
        ]
    elif cy:
        halves = [roll_lanes(v, BX * cy) for v in halves]
    if cy:
        carried = lane < BX if cy > 0 else lane >= LANES - BX
        halves = [
            jnp.where(carried, halves[1], halves[0]),
            jnp.where(carried, halves[0], halves[1]),
        ]
    return halves


def shift_ring(tiles, cx):
    if not cx:
        return tiles
    row = row_ids()
    turned = [roll_rows(t, cx) for t in tiles]
    if len(tiles) == 1:
        return turned
    edge = row == (0 if cx > 0 else ROWS - 1)
    n = len(tiles)
    return [jnp.where(edge, turned[(i - cx) % n], turned[i]) for i in range(n)]


def move_in_planes(halves):
    moved = [
        shift_plane([halves[0][i], halves[1][i]], int(VEL[i, 1]), int(VEL[i, 2]))
        for i in range(NPOP)
    ]
    return [[moved[i][h] for i in range(NPOP)] for h in range(2)]


def move_along(ring):
    out = [[[], []] for _ in ring]
    for h in range(2):
        for i in range(NPOP):
            for t, v in enumerate(shift_ring([tile[h][i] for tile in ring], int(VEL[i, 0]))):
                out[t][h].append(v)
    return out


def merge(mask, first, second):
    return [
        [jnp.where(mask, v, w) for v, w in zip(a, b)] for a, b in zip(first, second)
    ]


def means():
    shape = (2 * LANES, LANES)
    fine = lax.broadcasted_iota(jnp.int32, shape, 0)
    place = lax.broadcasted_iota(jnp.int32, shape, 1)
    same = (fine // (2 * BX) == place // BX) & (fine % BX // 2 == place % 8)
    return jnp.where(same, 0.125, 0.0).astype(jnp.bfloat16)


def squeeze(planes, matrix):
    cells = jnp.concatenate([jnp.concatenate(halves, axis=1) for halves in planes], axis=0)
    found = None
    for _ in range(3):
        part = cells.astype(jnp.bfloat16)
        product = jnp.dot(part, matrix, preferred_element_type=jnp.float32)
        found = product if found is None else found + product
        cells = cells - part.astype(jnp.float32)
    return [found[ROWS * k : ROWS * (k + 1)] for k in range(len(planes))]


INNER_TILES = (NPOP + 1) // 2 - 2


def fold(tiles):
    out = list(tiles[:INNER_TILES])
    for m in range(6):
        extra, at = tiles[INNER_TILES + m // 3], 2 * (m % 3)
        out[m] = pick(((0,), roll_rows(extra, -1 - at)), ((7,), roll_rows(extra, 5 - at)), (out[m],))
    return out


def unfold(tile, j):
    if j < INNER_TILES:
        return tile(j)
    rows = []
    for m in range(3):
        v = tile(3 * (j - INNER_TILES) + m)
        rows += [((1 + 2 * m,), roll_rows(v, 1 + 2 * m)), ((2 + 2 * m,), roll_rows(v, 2 * m - 5))]
    return pick(*rows, (rows[-1][1],))


def lower():
    return lane_ids() % BX < 8


def pair_up(first, second):
    return first if second is None else jnp.where(lower(), first, second)


def spread(first, second, which):
    if which:
        return jnp.where(lower(), roll_lanes(first, -8), second)
    return jnp.where(lower(), first, roll_lanes(second, 8))


def filled(chosen, h, sources):
    low, high = (sum(chosen[2 * h + z, s] for s in sources) for z in range(2))
    return jnp.where(lower(), low, high) > 0.5


def choose(chosen, quadrant, tiles):
    (_, out), *rest = tiles
    for s, tile in rest:
        out = jnp.where(chosen[quadrant, s] > 0.5, tile, out)
    return out


def half_lanes(h):
    return pl.ds(h * LANES, LANES)


FORWARD = [i for i in range(NPOP) if VEL[i, 0] > 0]
LEVEL = [i for i in range(NPOP) if VEL[i, 0] == 0]
BACKWARD = [i for i in range(NPOP) if VEL[i, 0] < 0]
MOVING = len(FORWARD)

PAIRS = (len(LEVEL) + 1) // 2
WORDS = MOVING + PAIRS


def pick(*choices):
    row = row_ids()
    out = choices[-1][-1]
    for rows, tile in choices[-2::-1]:
        mask = row == rows[0]
        for r in rows[1:]:
            mask = mask | (row == r)
        out = jnp.where(mask, tile, out)
    return out


def pack_message(message, first, second, rim, up):
    for k, i in enumerate(FORWARD if up else BACKWARD):
        f, s = [first(i, h) for h in range(2)], [second(i, h) for h in range(2)]
        s = [v + roll_rows(v, -1) for v in s]
        if up:
            message[k] = pick(
                ((7, 0), roll_rows(f[0], 1)),
                ((1, 2), roll_rows(f[1], 3)),
                ((3,), roll_rows(s[0], -2)),
                ((5,), s[1]),
                ((4,), rim[k]),
                (roll_rows(rim[k], -2),),
            )
        else:
            message[k] = pick(
                ((3, 4), roll_rows(f[0], 3)),
                ((5, 6), roll_rows(f[1], 5)),
                ((7,), roll_rows(s[0], -2)),
                ((1,), s[1]),
                ((0,), roll_rows(rim[k], -3)),
                (roll_rows(rim[k], 3),),
            )
    for k in range(PAIRS):
        shared = []
        for i in (LEVEL + [NPOP])[2 * k : 2 * k + 2]:
            f = [first(i, h) for h in range(2)]
            if up:
                if i < NPOP:
                    s = [roll_rows(second(i, 0), -3), roll_rows(second(i, 1), -1)]
                else:
                    s = [roll_rows(rim[MOVING], -1), roll_rows(rim[MOVING], 5)]
                shared.append(pick(((7,), f[0]), ((1,), roll_rows(f[1], 2)), ((3,), s[0]), (s[1],)))
            else:
                if i < NPOP:
                    s = [roll_rows(second(i, 0), -1), roll_rows(second(i, 1), 1)]
                else:
                    s = [roll_rows(rim[MOVING], -3), roll_rows(rim[MOVING], 3)]
                shared.append(
                    pick(((4,), roll_rows(f[0], 4)), ((6,), roll_rows(f[1], -2)), ((0,), s[0]), (s[1],))
                )
        own_rows = (1, 3, 5, 7) if up else (0, 2, 4, 6)
        message[MOVING + k] = pick((own_rows, shared[0]), (roll_rows(shared[1], 1),))


def shared_tile(message, i):
    k = (LEVEL + [NPOP]).index(i)
    return roll_rows(message[MOVING + k // 2], -(k % 2))


def rim_row(message, k, h, up):
    index, row = (k, 0) if k < MOVING else (WORDS - 1, 1)
    row = 4 + 2 * h if up else row + 2 * h
    return jnp.broadcast_to(message[index, pl.ds(row, 1), :], TILE)


def pack_kernel(
    fine, solid, coarse, coarse_solid, slot, moved, second, high, low, center, shade, slot_out, strip, rim, sem
):
    planes = fine.shape[2]
    last = coarse.shape[2] - 1

    def bring(source, target, which):
        pltpu.make_async_copy(source, target, sem.at[which]).start()

    def arrive(target, which):
        pltpu.make_async_copy(target, target, sem.at[which]).wait()

    ends = ((0, 0), (planes - 4, 4))
    for half in (pl.ds(0, 7), pl.ds(7, 6), pl.ds(13, 6)):
        for first, row in ends:
            bring(fine.at[0, half, pl.ds(first, 4), :], strip.at[half, pl.ds(row, 4), :], 0)
    bring(solid.at[0], shade, 0)
    for plane, row in ((last, 0), (0, 3)):
        bring(coarse.at[0, :, pl.ds(plane, 1), :], rim.at[pl.ds(0, NPOP), pl.ds(row, 1), :], 1)
        bring(coarse_solid.at[0, pl.ds(plane, 1), :], rim.at[NPOP, pl.ds(row, 1), :], 1)
    bring(slot, slot_out, 2)
    for first, row in ((4, 4), (8, 0)):
        bring(fine.at[0, :, pl.ds(first, 4), :], center.at[:, pl.ds(row, 4), :], 3)
    arrive(strip, 0)
    upper = row_ids() < 4
    solids = [
        jnp.where(upper, shade[pl.ds(0, ROWS), half_lanes(h)], shade[pl.ds(planes - ROWS, ROWS), half_lanes(h)])
        for h in range(2)
    ]
    once = move_in_planes(
        [collide([strip[i, :, half_lanes(h)] for i in range(NPOP)], solids[h], TAU_FINE) for h in range(2)]
    )
    arrive(slot_out, 2)
    arrive(rim.at[:, pl.ds(0, 2), :], 1)

    def rim_tile(i):
        v = [rim[i, :, half_lanes(h)] for h in range(2)]
        return pick(((0,), v[1]), ((3,), v[0]), ((4,), roll_rows(v[0], 4)), (roll_rows(v[1], 4),))

    s = rim_tile(NPOP)
    outer = collide([rim_tile(i) for i in range(NPOP)], s, TAU_COARSE) + [s]
    ring = move_along([once])[0]
    twice = [collide(ring[h], solids[h], TAU_FINE) for h in range(2)]
    for h in range(2):
        for i in range(NPOP):
            moved[i, h] = once[h][i]
            second[i, h] = twice[h][i]
        moved[NPOP, h] = solids[h]

    def first_of(i, h):
        return moved[i, h]

    def second_of(i, h):
        return second[i, h]

    pack_message(high, first_of, second_of, [outer[i] for i in FORWARD + [NPOP]], True)
    pack_message(low, first_of, second_of, [outer[i] for i in BACKWARD + [NPOP]], False)
    arrive(center, 3)


def inner_steps(center, solid, moved, inner, packed):
    upper = row_ids() < 4
    solids = [
        [solid[pl.ds(ROWS * t, ROWS), half_lanes(h)] for h in range(2)] for t in range(2)
    ]
    outer = [[moved[i, h] for i in range(NPOP)] for h in range(2)]
    between = move_in_planes(
        [
            collide(
                [center[i, :, half_lanes(h)] for i in range(NPOP)],
                jnp.where(upper, solids[1][h], solids[0][h]),
                TAU_FINE,
            )
            for h in range(2)
        ]
    )
    ring = move_along([merge(upper, outer, between), merge(upper, between, outer)])
    for t in range(2):
        for h in range(2):
            ring[t][h] = collide(ring[t][h], solids[t][h], TAU_FINE)
        ring[t] = move_in_planes(ring[t])
    ring = move_along(ring)
    for i in range(NPOP):
        for h in range(2):
            for t in range(2):
                inner[i, h, pl.ds(ROWS * t, ROWS), :] = ring[t][h][i]
    sums = [
        [
            inner[i, h, pl.ds(0, ROWS, stride=2), :] + inner[i, h, pl.ds(1, ROWS, stride=2), :]
            for h in range(2)
        ]
        for i in range(NPOP)
    ]
    out = restrict(squeeze(sums, means())) + [None]
    pairs = [pair_up(out[2 * j], out[2 * j + 1]) for j in range((NPOP + 1) // 2)]
    for j, tile in enumerate(fold(pairs)):
        packed[j] = tile


def starts_early():
    return lax.axis_index("blk") == 0


def prepare(slot, chosen, matrix):
    groups = chosen.shape[1]
    matrix[...] = means()
    me = lax.axis_index("grp")
    codes = slot[...].reshape(1, groups)
    group_ids = lax.broadcasted_iota(jnp.int32, codes.shape, 1)
    for s in range(groups):
        code = jnp.sum(jnp.where(group_ids == me ^ s, codes, 0), axis=1, keepdims=True)
        for q in range(4):
            chosen[q, s] = jnp.where(lane_ids() * 0 + (4 * me + q) == code, 1.0, 0.0)


def early_kernel(center, solid, moved, slot, low, inner, packed, chosen, matrix, low_out):
    low_out[...] = low[...]

    @pl.when(starts_early())
    def _():
        inner_steps(center, solid, moved, inner, packed)
        prepare(slot, chosen, matrix)


def inner_kernel(center, solid, moved, slot, *refs):
    *refs, padded = refs
    done, (inner, packed, chosen, matrix) = refs[:4], refs[4:]

    @pl.when(starts_early())
    def _():
        for source, target in zip(done, (inner, packed, chosen, matrix)):
            target[...] = source[...]

    @pl.when(jnp.logical_not(starts_early()))
    def _():
        inner_steps(center, solid, moved, inner, packed)
        prepare(slot, chosen, matrix)

    size = packed.shape[0]
    padded[pl.ds(0, size)] = packed[...]
    padded[size] = jnp.zeros(TILE, jnp.float32)


def edge_kernel(moved, second, below, above, matrix, coarse, coarse_solid, edges, packed):
    row = row_ids()

    def middle(i):
        v = [moved[i, h] for h in range(2)]
        if i in FORWARD:
            return pick(
                ((3, 4), roll_rows(v[0], -3)),
                ((5, 6), roll_rows(v[1], -1)),
                (below[FORWARD.index(i)],),
            )
        if i in BACKWARD:
            return pick(
                ((7, 0), roll_rows(v[0], -1)),
                ((1, 2), roll_rows(v[1], 1)),
                (above[BACKWARD.index(i)],),
            )
        return pick(
            ((0,), v[0]),
            ((2,), roll_rows(v[1], 2)),
            ((3,), roll_rows(v[0], 4)),
            ((5,), roll_rows(v[1], -2)),
            ((1, 7), shared_tile(below, i)),
            (shared_tile(above, i),),
        )

    twice = collide([middle(i) for i in range(NPOP)], middle(NPOP), TAU_FINE)
    nothing = jnp.zeros(TILE, jnp.float32)
    both = [[], []]
    for h in range(2):
        for i in range(NPOP):
            cx = int(VEL[i, 0])
            v, mine = roll_rows(twice[i], cx - 2 * h), second[i, h]
            if cx > 0:
                v = pick(
                    ((0, 1, 4, 5), v),
                    ((2, 3), roll_rows(mine, -3)),
                    ((7,), nothing),
                    (roll_rows(below[FORWARD.index(i)], 3 - 2 * h),),
                )
            elif cx < 0:
                v = pick(
                    ((2, 3, 6, 7), v),
                    ((0, 1), roll_rows(mine, -1)),
                    ((5,), nothing),
                    (roll_rows(above[BACKWARD.index(i)], -3 - 2 * h),),
                )
            else:
                v = pick(
                    ((0, 3, 4, 7), v),
                    ((1,), mine),
                    ((2,), roll_rows(mine, 4)),
                    ((6,), roll_rows(shared_tile(below, i), 3 - 2 * h)),
                    (roll_rows(shared_tile(above, i), -3 - 2 * h),),
                )
            both[h].append(v)
    both = move_in_planes(both)
    sums = [[v + roll_rows(v, -1) for v in half] + [None] for half in both]
    odd = row % 2 == 1
    pairs = [
        [half[i] if half[i + 1] is None else jnp.where(odd, roll_rows(half[i + 1], 1), half[i]) for half in sums]
        for i in range(0, NPOP, 2)
    ]
    mean = []
    for pair in squeeze(pairs, matrix[...]):
        mean += [pair, roll_rows(pair, -1)]
    out = restrict(mean[:NPOP]) + [None]
    pairs = [
        out[i] if out[i + 1] is None else jnp.where(odd, roll_rows(out[i + 1], 1), out[i])
        for i in range(0, NPOP, 2)
    ]
    for j in range(len(pairs) // 2):
        packed[j] = pair_up(pairs[2 * j], pairs[2 * j + 1])
    for i in range(NPOP):
        for h in range(2):
            edges[i, h] = both[h][i]


def write_kernel(inner, edges, out):
    row = row_ids()
    for i in range(NPOP):
        for h in range(2):
            edge = edges[i, h]
            out[0, i, pl.ds(0, ROWS), half_lanes(h)] = jnp.where(
                row < 2, edge, inner[i, h, pl.ds(0, ROWS), :]
            )
            out[0, i, pl.ds(ROWS, ROWS), half_lanes(h)] = jnp.where(
                row >= 6, roll_rows(edge, 4), inner[i, h, pl.ds(ROWS, ROWS), :]
            )


def split_kernel(after, tiles, first, second):
    half = first.shape[0]
    first[...] = tiles[pl.ds(0, half)]
    second[...] = tiles[pl.ds(half, half)]


def paste_inner(chosen, sources, tile, base, out):
    masks = [filled(chosen, h, sources) for h in range(2)]
    for j in range((NPOP + 1) // 2):
        tiles = [(s, tile(s, j)) for s in sources]
        for h in range(2):
            low, high = (choose(chosen, 2 * h + z, tiles) for z in range(2))
            for i in range(2 * j, min(2 * j + 2, NPOP)):
                out(i, h, jnp.where(masks[h], spread(low, high, i % 2), base(i, h)))


def paste_kernel(after, coarse, solid, chosen, below, above, *refs):
    *packed, out, ends = refs
    sources = [1, *range(0, chosen.shape[1], 2)]
    parts = dict(zip(sources, packed))

    def write(i, h, tile):
        out[i, h] = tile

    paste_inner(
        chosen, sources, lambda s, j: unfold(lambda k: parts[s][k], j), lambda i, h: coarse[0, i, :, half_lanes(h)], write
    )
    for i in range(NPOP + 1):
        v = [coarse[0, i, :, half_lanes(h)] if i < NPOP else solid[0, :, half_lanes(h)] for h in range(2)]
        tile = pick(((0,), v[0]), ((1,), roll_rows(v[1], 1)), ((2,), roll_rows(v[0], 3)), (roll_rows(v[1], 4),))
        if i == NPOP:
            tile = pick(
                ((4,), rim_row(above, MOVING, 0, False)),
                ((5,), rim_row(above, MOVING, 1, False)),
                ((6,), rim_row(below, MOVING, 0, True)),
                ((7,), rim_row(below, MOVING, 1, True)),
                (tile,),
            )
        ends[i] = tile


def coarse_kernel(after, base, solid, chosen, *refs):
    relayed, out = refs[:-1], refs[-1]
    sources = [2 * k + 3 for k in range(len(relayed) // 2)]
    f = [[None] * NPOP, [None] * NPOP]

    def write(i, h, tile):
        f[h][i] = tile

    half = relayed[0].shape[0]

    def tile(s, j):
        return unfold(lambda k: relayed[s - 3 + k // half][k % half], j)

    paste_inner(chosen, sources, tile, lambda i, h: base[i, h], write)
    f = move_in_planes([collide(f[h], solid[0, :, half_lanes(h)], TAU_COARSE) for h in range(2)])
    for h in range(2):
        for i in range(NPOP):
            out[i, h] = f[h][i]


CHUNKS = (0, 3, 6, 9, 12, 15, 17, NPOP)


def last_kernel(chosen, below, above, base, middle, *refs):
    *packed, result, out, sem = refs
    sources = [0, *others(len(packed))]
    row, lane = row_ids(), lane_ids()
    odd = row % 2 == 1
    pasted = [filled(chosen, h, sources) for h in range(2)]
    pasted = (odd & pasted[1]) | (~odd & pasted[0])
    f = []
    for j in range((NPOP + 1) // 4):
        tiles = [(s, part[j]) for s, part in zip(sources, packed)]
        quadrants = [choose(chosen, q, tiles) for q in range(4)]
        for which in range(2):
            v = [spread(quadrants[2 * h], quadrants[2 * h + 1], which) for h in range(2)]
            f.append(jnp.where(odd, roll_rows(v[1], 1), v[0]))
            f.append(jnp.where(odd, v[1], roll_rows(v[0], -1)))
    f = [jnp.where(pasted, f[i], base[i]) for i in range(NPOP)]
    f = collide(f, base[NPOP], TAU_COARSE)
    copied = 0
    for i in range(NPOP):
        cx, cy, cz = (int(c) for c in VEL[i])
        v = f[i]
        if cx:
            k = (FORWARD if cx > 0 else BACKWARD).index(i)
            rim = [rim_row(below if cx > 0 else above, k, h, cx > 0) for h in range(2)]
            at = row >= 6 if cx > 0 else (row == 4) | (row == 5)
            v = jnp.where(at & ~pasted, jnp.where(odd, rim[1], rim[0]), v)
        if cz:
            edge = lane % BX == (0 if cz > 0 else BX - 1)
            v = jnp.where(
                edge, roll_lanes(v, BX * cy + cz - BX * cz), roll_lanes(v, BX * cy + cz)
            )
        elif cy:
            v = roll_lanes(v, BX * cy)
        if cy:
            carried = lane < BX if cy > 0 else lane >= LANES - BX
            v = jnp.where(carried, jnp.where(odd, roll_rows(v, 1), roll_rows(v, -1)), v)
        for h in range(2):
            inside = middle[i, h]
            if cx > 0:
                tile = pick(
                    ((0,), roll_rows(v, 2 - h)), ((1,), roll_rows(v, 1 - h)), (roll_rows(inside, 1),)
                )
            elif cx < 0:
                tile = pick(
                    ((7,), roll_rows(v, 3 - h)), ((6,), roll_rows(v, 4 - h)), (roll_rows(inside, -1),)
                )
            else:
                tile = pick(((0,), roll_rows(v, -h)), ((7,), roll_rows(v, 5 - h)), (inside,))
            out[0, i, :, half_lanes(h)] = tile
        if i + 1 in CHUNKS:
            some = pl.ds(copied, i + 1 - copied)
            pltpu.make_async_copy(out.at[0, some], result.at[0, some], sem).start()
            copied = i + 1
    pltpu.make_async_copy(out, result, sem).wait()


def others(groups):
    return range(1, groups)


def exchange(array, distance):
    groups = lax.axis_size("grp")
    return lax.ppermute(array, "grp", [(i, i ^ distance) for i in range(groups)])


def held(array):
    return pltpu.with_memory_space_constraint(array, VMEM)


def left(array):
    return pltpu.with_memory_space_constraint(array, pltpu.HBM)


def in_vmem(*shape):
    return VMEM(shape, jnp.float32)


def call(kernel, args, specs, outs, scratch=(), flops=0, name=None, out_space=VMEM):
    single = not isinstance(outs, (list, tuple))
    outs = [outs] if single else list(outs)
    result = pl.pallas_call(
        kernel,
        in_specs=[pl.BlockSpec(memory_space=s) for s in specs],
        out_specs=[pl.BlockSpec(memory_space=out_space)] * len(outs),
        out_shape=outs,
        scratch_shapes=list(scratch),
        compiler_params=pltpu.CompilerParams(vmem_limit_bytes=24 << 20),
        cost_estimate=pl.CostEstimate(flops=flops, bytes_accessed=1, transcendentals=0),
        name=name,
    )(*args)
    return result[0] if single else result


def per_device(fine_pops, fine_solid, coarse_pops, coarse_solid, coarse_slot):
    groups = lax.axis_size("grp")
    blocks = lax.axis_size("blk")
    moved, second, high, low, center, shade, slot = call(
        pack_kernel,
        tuple(map(left, (fine_pops, fine_solid, coarse_pops, coarse_solid, coarse_slot))),
        [pl.ANY] * 5,
        [
            in_vmem(NPOP + 1, 2, *TILE),
            in_vmem(NPOP, 2, *TILE),
            in_vmem(WORDS, *TILE),
            in_vmem(WORDS, *TILE),
            in_vmem(NPOP, ROWS, 2 * LANES),
            in_vmem(*fine_solid.shape[1:]),
            VMEM((groups,), jnp.int32),
        ],
        [
            in_vmem(NPOP + 2, ROWS, 2 * LANES),
            in_vmem(NPOP + 1, ROWS, 2 * LANES),
            pltpu.SemaphoreType.DMA((4,)),
        ],
        name="pack",
    )
    coarse_v, coarse_solid_v = held(coarse_pops), held(coarse_solid)
    inner_shapes = [
        in_vmem(NPOP, 2, 2 * ROWS, LANES),
        in_vmem(INNER_TILES, *TILE),
        in_vmem(4, groups, *TILE),
        VMEM((2 * LANES, LANES), jnp.bfloat16),
    ]
    inner_args = (held(center), held(shade), held(moved), held(slot))
    *done, low = call(
        early_kernel,
        (*inner_args, held(low)),
        [VMEM] * 5,
        [*inner_shapes, in_vmem(WORDS, *TILE)],
        name="early",
    )
    forward = [(i, (i + 1) % blocks) for i in range(blocks)]
    backward = [(i, (i - 1) % blocks) for i in range(blocks)]
    below = lax.ppermute(high, "blk", forward)
    above = lax.ppermute(low, "blk", backward)
    inner, packed_inner, chosen, matrix, padded_inner = call(
        inner_kernel,
        (*inner_args, *map(held, done)),
        [VMEM] * 8,
        [*inner_shapes, in_vmem(INNER_TILES + 1, *TILE)],
        name="inner",
    )

    across = [exchange(packed_inner, s) for s in range(2, groups, 2)]
    beside = exchange(padded_inner, 1)
    edges, packed_edges = call(
        edge_kernel,
        (held(moved), held(second), held(below), held(above), held(matrix), coarse_v, coarse_solid_v),
        [VMEM] * 7,
        [in_vmem(NPOP, 2, *TILE), in_vmem((NPOP + 1) // 4, *TILE)],
        name="edge",
    )
    edge_parts = [packed_edges] + [exchange(packed_edges, s) for s in others(groups)]
    fine_out = call(
        write_kernel,
        (held(inner), held(edges)),
        [VMEM] * 2,
        jax.ShapeDtypeStruct(fine_pops.shape, jnp.float32),
        name="write",
    )
    inner_parts = [beside, packed_inner, *across]
    base, ends = call(
        paste_kernel,
        (
            held(edges),
            coarse_v,
            coarse_solid_v,
            held(chosen),
            held(below),
            held(above),
            *map(held, inner_parts),
        ),
        [VMEM] * (6 + len(inner_parts)),
        [in_vmem(NPOP, 2, *TILE), in_vmem(NPOP + 1, *TILE)],
        name="paste",
    )
    relayed = []
    for part in across:
        halves = call(
            split_kernel,
            (held(edges), held(part)),
            [VMEM] * 2,
            [in_vmem(part.shape[0] // 2, *TILE)] * 2,
            name="split",
        )
        relayed += [exchange(half, 1) for half in halves]
    middle = call(
        coarse_kernel,
        (left(fine_out), held(base), coarse_solid_v, held(chosen), *map(held, relayed)),
        [pl.ANY] + [VMEM] * (3 + len(relayed)),
        in_vmem(NPOP, 2, *TILE),
        name="coarse",
    )
    coarse_out = call(
        last_kernel,
        (held(chosen), held(below), held(above), held(ends), held(middle), *map(held, edge_parts)),
        [VMEM] * (5 + len(edge_parts)),
        jax.ShapeDtypeStruct(coarse_pops.shape, jnp.float32),
        [in_vmem(*coarse_pops.shape), pltpu.SemaphoreType.DMA],
        out_space=pl.ANY,
        name="last",
    )
    return fine_out, coarse_out


def solution(mesh):
    placed = (
        P("grp", None, "blk", None),
        P("grp", "blk", None),
        P("grp", None, "blk", None),
        P("grp", "blk", None),
        P(),
    )
    return jax.shard_map(
        per_device,
        mesh=mesh,
        in_specs=placed,
        out_specs=(P("grp", None, "blk", None), P("grp", None, "blk", None)),
        check_vma=False,
    )
```

```python
import jax
import jax.numpy as jnp
import numpy as np
from jax import lax
from jax.experimental import pallas as pl
from jax.experimental.pallas import tpu as pltpu
from jax.sharding import PartitionSpec as P

VEL = np.array(
    [
        [0, 0, 0],
        [1, 0, 0],
        [-1, 0, 0],
        [0, 1, 0],
        [0, -1, 0],
        [0, 0, 1],
        [0, 0, -1],
        [1, 1, 0],
        [-1, -1, 0],
        [1, -1, 0],
        [-1, 1, 0],
        [1, 0, 1],
        [-1, 0, -1],
        [1, 0, -1],
        [-1, 0, 1],
        [0, 1, 1],
        [0, -1, -1],
        [0, 1, -1],
        [0, -1, 1],
    ]
)
NPOP = 19
BX = 16
TAU_FINE = 0.6
TAU_COARSE = 0.55
RESCALE = 2.0 * TAU_COARSE / TAU_FINE

ROWS, LANES = 8, 128
TILE = (ROWS, LANES)
VMEM = pltpu.VMEM


def row_ids():
    return lax.broadcasted_iota(jnp.int32, TILE, 0)


def lane_ids():
    return lax.broadcasted_iota(jnp.int32, TILE, 1)


def roll_rows(tile, shift):
    return pltpu.roll(tile, shift % ROWS, 0)


def roll_lanes(tile, shift):
    return pltpu.roll(tile, shift % LANES, 1)


def moments(f, scale):
    minus = [f[i] - f[i + 1] for i in range(1, NPOP, 2)]
    plus = [f[i] + f[i + 1] for i in range(1, NPOP, 2)]
    rho = ((f[0] + plus[0]) + (plus[1] + plus[2])) + (
        (plus[3] + plus[4]) + (plus[5] + plus[6])
    ) + (plus[7] + plus[8])
    jx = (minus[0] + minus[3]) + (minus[4] + minus[5]) + minus[6]
    jy = (minus[1] + minus[3]) - (minus[4] - minus[7]) + minus[8]
    jz = (minus[2] + minus[5]) - (minus[6] - minus[7]) - minus[8]
    inverse = 1.5 / rho
    ux, uy, uz = jx * inverse, jy * inverse, jz * inverse
    amount = scale(rho)
    base = amount * (1.0 - (2.0 / 3.0) * (ux * ux + uy * uy + uz * uz))
    directions = [ux, uy, uz, ux + uy, ux - uy, ux + uz, ux - uz, uy + uz, uy - uz]
    base_axis, base_diag = base * (1.0 / 18.0), base * (1.0 / 36.0)
    amount_axis, amount_diag = amount * (1.0 / 9.0), amount * (1.0 / 18.0)
    pairs = []
    for k, along in enumerate(directions):
        odd = (amount_axis if k < 3 else amount_diag) * along
        pairs.append(((base_axis if k < 3 else base_diag) + odd * along, odd))
    return base * (1.0 / 3.0), pairs, plus, minus


def collide(f, solid, tau):
    rate = (1.0 - solid) * (1.0 / tau)
    rest, pairs, plus, minus = moments(f, lambda rho: rate * rho)
    keep = 1.0 - rate
    half = 0.5 * keep
    half_odd = half - solid
    out = [keep * f[0] + rest]
    for (even, odd), p, m in zip(pairs, plus, minus):
        symmetric = half * p + even
        antisymmetric = half_odd * m + odd
        out += [symmetric + antisymmetric, symmetric - antisymmetric]
    return out


def restrict(f):
    rest, pairs, _, _ = moments(f, lambda rho: (1.0 - RESCALE) * rho)
    out = [RESCALE * f[0] + rest]
    for k, (even, odd) in enumerate(pairs):
        out += [RESCALE * f[2 * k + 1] + (even + odd), RESCALE * f[2 * k + 2] + (even - odd)]
    return out


def shift_plane(halves, cy, cz):
    lane = lane_ids()
    if cz:
        edge = lane % BX == (0 if cz > 0 else BX - 1)
        halves = [
            jnp.where(
                edge,
                roll_lanes(v, BX * cy + cz - BX * cz),
                roll_lanes(v, BX * cy + cz),
            )
            for v in halves
        ]
    elif cy:
        halves = [roll_lanes(v, BX * cy) for v in halves]
    if cy:
        carried = lane < BX if cy > 0 else lane >= LANES - BX
        halves = [
            jnp.where(carried, halves[1], halves[0]),
            jnp.where(carried, halves[0], halves[1]),
        ]
    return halves


def shift_ring(tiles, cx):
    if not cx:
        return tiles
    row = row_ids()
    turned = [roll_rows(t, cx) for t in tiles]
    if len(tiles) == 1:
        return turned
    edge = row == (0 if cx > 0 else ROWS - 1)
    n = len(tiles)
    return [jnp.where(edge, turned[(i - cx) % n], turned[i]) for i in range(n)]


def move_in_planes(halves):
    moved = [
        shift_plane([halves[0][i], halves[1][i]], int(VEL[i, 1]), int(VEL[i, 2]))
        for i in range(NPOP)
    ]
    return [[moved[i][h] for i in range(NPOP)] for h in range(2)]


def move_along(ring):
    out = [[[], []] for _ in ring]
    for h in range(2):
        for i in range(NPOP):
            for t, v in enumerate(shift_ring([tile[h][i] for tile in ring], int(VEL[i, 0]))):
                out[t][h].append(v)
    return out


def merge(mask, first, second):
    return [
        [jnp.where(mask, v, w) for v, w in zip(a, b)] for a, b in zip(first, second)
    ]


def means():
    shape = (2 * LANES, LANES)
    fine = lax.broadcasted_iota(jnp.int32, shape, 0)
    place = lax.broadcasted_iota(jnp.int32, shape, 1)
    same = (fine // (2 * BX) == place // BX) & (fine % BX // 2 == place % 8)
    return jnp.where(same, 0.125, 0.0).astype(jnp.bfloat16)


def squeeze(planes, matrix):
    cells = jnp.concatenate([jnp.concatenate(halves, axis=1) for halves in planes], axis=0)
    found = None
    for _ in range(3):
        part = cells.astype(jnp.bfloat16)
        product = jnp.dot(part, matrix, preferred_element_type=jnp.float32)
        found = product if found is None else found + product
        cells = cells - part.astype(jnp.float32)
    return [found[ROWS * k : ROWS * (k + 1)] for k in range(len(planes))]


INNER_TILES = (NPOP + 1) // 2 - 2


def fold(tiles):
    out = list(tiles[:INNER_TILES])
    for m in range(6):
        extra, at = tiles[INNER_TILES + m // 3], 2 * (m % 3)
        out[m] = pick(((0,), roll_rows(extra, -1 - at)), ((7,), roll_rows(extra, 5 - at)), (out[m],))
    return out


def unfold(tile, j):
    if j < INNER_TILES:
        return tile(j)
    rows = []
    for m in range(3):
        v = tile(3 * (j - INNER_TILES) + m)
        rows += [((1 + 2 * m,), roll_rows(v, 1 + 2 * m)), ((2 + 2 * m,), roll_rows(v, 2 * m - 5))]
    return pick(*rows, (rows[-1][1],))


def lower():
    return lane_ids() % BX < 8


def pair_up(first, second):
    return first if second is None else jnp.where(lower(), first, second)


def spread(first, second, which):
    if which:
        return jnp.where(lower(), roll_lanes(first, -8), second)
    return jnp.where(lower(), first, roll_lanes(second, 8))


def filled(chosen, h, sources):
    low, high = (sum(chosen[2 * h + z, s] for s in sources) for z in range(2))
    return jnp.where(lower(), low, high) > 0.5


def choose(chosen, quadrant, tiles):
    (_, out), *rest = tiles
    for s, tile in rest:
        out = jnp.where(chosen[quadrant, s] > 0.5, tile, out)
    return out


def half_lanes(h):
    return pl.ds(h * LANES, LANES)


FORWARD = [i for i in range(NPOP) if VEL[i, 0] > 0]
LEVEL = [i for i in range(NPOP) if VEL[i, 0] == 0]
BACKWARD = [i for i in range(NPOP) if VEL[i, 0] < 0]
MOVING = len(FORWARD)

PAIRS = (len(LEVEL) + 1) // 2
WORDS = MOVING + PAIRS


def pick(*choices):
    row = row_ids()
    out = choices[-1][-1]
    for rows, tile in choices[-2::-1]:
        mask = row == rows[0]
        for r in rows[1:]:
            mask = mask | (row == r)
        out = jnp.where(mask, tile, out)
    return out


def pack_message(message, first, second, rim, up):
    for k, i in enumerate(FORWARD if up else BACKWARD):
        f, s = [first(i, h) for h in range(2)], [second(i, h) for h in range(2)]
        s = [v + roll_rows(v, -1) for v in s]
        if up:
            message[k] = pick(
                ((7, 0), roll_rows(f[0], 1)),
                ((1, 2), roll_rows(f[1], 3)),
                ((3,), roll_rows(s[0], -2)),
                ((5,), s[1]),
                ((4,), rim[k]),
                (roll_rows(rim[k], -2),),
            )
        else:
            message[k] = pick(
                ((3, 4), roll_rows(f[0], 3)),
                ((5, 6), roll_rows(f[1], 5)),
                ((7,), roll_rows(s[0], -2)),
                ((1,), s[1]),
                ((0,), roll_rows(rim[k], -3)),
                (roll_rows(rim[k], 3),),
            )
    for k in range(PAIRS):
        shared = []
        for i in (LEVEL + [NPOP])[2 * k : 2 * k + 2]:
            f = [first(i, h) for h in range(2)]
            if up:
                if i < NPOP:
                    s = [roll_rows(second(i, 0), -3), roll_rows(second(i, 1), -1)]
                else:
                    s = [roll_rows(rim[MOVING], -1), roll_rows(rim[MOVING], 5)]
                shared.append(pick(((7,), f[0]), ((1,), roll_rows(f[1], 2)), ((3,), s[0]), (s[1],)))
            else:
                if i < NPOP:
                    s = [roll_rows(second(i, 0), -1), roll_rows(second(i, 1), 1)]
                else:
                    s = [roll_rows(rim[MOVING], -3), roll_rows(rim[MOVING], 3)]
                shared.append(
                    pick(((4,), roll_rows(f[0], 4)), ((6,), roll_rows(f[1], -2)), ((0,), s[0]), (s[1],))
                )
        own_rows = (1, 3, 5, 7) if up else (0, 2, 4, 6)
        message[MOVING + k] = pick((own_rows, shared[0]), (roll_rows(shared[1], 1),))


def shared_tile(message, i):
    k = (LEVEL + [NPOP]).index(i)
    return roll_rows(message[MOVING + k // 2], -(k % 2))


def rim_row(message, k, h, up):
    index, row = (k, 0) if k < MOVING else (WORDS - 1, 1)
    row = 4 + 2 * h if up else row + 2 * h
    return jnp.broadcast_to(message[index, pl.ds(row, 1), :], TILE)


def pack_kernel(
    fine, solid, coarse, coarse_solid, slot, moved, second, high, low, center, shade, slot_out, strip, rim, sem
):
    planes = fine.shape[2]
    last = coarse.shape[2] - 1

    def bring(source, target, which):
        pltpu.make_async_copy(source, target, sem.at[which]).start()

    def arrive(target, which):
        pltpu.make_async_copy(target, target, sem.at[which]).wait()

    ends = ((0, 0), (planes - 4, 4))
    for half in (pl.ds(0, 7), pl.ds(7, 6), pl.ds(13, 6)):
        for first, row in ends:
            bring(fine.at[0, half, pl.ds(first, 4), :], strip.at[half, pl.ds(row, 4), :], 0)
    bring(solid.at[0], shade, 0)
    for plane, row in ((last, 0), (0, 3)):
        bring(coarse.at[0, :, pl.ds(plane, 1), :], rim.at[pl.ds(0, NPOP), pl.ds(row, 1), :], 1)
        bring(coarse_solid.at[0, pl.ds(plane, 1), :], rim.at[NPOP, pl.ds(row, 1), :], 1)
    bring(slot, slot_out, 2)
    for first, row in ((4, 4), (8, 0)):
        bring(fine.at[0, :, pl.ds(first, 4), :], center.at[:, pl.ds(row, 4), :], 3)
    arrive(strip, 0)
    upper = row_ids() < 4
    solids = [
        jnp.where(upper, shade[pl.ds(0, ROWS), half_lanes(h)], shade[pl.ds(planes - ROWS, ROWS), half_lanes(h)])
        for h in range(2)
    ]
    once = move_in_planes(
        [collide([strip[i, :, half_lanes(h)] for i in range(NPOP)], solids[h], TAU_FINE) for h in range(2)]
    )
    arrive(slot_out, 2)
    arrive(rim.at[:, pl.ds(0, 2), :], 1)

    def rim_tile(i):
        v = [rim[i, :, half_lanes(h)] for h in range(2)]
        return pick(((0,), v[1]), ((3,), v[0]), ((4,), roll_rows(v[0], 4)), (roll_rows(v[1], 4),))

    s = rim_tile(NPOP)
    outer = collide([rim_tile(i) for i in range(NPOP)], s, TAU_COARSE) + [s]
    ring = move_along([once])[0]
    twice = [collide(ring[h], solids[h], TAU_FINE) for h in range(2)]
    for h in range(2):
        for i in range(NPOP):
            moved[i, h] = once[h][i]
            second[i, h] = twice[h][i]
        moved[NPOP, h] = solids[h]

    def first_of(i, h):
        return moved[i, h]

    def second_of(i, h):
        return second[i, h]

    pack_message(high, first_of, second_of, [outer[i] for i in FORWARD + [NPOP]], True)
    pack_message(low, first_of, second_of, [outer[i] for i in BACKWARD + [NPOP]], False)
    arrive(center, 3)


def inner_steps(center, solid, moved, inner, packed):
    upper = row_ids() < 4
    solids = [
        [solid[pl.ds(ROWS * t, ROWS), half_lanes(h)] for h in range(2)] for t in range(2)
    ]
    outer = [[moved[i, h] for i in range(NPOP)] for h in range(2)]
    between = move_in_planes(
        [
            collide(
                [center[i, :, half_lanes(h)] for i in range(NPOP)],
                jnp.where(upper, solids[1][h], solids[0][h]),
                TAU_FINE,
            )
            for h in range(2)
        ]
    )
    ring = move_along([merge(upper, outer, between), merge(upper, between, outer)])
    for t in range(2):
        for h in range(2):
            ring[t][h] = collide(ring[t][h], solids[t][h], TAU_FINE)
        ring[t] = move_in_planes(ring[t])
    ring = move_along(ring)
    for i in range(NPOP):
        for h in range(2):
            for t in range(2):
                inner[i, h, pl.ds(ROWS * t, ROWS), :] = ring[t][h][i]
    sums = [
        [
            inner[i, h, pl.ds(0, ROWS, stride=2), :] + inner[i, h, pl.ds(1, ROWS, stride=2), :]
            for h in range(2)
        ]
        for i in range(NPOP)
    ]
    out = restrict(squeeze(sums, means())) + [None]
    pairs = [pair_up(out[2 * j], out[2 * j + 1]) for j in range((NPOP + 1) // 2)]
    for j, tile in enumerate(fold(pairs)):
        packed[j] = tile


def starts_early():
    return lax.axis_index("blk") == 0


def prepare(slot, chosen, matrix):
    groups = chosen.shape[1]
    matrix[...] = means()
    me = lax.axis_index("grp")
    codes = slot[...].reshape(1, groups)
    group_ids = lax.broadcasted_iota(jnp.int32, codes.shape, 1)
    for s in range(groups):
        code = jnp.sum(jnp.where(group_ids == me ^ s, codes, 0), axis=1, keepdims=True)
        for q in range(4):
            chosen[q, s] = jnp.where(lane_ids() * 0 + (4 * me + q) == code, 1.0, 0.0)


def early_kernel(center, solid, moved, slot, low, inner, packed, chosen, matrix, low_out):
    low_out[...] = low[...]

    @pl.when(starts_early())
    def _():
        inner_steps(center, solid, moved, inner, packed)
        prepare(slot, chosen, matrix)


def inner_kernel(center, solid, moved, slot, *refs):
    *refs, padded = refs
    done, (inner, packed, chosen, matrix) = refs[:4], refs[4:]

    @pl.when(starts_early())
    def _():
        for source, target in zip(done, (inner, packed, chosen, matrix)):
            target[...] = source[...]

    @pl.when(jnp.logical_not(starts_early()))
    def _():
        inner_steps(center, solid, moved, inner, packed)
        prepare(slot, chosen, matrix)

    size = packed.shape[0]
    padded[pl.ds(0, size)] = packed[...]
    padded[size] = jnp.zeros(TILE, jnp.float32)


def edge_kernel(moved, second, below, above, matrix, coarse, coarse_solid, edges, packed):
    row = row_ids()

    def middle(i):
        v = [moved[i, h] for h in range(2)]
        if i in FORWARD:
            return pick(
                ((3, 4), roll_rows(v[0], -3)),
                ((5, 6), roll_rows(v[1], -1)),
                (below[FORWARD.index(i)],),
            )
        if i in BACKWARD:
            return pick(
                ((7, 0), roll_rows(v[0], -1)),
                ((1, 2), roll_rows(v[1], 1)),
                (above[BACKWARD.index(i)],),
            )
        return pick(
            ((0,), v[0]),
            ((2,), roll_rows(v[1], 2)),
            ((3,), roll_rows(v[0], 4)),
            ((5,), roll_rows(v[1], -2)),
            ((1, 7), shared_tile(below, i)),
            (shared_tile(above, i),),
        )

    twice = collide([middle(i) for i in range(NPOP)], middle(NPOP), TAU_FINE)
    nothing = jnp.zeros(TILE, jnp.float32)
    both = [[], []]
    for h in range(2):
        for i in range(NPOP):
            cx = int(VEL[i, 0])
            v, mine = roll_rows(twice[i], cx - 2 * h), second[i, h]
            if cx > 0:
                v = pick(
                    ((0, 1, 4, 5), v),
                    ((2, 3), roll_rows(mine, -3)),
                    ((7,), nothing),
                    (roll_rows(below[FORWARD.index(i)], 3 - 2 * h),),
                )
            elif cx < 0:
                v = pick(
                    ((2, 3, 6, 7), v),
                    ((0, 1), roll_rows(mine, -1)),
                    ((5,), nothing),
                    (roll_rows(above[BACKWARD.index(i)], -3 - 2 * h),),
                )
            else:
                v = pick(
                    ((0, 3, 4, 7), v),
                    ((1,), mine),
                    ((2,), roll_rows(mine, 4)),
                    ((6,), roll_rows(shared_tile(below, i), 3 - 2 * h)),
                    (roll_rows(shared_tile(above, i), -3 - 2 * h),),
                )
            both[h].append(v)
    both = move_in_planes(both)
    sums = [[v + roll_rows(v, -1) for v in half] + [None] for half in both]
    odd = row % 2 == 1
    pairs = [
        [half[i] if half[i + 1] is None else jnp.where(odd, roll_rows(half[i + 1], 1), half[i]) for half in sums]
        for i in range(0, NPOP, 2)
    ]
    mean = []
    for pair in squeeze(pairs, matrix[...]):
        mean += [pair, roll_rows(pair, -1)]
    out = restrict(mean[:NPOP]) + [None]
    pairs = [
        out[i] if out[i + 1] is None else jnp.where(odd, roll_rows(out[i + 1], 1), out[i])
        for i in range(0, NPOP, 2)
    ]
    for j in range(len(pairs) // 2):
        packed[j] = pair_up(pairs[2 * j], pairs[2 * j + 1])
    for i in range(NPOP):
        for h in range(2):
            edges[i, h] = both[h][i]


def write_kernel(inner, edges, out):
    row = row_ids()
    for i in range(NPOP):
        for h in range(2):
            edge = edges[i, h]
            out[0, i, pl.ds(0, ROWS), half_lanes(h)] = jnp.where(
                row < 2, edge, inner[i, h, pl.ds(0, ROWS), :]
            )
            out[0, i, pl.ds(ROWS, ROWS), half_lanes(h)] = jnp.where(
                row >= 6, roll_rows(edge, 4), inner[i, h, pl.ds(ROWS, ROWS), :]
            )


def split_kernel(after, tiles, first, second):
    half = first.shape[0]
    first[...] = tiles[pl.ds(0, half)]
    second[...] = tiles[pl.ds(half, half)]


def paste_inner(chosen, sources, tile, base, out):
    masks = [filled(chosen, h, sources) for h in range(2)]
    for j in range((NPOP + 1) // 2):
        tiles = [(s, tile(s, j)) for s in sources]
        for h in range(2):
            low, high = (choose(chosen, 2 * h + z, tiles) for z in range(2))
            for i in range(2 * j, min(2 * j + 2, NPOP)):
                out(i, h, jnp.where(masks[h], spread(low, high, i % 2), base(i, h)))


def paste_kernel(after, coarse, solid, chosen, below, above, *refs):
    *packed, out, ends = refs
    sources = [1, *range(0, chosen.shape[1], 2)]
    parts = dict(zip(sources, packed))

    def write(i, h, tile):
        out[i, h] = tile

    paste_inner(
        chosen, sources, lambda s, j: unfold(lambda k: parts[s][k], j), lambda i, h: coarse[0, i, :, half_lanes(h)], write
    )
    for i in range(NPOP + 1):
        v = [coarse[0, i, :, half_lanes(h)] if i < NPOP else solid[0, :, half_lanes(h)] for h in range(2)]
        tile = pick(((0,), v[0]), ((1,), roll_rows(v[1], 1)), ((2,), roll_rows(v[0], 3)), (roll_rows(v[1], 4),))
        if i == NPOP:
            tile = pick(
                ((4,), rim_row(above, MOVING, 0, False)),
                ((5,), rim_row(above, MOVING, 1, False)),
                ((6,), rim_row(below, MOVING, 0, True)),
                ((7,), rim_row(below, MOVING, 1, True)),
                (tile,),
            )
        ends[i] = tile


def coarse_kernel(after, base, solid, chosen, *refs):
    relayed, out = refs[:-1], refs[-1]
    sources = [2 * k + 3 for k in range(len(relayed) // 2)]
    f = [[None] * NPOP, [None] * NPOP]

    def write(i, h, tile):
        f[h][i] = tile

    half = relayed[0].shape[0]

    def tile(s, j):
        return unfold(lambda k: relayed[s - 3 + k // half][k % half], j)

    paste_inner(chosen, sources, tile, lambda i, h: base[i, h], write)
    f = move_in_planes([collide(f[h], solid[0, :, half_lanes(h)], TAU_COARSE) for h in range(2)])
    for h in range(2):
        for i in range(NPOP):
            out[i, h] = f[h][i]


CHUNKS = (0, 1, 3, 5, 7, 9, 11, 13, 15, 17, 18, NPOP)


def last_kernel(chosen, below, above, base, middle, *refs):
    *packed, result, out, sem = refs
    sources = [0, *others(len(packed))]
    row, lane = row_ids(), lane_ids()
    odd = row % 2 == 1
    pasted = [filled(chosen, h, sources) for h in range(2)]
    pasted = (odd & pasted[1]) | (~odd & pasted[0])
    f = []
    for j in range((NPOP + 1) // 4):
        tiles = [(s, part[j]) for s, part in zip(sources, packed)]
        quadrants = [choose(chosen, q, tiles) for q in range(4)]
        for which in range(2):
            v = [spread(quadrants[2 * h], quadrants[2 * h + 1], which) for h in range(2)]
            f.append(jnp.where(odd, roll_rows(v[1], 1), v[0]))
            f.append(jnp.where(odd, v[1], roll_rows(v[0], -1)))
    f = [jnp.where(pasted, f[i], base[i]) for i in range(NPOP)]
    f = collide(f, base[NPOP], TAU_COARSE)
    copied = 0
    for i in range(NPOP):
        cx, cy, cz = (int(c) for c in VEL[i])
        v = f[i]
        if cx:
            k = (FORWARD if cx > 0 else BACKWARD).index(i)
            rim = [rim_row(below if cx > 0 else above, k, h, cx > 0) for h in range(2)]
            at = row >= 6 if cx > 0 else (row == 4) | (row == 5)
            v = jnp.where(at & ~pasted, jnp.where(odd, rim[1], rim[0]), v)
        if cz:
            edge = lane % BX == (0 if cz > 0 else BX - 1)
            v = jnp.where(
                edge, roll_lanes(v, BX * cy + cz - BX * cz), roll_lanes(v, BX * cy + cz)
            )
        elif cy:
            v = roll_lanes(v, BX * cy)
        if cy:
            carried = lane < BX if cy > 0 else lane >= LANES - BX
            v = jnp.where(carried, jnp.where(odd, roll_rows(v, 1), roll_rows(v, -1)), v)
        for h in range(2):
            inside = middle[i, h]
            if cx > 0:
                tile = pick(
                    ((0,), roll_rows(v, 2 - h)), ((1,), roll_rows(v, 1 - h)), (roll_rows(inside, 1),)
                )
            elif cx < 0:
                tile = pick(
                    ((7,), roll_rows(v, 3 - h)), ((6,), roll_rows(v, 4 - h)), (roll_rows(inside, -1),)
                )
            else:
                tile = pick(((0,), roll_rows(v, -h)), ((7,), roll_rows(v, 5 - h)), (inside,))
            out[0, i, :, half_lanes(h)] = tile
        if i + 1 in CHUNKS:
            some = pl.ds(copied, i + 1 - copied)
            pltpu.make_async_copy(out.at[0, some], result.at[0, some], sem).start()
            copied = i + 1
    pltpu.make_async_copy(out, result, sem).wait()


def others(groups):
    return range(1, groups)


def exchange(array, distance):
    groups = lax.axis_size("grp")
    return lax.ppermute(array, "grp", [(i, i ^ distance) for i in range(groups)])


def held(array):
    return pltpu.with_memory_space_constraint(array, VMEM)


def left(array):
    return pltpu.with_memory_space_constraint(array, pltpu.HBM)


def in_vmem(*shape):
    return VMEM(shape, jnp.float32)


def call(kernel, args, specs, outs, scratch=(), flops=0, name=None, out_space=VMEM):
    single = not isinstance(outs, (list, tuple))
    outs = [outs] if single else list(outs)
    result = pl.pallas_call(
        kernel,
        in_specs=[pl.BlockSpec(memory_space=s) for s in specs],
        out_specs=[pl.BlockSpec(memory_space=out_space)] * len(outs),
        out_shape=outs,
        scratch_shapes=list(scratch),
        compiler_params=pltpu.CompilerParams(vmem_limit_bytes=24 << 20),
        cost_estimate=pl.CostEstimate(flops=flops, bytes_accessed=1, transcendentals=0),
        name=name,
    )(*args)
    return result[0] if single else result


def per_device(fine_pops, fine_solid, coarse_pops, coarse_solid, coarse_slot):
    groups = lax.axis_size("grp")
    blocks = lax.axis_size("blk")
    moved, second, high, low, center, shade, slot = call(
        pack_kernel,
        tuple(map(left, (fine_pops, fine_solid, coarse_pops, coarse_solid, coarse_slot))),
        [pl.ANY] * 5,
        [
            in_vmem(NPOP + 1, 2, *TILE),
            in_vmem(NPOP, 2, *TILE),
            in_vmem(WORDS, *TILE),
            in_vmem(WORDS, *TILE),
            in_vmem(NPOP, ROWS, 2 * LANES),
            in_vmem(*fine_solid.shape[1:]),
            VMEM((groups,), jnp.int32),
        ],
        [
            in_vmem(NPOP + 2, ROWS, 2 * LANES),
            in_vmem(NPOP + 1, ROWS, 2 * LANES),
            pltpu.SemaphoreType.DMA((4,)),
        ],
        name="pack",
    )
    coarse_v, coarse_solid_v = held(coarse_pops), held(coarse_solid)
    inner_shapes = [
        in_vmem(NPOP, 2, 2 * ROWS, LANES),
        in_vmem(INNER_TILES, *TILE),
        in_vmem(4, groups, *TILE),
        VMEM((2 * LANES, LANES), jnp.bfloat16),
    ]
    inner_args = (held(center), held(shade), held(moved), held(slot))
    *done, low = call(
        early_kernel,
        (*inner_args, held(low)),
        [VMEM] * 5,
        [*inner_shapes, in_vmem(WORDS, *TILE)],
        name="early",
    )
    forward = [(i, (i + 1) % blocks) for i in range(blocks)]
    backward = [(i, (i - 1) % blocks) for i in range(blocks)]
    below = lax.ppermute(high, "blk", forward)
    above = lax.ppermute(low, "blk", backward)
    inner, packed_inner, chosen, matrix, padded_inner = call(
        inner_kernel,
        (*inner_args, *map(held, done)),
        [VMEM] * 8,
        [*inner_shapes, in_vmem(INNER_TILES + 1, *TILE)],
        name="inner",
    )

    across = [exchange(packed_inner, s) for s in range(2, groups, 2)]
    beside = exchange(padded_inner, 1)
    edges, packed_edges = call(
        edge_kernel,
        (held(moved), held(second), held(below), held(above), held(matrix), coarse_v, coarse_solid_v),
        [VMEM] * 7,
        [in_vmem(NPOP, 2, *TILE), in_vmem((NPOP + 1) // 4, *TILE)],
        name="edge",
    )
    edge_parts = [packed_edges] + [exchange(packed_edges, s) for s in others(groups)]
    fine_out = call(
        write_kernel,
        (held(inner), held(edges)),
        [VMEM] * 2,
        jax.ShapeDtypeStruct(fine_pops.shape, jnp.float32),
        name="write",
    )
    inner_parts = [beside, packed_inner, *across]
    base, ends = call(
        paste_kernel,
        (
            held(edges),
            coarse_v,
            coarse_solid_v,
            held(chosen),
            held(below),
            held(above),
            *map(held, inner_parts),
        ),
        [VMEM] * (6 + len(inner_parts)),
        [in_vmem(NPOP, 2, *TILE), in_vmem(NPOP + 1, *TILE)],
        name="paste",
    )
    relayed = []
    for part in across:
        halves = call(
            split_kernel,
            (held(edges), held(part)),
            [VMEM] * 2,
            [in_vmem(part.shape[0] // 2, *TILE)] * 2,
            name="split",
        )
        relayed += [exchange(half, 1) for half in halves]
    middle = call(
        coarse_kernel,
        (left(fine_out), held(base), coarse_solid_v, held(chosen), *map(held, relayed)),
        [pl.ANY] + [VMEM] * (3 + len(relayed)),
        in_vmem(NPOP, 2, *TILE),
        name="coarse",
    )
    coarse_out = call(
        last_kernel,
        (held(chosen), held(below), held(above), held(ends), held(middle), *map(held, edge_parts)),
        [VMEM] * (5 + len(edge_parts)),
        jax.ShapeDtypeStruct(coarse_pops.shape, jnp.float32),
        [in_vmem(*coarse_pops.shape), pltpu.SemaphoreType.DMA],
        out_space=pl.ANY,
        name="last",
    )
    return fine_out, coarse_out


def solution(mesh):
    placed = (
        P("grp", None, "blk", None),
        P("grp", "blk", None),
        P("grp", None, "blk", None),
        P("grp", "blk", None),
        P(),
    )
    return jax.shard_map(
        per_device,
        mesh=mesh,
        in_specs=placed,
        out_specs=(P("grp", None, "blk", None), P("grp", None, "blk", None)),
        check_vma=False,
    )
```
